32 devices in a mesh: fsdp: 8 (over z, core), ctx: 2 (over x), tp: 2 (over y).
Axes of the slice: x: 2, y: 2, z: 4, core: 2. Of those that a mesh axis runs over, the one named last changes fastest.
Arguments:
- tokens: bfloat16 [32, 1024, 768], P(('fsdp', 'tp'), 'ctx'), may hold values from -6 to 6
- query_key_value_weight: bfloat16 [768, 2304], P('fsdp'), may hold values from -0.21875 to 0.21875
- output_weight: bfloat16 [768, 768], P('fsdp'), may hold values from -3.5 to 3.5
- gate_weight: bfloat16 [768, 3072], P('fsdp', 'tp'), may hold values from -0.21875 to 0.21875
- up_weight: bfloat16 [768, 3072], P('fsdp', 'tp'), may hold values from -0.21875 to 0.21875
- down_weight: bfloat16 [3072, 768], P('tp', 'fsdp'), may hold values from -0.109375 to 0.109375
- gain_one: bfloat16 [768], P('fsdp'), may hold values from 0.25 to 1.75
- shift_one: bfloat16 [768], P('fsdp'), may hold values from -2.5 to 2.5
- gain_two: bfloat16 [768], P('fsdp'), may hold values from 0.25 to 1.75
- shift_two: bfloat16 [768], P('fsdp'), may hold values from -2.5 to 2.5
- lengths: int32 [32], P(('fsdp', 'tp')), may hold values from 256 to 1024, as said below
- positions: int32 [32, 1024], P(('fsdp', 'tp'), 'ctx'), may hold values from 0 to 2046, as said below
- cotangent: bfloat16 [32, 1024, 768], P(('fsdp', 'tp'), 'ctx'), may hold values from -6 to 6
Outputs:
- mixed_out: bfloat16 [32, 1024, 768], P(('fsdp', 'tp'), 'ctx')
- grad_tokens: float32 [32, 1024, 768], P(('fsdp', 'tp'), 'ctx')
- grad_w_qkv: float32 [768, 2304], P('fsdp')
- grad_w_out: float32 [768, 768], P('fsdp')
- grad_w_gate: float32 [768, 3072], P('fsdp', 'tp')
- grad_w_up: float32 [768, 3072], P('fsdp', 'tp')
- grad_w_down: float32 [3072, 768], P('tp', 'fsdp')
- grad_gain_one: float32 [768], P('fsdp')
- grad_shift_one: float32 [768], P('fsdp')
- grad_gain_two: float32 [768], P('fsdp')
- grad_shift_two: float32 [768], P('fsdp')
The draws below stay inside these ranges and needn't reach their ends.
Inputs may be any that keep to these rules, and one draw needn't show every extreme that they name: `lengths`: each slot's valid tokens are its first ones; in each aligned block of 2 slots (the slots of one device) at least one slot holds 1024, which one drawn from the seed. `positions`: in each slot the first id is 0 and each next one is 1 or 2 larger; in some slot, drawn from the seed, every step is 2.
All inputs are finite; a program needn't handle non-finite values.
Results may differ from the reference program's by a relative error of at most 0.023.
Values may be sent and summed in bfloat16 or wider, within the bound.
No kernel may reach another device: no remote copies, remote signals or barrier semaphores. Data moves between devices by JAX's collectives and lax.ppermute only.
A program may use at most 192 MiB of HBM per device.

```python
import jax
import jax.numpy as jnp
from jax import lax

D = 768
HEADS = 12
HEAD_DIM = 64
FF = 3072
SEQ = 1024
MIN_LEN = 256
SLOT_DEV = 2
SLOTS = 32


def draw_lengths(key, part):
    key = jax.random.fold_in(key, 11)
    first_key, second_key = jax.random.split(key)
    ragged = jax.random.randint(first_key, (SLOTS,), MIN_LEN, SEQ + 1)
    chosen = jax.random.randint(second_key, (SLOTS // SLOT_DEV,), 0, SLOT_DEV)
    full_slot = (jnp.arange(SLOT_DEV)[None, :] == chosen[:, None]).reshape(SLOTS)
    return jnp.where(full_slot, SEQ, ragged).astype(jnp.int32)


def draw_positions(key, part):
    key = jax.random.fold_in(key, 23)
    stride_key, slot_key = jax.random.split(key)
    strides = jax.random.randint(stride_key, (SLOTS, SEQ), 1, 3)
    widest = jax.random.randint(slot_key, (), 0, SLOTS)
    strides = jnp.where(jnp.arange(SLOTS)[:, None] == widest, 2, strides)
    strides = jnp.where(jnp.arange(SEQ)[None, :] == 0, 0, strides)
    return jnp.cumsum(strides, axis=1).astype(jnp.int32)


def raised(values, rng, source, target, shards_of, factor):
    def block_of(position):
        return (jnp.arange(values.shape[position]) // (values.shape[position] // shards_of)).reshape((-1,) + (1,) * (values.ndim - 1 - position))

    near = jax.random.permutation(rng, shards_of)[block_of(target)]
    second = (block_of(target) + shards_of // 2) % shards_of
    return jnp.where((block_of(source) == near) | (block_of(source) == second), factor * values, values)


def block_levels(own_key, extent, cuts, smallest, top_value):
    level = 1.0
    for position, blocks in cuts:
        heights = jax.random.uniform(jax.random.fold_in(jax.random.fold_in(own_key, 6), position), (blocks,), jnp.float32, smallest / len(cuts), top_value / len(cuts))
        level = level * jnp.repeat(jnp.exp(heights), extent[position] // blocks).reshape((-1,) + (1,) * (len(extent) - 1 - position))
    return level


def scatter_about(own_key, extent, spread, reach, cuts=(), kind=jnp.bfloat16):
    entries = spread * jax.random.normal(own_key, extent, jnp.float32)
    if cuts:
        entries = entries * block_levels(own_key, extent, cuts, -0.22, 0.18)
    return jnp.clip(entries, -reach, reach).astype(kind)


def gaussian_with(key, extent, spread, most, shards, heavy, kind=jnp.bfloat16):
    array = spread * jax.random.normal(key, extent, jnp.float32)
    if shards:
        array = array * block_levels(key, extent, shards, -0.22, 0.18)
    return jnp.clip(raised(array, jax.random.fold_in(key, 3), *heavy), -most, most).astype(kind)


def setup_inputs(seed: int = 0) -> dict:
    splits = jax.random.split(jax.random.key(seed), 14)
    tokens = gaussian_with(splits[0], (SLOTS, SEQ, D), 1.0, 6.0, ((0, 16), (1, 2)), (0, 2, 16, 2.0))
    query_key_value_weight = scatter_about(splits[1], (D, 3 * D), D ** -0.5, 0.21875, ((0, 8),))
    output_weight = scatter_about(splits[2], (D, D), (max(D // 256, 1)) ** -0.5, 3.5, ((0, 8),))
    gate_weight = scatter_about(splits[3], (D, FF), D ** -0.5, 0.21875, ((0, 8), (1, 2)))
    up_weight = scatter_about(splits[4], (D, FF), D ** -0.5, 0.21875, ((0, 8), (1, 2)))
    down_weight = scatter_about(splits[5], (FF, D), FF ** -0.5, 0.109375, ((0, 2), (1, 8)))
    gain_one = jnp.clip(1.0 + 0.15 * jax.random.normal(splits[6], (D,), jnp.float32), 0.25, 1.75).astype(jnp.bfloat16)
    shift_one = scatter_about(splits[7], (D,), 0.5, 2.5, ((0, 8),))
    gain_two = jnp.clip(1.0 + 0.15 * jax.random.normal(splits[8], (D,), jnp.float32), 0.25, 1.75).astype(jnp.bfloat16)
    shift_two = scatter_about(splits[9], (D,), 0.5, 2.5, ((0, 8),))
    lengths = draw_lengths(jax.random.fold_in(splits[13], 71), 0)
    positions = draw_positions(jax.random.fold_in(splits[13], 71), 0)
    cotangent = gaussian_with(splits[12], (SLOTS, SEQ, D), 1.0, 6.0, ((0, 16), (1, 2)), (0, 2, 16, 2.0))
    return {"tokens": tokens, "query_key_value_weight": query_key_value_weight, "output_weight": output_weight, "gate_weight": gate_weight, "up_weight": up_weight, "down_weight": down_weight, "gain_one": gain_one, "shift_one": shift_one, "gain_two": gain_two, "shift_two": shift_two, "lengths": lengths, "positions": positions, "cotangent": cotangent}


@jax.custom_vjp
def low(v):
    return lax.optimization_barrier(v.astype(jnp.bfloat16)).astype(jnp.float32)

@jax.custom_vjp
def low_back(v):
    return v

def low_keep(v):
    return (low(v), None)

def low_pass(kept, grad):
    return (grad,)

def back_keep(v):
    return (v, None)

def back_low(kept, grad):
    return (low(grad),)
low.defvjp(low_keep, low_pass)
low_back.defvjp(back_keep, back_low)
norm_eps = 1e-05
rope_base = 1000.0
highest_precision = lax.Precision.HIGHEST

def rotate(heads_in, places):
    half_dim = heads_in.shape[-1] // 2
    frequency = rope_base ** (-jnp.arange(half_dim, dtype=jnp.float32) * 2.0 / heads_in.shape[-1])
    angles = places.astype(jnp.float32)[..., None] * frequency
    cosine = jnp.cos(angles)[..., None, :]
    sine_val = jnp.sin(angles)[..., None, :]
    first_half = heads_in[..., :half_dim]
    second_half = heads_in[..., half_dim:]
    return jnp.concatenate([first_half * cosine - second_half * sine_val, second_half * cosine + first_half * sine_val], axis=-1)

def norm_layer(value_in, gain_in, shift_in):
    row_mean = lax.optimization_barrier(jnp.mean(value_in, axis=-1, keepdims=True))
    centered = value_in - row_mean
    inverse = lax.rsqrt(lax.optimization_barrier(jnp.mean(centered * centered, axis=-1, keepdims=True)) + norm_eps)
    return centered * inverse * gain_in + shift_in

def attend(slot_data):
    queries, key_rows, values, length = slot_data
    scores = jnp.einsum('qhe,khe->hqk', queries, key_rows, precision=highest_precision) * HEAD_DIM ** (-0.5)
    valid_keys = jnp.arange(key_rows.shape[0]) < length
    scores = low_back(jnp.where(valid_keys, scores, -1000000000.0))
    row_top = lax.optimization_barrier(jnp.max(scores, axis=-1, keepdims=True))
    exponent = jnp.exp(scores - row_top)
    softmax_out = exponent / lax.optimization_barrier(jnp.sum(exponent, axis=-1, keepdims=True))
    return jnp.einsum('hqk,khe->qhe', low(softmax_out), values, precision=highest_precision)

def block_layer(layer_input, query_key_value_weight, output_weight, gate_weight, up_weight, down_weight, gain_one, shift_one, gain_two, shift_two, slot_lengths, places):
    slot_count, seq_len, model_width = layer_input.shape
    unrotated_projection = low_back(jnp.einsum('gfi,in->gfn', layer_input, query_key_value_weight, precision=highest_precision))
    unrotated_projection = unrotated_projection.reshape(slot_count, seq_len, 3, HEADS, HEAD_DIM)
    queries = low(rotate(unrotated_projection[:, :, 0], places))
    key_rows = low(rotate(unrotated_projection[:, :, 1], places))
    values = low(unrotated_projection[:, :, 2])
    context_value = lax.map(jax.checkpoint(attend), (queries, key_rows, values, slot_lengths))
    context_value = low_back(low(context_value.reshape(slot_count, seq_len, model_width)))
    attention_result = low_back(jnp.einsum('gfi,in->gfn', context_value, output_weight, precision=highest_precision))
    normed_one = norm_layer(layer_input + attention_result, gain_one, shift_one)
    feed_input = low(normed_one)
    gate_preactivation = low_back(jnp.einsum('zmc,ci->zmi', feed_input, gate_weight, precision=highest_precision))
    upper_output = low_back(jnp.einsum('zmc,ci->zmi', feed_input, up_weight, precision=highest_precision))
    hidden_state = low(gate_preactivation * jax.nn.sigmoid(gate_preactivation) * upper_output)
    branch_output = low_back(jnp.einsum('pin,nw->piw', hidden_state, down_weight, precision=highest_precision))
    return norm_layer(normed_one + branch_output, gain_two, shift_two)

def reference(tokens, query_key_value_weight, output_weight, gate_weight, up_weight, down_weight, gain_one, shift_one, gain_two, shift_two, lengths, positions, cotangent):
    weights = tuple((entry.astype(jnp.float32) for entry in (query_key_value_weight, output_weight, gate_weight, up_weight, down_weight, gain_one, shift_one, gain_two, shift_two)))
    groups = SLOTS // 4
    layer_input = tokens.astype(jnp.float32).reshape(groups, 4, SEQ, D)
    upstream = cotangent.astype(jnp.float32).reshape(groups, 4, SEQ, D)

    def advance(totals, group_data):
        slab_in, slot_lengths, places, grad_out = group_data

        def forward(slab_value, *params):
            return block_layer(slab_value, *params, slot_lengths, places)
        result, pullback = jax.vjp(forward, slab_in, *weights)
        gradients = pullback(grad_out)
        totals = tuple((total_one + extra for total_one, extra in zip(totals, gradients[1:])))
        return (totals, (result.astype(jnp.bfloat16), gradients[0]))
    start_totals = tuple((jnp.zeros_like(entry) for entry in weights))
    totals, (results, grad_inputs) = lax.scan(advance, start_totals, (layer_input, lengths.reshape(groups, 4), positions.reshape(groups, 4, SEQ), upstream))
    return (results.reshape(SLOTS, SEQ, D), grad_inputs.reshape(SLOTS, SEQ, D), totals[0], totals[1], totals[2], totals[3], totals[4], totals[5], totals[6], totals[7], totals[8])
```

```python
import functools

import jax
import jax.numpy as jnp
from jax import lax
from jax.experimental import pallas as pl
from jax.experimental.pallas import tpu as pltpu
from jax.sharding import PartitionSpec as P

HEADS = 12
HEAD_DIM = 64
PAIR = 2 * HEAD_DIM

norm_eps = 1e-05
rope_base = 1000.0
masked_bias = -1000000000.0

bf16 = jnp.bfloat16
f32 = jnp.float32
NN = (((1,), (0,)), ((), ()))
NT = (((1,), (1,)), ((), ()))
VMEM_LIMIT = 60 * 2**20
ANY = pl.BlockSpec(memory_space=pl.ANY)


def dot(left, right, dims=NN):
    return lax.dot_general(left, right, dims, preferred_element_type=f32)


def params():
    return pltpu.CompilerParams(vmem_limit_bytes=VMEM_LIMIT)


def cost(flops, moved, exps=0):
    return pl.CostEstimate(flops=int(flops), bytes_accessed=int(moved), transcendentals=int(exps))


def piece_copies(own, other, spots, full, sems):
    col_blocks, row_blocks, rows, width = own.shape
    copies = []
    for side, source in enumerate((own, other)):
        for row in range(row_blocks):
            for col in range(col_blocks):
                start = pl.multiple_of(spots[side * row_blocks + row], 16)
                left = pl.multiple_of(spots[2 * row_blocks + col], 128)
                copies.append(
                    pltpu.make_async_copy(
                        source.at[col, row],
                        full.at[pl.ds(start, rows), pl.ds(left, width)],
                        sems.at[(side * row_blocks + row) * col_blocks + col],
                    )
                )
    return copies


def piece_count(own):
    return 2 * own.shape[0] * own.shape[1]


def turned(block, cosine, sine):
    lane = lax.broadcasted_iota(jnp.int32, block.shape, 1)
    first = (lane % HEAD_DIM) < HEAD_DIM // 2
    partner = jnp.where(
        first, pltpu.roll(block, PAIR - HEAD_DIM // 2, 1), pltpu.roll(block, HEAD_DIM // 2, 1)
    )
    return block * cosine + partner * sine


def turn_tables(places):
    half_dim = HEAD_DIM // 2
    frequency = rope_base ** (-jnp.arange(half_dim, dtype=f32) * 2.0 / HEAD_DIM)
    angles = places.astype(f32)[:, None] * frequency
    cosine = jnp.cos(angles)
    sine = jnp.sin(angles)
    return jnp.concatenate([cosine] * 4, 1), jnp.concatenate([-sine, sine, -sine, sine], 1)


def project_kernel(spots, tokens, cosine, sine, own, other, q_out, k_out, v_out, weight, sems):
    width = q_out.shape[1]

    @pl.when(pl.program_id(0) == 0)
    def _():
        copies = piece_copies(own, other, spots, weight, sems)
        for copy in copies:
            copy.start()
        for copy in copies:
            copy.wait()

    rows = tokens[...]
    cos_part = cosine[...]
    sin_part = sine[...]
    for part, out in enumerate((q_out, k_out, v_out)):
        raw = dot(rows, weight[:, part * width : (part + 1) * width])
        for pair in range(width // PAIR):
            cols = slice(pair * PAIR, (pair + 1) * PAIR)
            block = raw[:, cols]
            if part < 2:
                block = turned(block, cos_part, sin_part)
            block = block.astype(bf16)
            if part == 0:
                block = block * jnp.asarray(HEAD_DIM**-0.5, bf16)
            out[:, cols] = block


def project(spots, tokens, cosine, sine, own, other, block=256):
    rows, width = tokens.shape
    total = own.shape[0] * own.shape[3]
    row_spec = pl.BlockSpec((block, width), lambda i, *_: (i, 0))
    table = pl.BlockSpec((block, PAIR), lambda i, *_: (i, 0))
    part = total // 3
    out_spec = pl.BlockSpec((block, part), lambda i, *_: (i, 0))
    return pl.pallas_call(
        project_kernel,
        grid_spec=pltpu.PrefetchScalarGridSpec(
            num_scalar_prefetch=1,
            grid=(rows // block,),
            in_specs=[row_spec, table, table, ANY, ANY],
            out_specs=[out_spec] * 3,
            scratch_shapes=[
                pltpu.VMEM((width, total), bf16),
                pltpu.SemaphoreType.DMA((piece_count(own),)),
            ],
        ),
        out_shape=[jax.ShapeDtypeStruct((rows, part), bf16)] * 3,
        compiler_params=params(),
        cost_estimate=cost(2 * rows * width * total, 4 * rows * total + 2 * width * total),
        name="project",
    )(spots, tokens, cosine, sine, own, other)


def lane_ids(shape):
    return lax.broadcasted_iota(jnp.int32, shape, 1)


def key_bias(length, shape):
    return jnp.where(lax.broadcasted_iota(jnp.int32, shape, 0) < length, 0.0, masked_bias).astype(
        bf16
    )


def attend_kernel(length, q_ref, k_ref, v_ref, out_ref, summit_ref):
    lane_q = lane_ids(q_ref.shape)
    lane_k = lane_ids(k_ref.shape)
    bias = key_bias(length[0], k_ref.shape)
    queries = q_ref[...]
    keys = k_ref[...]
    values = v_ref[...]
    one = jnp.ones((), bf16)
    zero = jnp.zeros((), bf16)
    outs = []
    summits = []
    for head in range(2):
        mine_q = (lane_q < HEAD_DIM) if head == 0 else (lane_q >= HEAD_DIM)
        mine_k = (lane_k < HEAD_DIM) if head == 0 else (lane_k >= HEAD_DIM)
        spare = HEAD_DIM * (1 - head)
        query = jnp.where(mine_q, queries, jnp.where(lane_q == spare, one, zero))
        key = jnp.where(mine_k, keys, bias)
        value = jnp.where(mine_k, values, one)
        scores = dot(query, key, NT)
        top = jnp.max(scores, axis=1, keepdims=True)
        summed = dot(jnp.exp(scores - top).astype(bf16), value)
        totals = pltpu.roll(summed, HEAD_DIM, 1)
        outs.append(summed / totals)
        summits.append(top + jnp.log(summed))
    low = lane_q < HEAD_DIM
    out_ref[...] = jnp.where(low, outs[0], outs[1]).astype(bf16)
    summit_ref[0] = jnp.where(low, summits[1], summits[0])


def attend(length, queries, keys, values):
    rows, width = queries.shape
    seq = keys.shape[0]
    pairs = width // PAIR
    q_spec = pl.BlockSpec((rows, PAIR), lambda h, *_: (0, h))
    k_spec = pl.BlockSpec((seq, PAIR), lambda h, *_: (0, h))
    return pl.pallas_call(
        attend_kernel,
        grid_spec=pltpu.PrefetchScalarGridSpec(
            num_scalar_prefetch=1,
            grid=(pairs,),
            in_specs=[q_spec, k_spec, k_spec],
            out_specs=[q_spec, pl.BlockSpec((1, rows, PAIR), lambda h, *_: (h, 0, 0))],
        ),
        out_shape=[
            jax.ShapeDtypeStruct((rows, width), bf16),
            jax.ShapeDtypeStruct((pairs, rows, PAIR), f32),
        ],
        compiler_params=params(),
        cost_estimate=cost(16 * rows * seq * width, 12 * rows * width),
        name="attend",
    )(length, queries, keys, values)


def three_parts(value):
    high = value.astype(bf16)
    rest = value - high.astype(f32)
    middle = rest.astype(bf16)
    return high, middle, (rest - middle.astype(f32)).astype(bf16)


def attend_back_kernel(
    length, q_ref, k_ref, v_ref, out_ref, summit_ref, grad_ref, cos_ref, sin_ref, kcos, ksin, dq_ref, dk_ref, dv_ref
):
    rows = q_ref.shape[0]
    lane_q = lane_ids(q_ref.shape)
    lane_k = lane_ids(k_ref.shape)
    bias = key_bias(length[0], k_ref.shape)
    queries = q_ref[...]
    keys = k_ref[...]
    values = v_ref[...]
    grads = grad_ref[...]
    summit = three_parts(summit_ref[0])
    product = grads.astype(f32) * out_ref[...].astype(f32)
    one = jnp.ones((), bf16)
    zero = jnp.zeros((), bf16)
    grads_t = grads.T
    queries_t = queries.T
    dq, dk, dv = [], [], []
    for head in range(2):
        mine_q = (lane_q < HEAD_DIM) if head == 0 else (lane_q >= HEAD_DIM)
        mine_k = (lane_k < HEAD_DIM) if head == 0 else (lane_k >= HEAD_DIM)
        spare = HEAD_DIM * (1 - head)
        own = slice(HEAD_DIM * head, HEAD_DIM * (head + 1))
        row_dot = jnp.sum(jnp.where(mine_q, product, 0.0), axis=1, keepdims=True)
        row_dot = three_parts(jnp.broadcast_to(row_dot, (rows, PAIR)))

        def beside(main, mine, lane, parts, last):
            extra = jnp.where(lane == spare + 3, last, zero)
            for place in range(3):
                extra = jnp.where(lane == spare + place, parts[place], extra)
            return jnp.where(mine, main, extra)

        minus = (-one, -one, -one)
        query = beside(queries, mine_q, lane_q, summit, one)
        key = beside(keys, mine_k, lane_k, minus, bias)
        grad = beside(grads, mine_q, lane_q, row_dot, zero)
        value = beside(values, mine_k, lane_k, minus, zero)
        probs = jnp.exp(dot(query, key, NT))
        grad_scores = (probs * dot(grad, value, NT)).astype(bf16)
        dv.append(dot(grads_t[own], probs.astype(bf16)))
        dk.append(dot(queries_t[own], grad_scores))
        dq.append(dot(grad_scores, keys))
    grad_query = jnp.where(lane_q < HEAD_DIM, dq[0], dq[1]) * HEAD_DIM**-0.5
    grad_keys = jnp.concatenate(dk, 0).T
    dq_ref[...] = turned(grad_query, cos_ref[...], -sin_ref[...]).astype(bf16)
    dk_ref[...] = turned(grad_keys, kcos[...], -ksin[...]).astype(bf16)
    dv_ref[...] = jnp.concatenate(dv, 0).T.astype(bf16)


def attend_back(length, queries, keys, values, out, summit, grads, cosine, sine, kcos, ksin):
    rows, width = queries.shape
    seq = keys.shape[0]
    pairs = width // PAIR
    q_spec = pl.BlockSpec((rows, PAIR), lambda h, *_: (0, h))
    k_spec = pl.BlockSpec((seq, PAIR), lambda h, *_: (0, h))
    q_table = pl.BlockSpec((rows, PAIR), lambda h, *_: (0, 0))
    k_table = pl.BlockSpec((seq, PAIR), lambda h, *_: (0, 0))
    return pl.pallas_call(
        attend_back_kernel,
        grid_spec=pltpu.PrefetchScalarGridSpec(
            num_scalar_prefetch=1,
            grid=(pairs,),
            in_specs=[
                q_spec,
                k_spec,
                k_spec,
                q_spec,
                pl.BlockSpec((1, rows, PAIR), lambda h, *_: (h, 0, 0)),
                q_spec,
                q_table,
                q_table,
                k_table,
                k_table,
            ],
            out_specs=[q_spec, k_spec, k_spec],
        ),
        out_shape=[jax.ShapeDtypeStruct((count, width), bf16) for count in (rows, seq, seq)],
        compiler_params=params(),
        cost_estimate=cost(40 * rows * seq * width, 16 * rows * width),
        name="attend_back",
    )(length, queries, keys, values, out, summit, grads, cosine, sine, kcos, ksin)


def row_mean(value):
    return jnp.mean(value, axis=-1, keepdims=True)


def normalize(value):
    centered = value - row_mean(value)
    inverse = lax.rsqrt(row_mean(centered * centered) + norm_eps)
    return centered * inverse, inverse


def normalize_back(normed, inverse, gain, upstream):
    scaled = upstream * gain
    return inverse * (scaled - row_mean(scaled) - normed * row_mean(scaled * normed))


def feed_kernel(
    slot_half,
    spots_attn,
    spots_feed,
    tokens,
    context,
    cotangent,
    norms,
    out_own,
    out_other,
    gate_own,
    gate_other,
    up_own,
    up_other,
    down_own,
    down_other,
    mixed,
    hidden,
    dgate,
    dupper,
    feed_t,
    branch_t,
    context_t,
    tokens_t,
    grad_mix_one,
    grad_attn,
    grad_context,
    vectors,
    w_out,
    w_gate,
    w_up,
    w_down,
    gate_pre,
    upper,
    sems,
    chunk=768,
):
    step = pl.program_id(0)
    feed_total = w_gate.shape[1]
    loads = [
        piece_copies(out_own, out_other, spots_attn, w_out, sems.at[0]),
        piece_copies(gate_own, gate_other, spots_feed, w_gate, sems.at[1]),
        piece_copies(up_own, up_other, spots_feed, w_up, sems.at[2]),
        piece_copies(down_own, down_other, spots_feed, w_down, sems.at[3]),
    ]

    @pl.when(step == 0)
    def _():
        for group in loads:
            for copy in group:
                copy.start()
        vectors[...] = jnp.zeros_like(vectors)

    def arrive(group):
        @pl.when(step == 0)
        def _():
            for copy in loads[group]:
                copy.wait()

    gain_one = norms[0:1, :]
    shift_one = norms[1:2, :]
    gain_two = norms[2:3, :]
    shift_two = norms[3:4, :]
    token_rows = tokens[...]
    context_rows = context[...]
    tokens_t[...] = token_rows.T
    context_t[...] = context_rows.T
    arrive(0)
    normed_one, inverse_one = normalize(
        token_rows.astype(f32) + dot(context_rows, w_out[...])
    )
    out_one = normed_one * gain_one + shift_one
    feed_in = out_one.astype(bf16)
    feed_t[...] = feed_in.T
    arrive(1)
    arrive(2)
    arrive(3)
    total = out_one
    for left in range(0, feed_total, chunk):
        cols = slice(left, left + chunk)
        gate = dot(feed_in, w_gate[:, cols])
        up = dot(feed_in, w_up[:, cols])
        gate_pre[:, cols] = gate
        upper[:, cols] = up
        hid = (gate * jax.nn.sigmoid(gate) * up).astype(bf16)
        hidden[:, cols] = hid
        total = total + dot(hid, w_down[:, cols], NT)
    normed_two, inverse_two = normalize(total)
    mixed[0] = (normed_two * gain_two + shift_two).astype(bf16)
    upstream = cotangent[...].astype(f32)
    grad_mix_two = normalize_back(normed_two, inverse_two, gain_two, upstream)
    grad_branch = grad_mix_two.astype(bf16)
    branch_t[...] = grad_branch.T
    grad_out_one = grad_mix_two
    for left in range(0, feed_total, chunk):
        cols = slice(left, left + chunk)
        grad_hidden = dot(grad_branch, w_down[:, cols])
        gate = gate_pre[:, cols]
        sig = jax.nn.sigmoid(gate)
        swish = gate * sig
        grad_gate = (grad_hidden * upper[:, cols] * (sig + swish * (1.0 - sig))).astype(bf16)
        grad_up = (grad_hidden * swish).astype(bf16)
        dgate[:, cols] = grad_gate
        dupper[:, cols] = grad_up
        grad_out_one = (
            grad_out_one + dot(grad_gate, w_gate[:, cols], NT) + dot(grad_up, w_up[:, cols], NT)
        )
    vectors[0:1, :] += jnp.sum(grad_out_one * normed_one, axis=0, keepdims=True)
    vectors[1:2, :] += jnp.sum(grad_out_one, axis=0, keepdims=True)
    vectors[2:3, :] += jnp.sum(upstream * normed_two, axis=0, keepdims=True)
    vectors[3:4, :] += jnp.sum(upstream, axis=0, keepdims=True)
    grad_one = normalize_back(normed_one, inverse_one, gain_one, grad_out_one)
    grad_mix_one[...] = grad_one
    grad_rows = grad_one.astype(bf16)
    grad_attn[...] = grad_rows
    grad_context[...] = dot(grad_rows, w_out[...], NT).astype(bf16)


def feed_forward(
    slot_half, spots_attn, spots_feed, tokens, context, cotangent, norms, out_w, gate_w, up_w, down_w, block=256
):
    rows, width = tokens.shape
    feed_total = gate_w[0].shape[0] * gate_w[0].shape[3]
    half = rows // 2
    halves = half // block
    row_spec = pl.BlockSpec((block, width), lambda i, *_: (i, 0))
    wide_spec = pl.BlockSpec((block, feed_total), lambda i, *_: (i, 0))
    turned_spec = pl.BlockSpec((width, block), lambda i, *_: (0, i))
    mixed_spec = pl.BlockSpec(
        (1, block, width), lambda i, s, *_: ((i // halves + s[0]) % 2, i % halves, 0)
    )
    whole = pl.BlockSpec((8, width), lambda i, *_: (0, 0))
    count = max(piece_count(out_w[0]), piece_count(gate_w[0]))
    return pl.pallas_call(
        feed_kernel,
        grid_spec=pltpu.PrefetchScalarGridSpec(
            num_scalar_prefetch=3,
            grid=(rows // block,),
            in_specs=[row_spec, row_spec, row_spec, whole] + [ANY] * 8,
            out_specs=[mixed_spec]
            + [wide_spec] * 3
            + [turned_spec] * 4
            + [row_spec] * 3
            + [whole],
            scratch_shapes=[
                pltpu.VMEM((width, width), bf16),
                pltpu.VMEM((width, feed_total), bf16),
                pltpu.VMEM((width, feed_total), bf16),
                pltpu.VMEM((width, feed_total), bf16),
                pltpu.VMEM((block, feed_total), f32),
                pltpu.VMEM((block, feed_total), f32),
                pltpu.SemaphoreType.DMA((4, count)),
            ],
        ),
        out_shape=[jax.ShapeDtypeStruct((2, half, width), bf16)]
        + [jax.ShapeDtypeStruct((rows, feed_total), bf16)] * 3
        + [jax.ShapeDtypeStruct((width, rows), bf16)] * 4
        + [
            jax.ShapeDtypeStruct((rows, width), f32),
            jax.ShapeDtypeStruct((rows, width), bf16),
            jax.ShapeDtypeStruct((rows, width), bf16),
            jax.ShapeDtypeStruct((8, width), f32),
        ],
        compiler_params=params(),
        cost_estimate=cost(
            2 * rows * width * (6 * feed_total + 2 * width),
            rows * (6 * feed_total + 20 * width) + 6 * width * feed_total,
        ),
        name="feed_forward",
    )(slot_half, spots_attn, spots_feed, tokens, context, cotangent, norms, *out_w, *gate_w, *up_w, *down_w)


def outer_kernel(spots, left_t, right, keep, send, total):
    row_blocks, rows = keep.shape[1], keep.shape[2]
    total[...] = dot(left_t[...], right[...])
    for side, out in enumerate((keep, send)):
        for row in range(row_blocks):
            start = pl.multiple_of(spots[side * row_blocks + row], 16)
            out[0, row] = total[pl.ds(start, rows), :].astype(bf16)


def outer(spots, left_t, right, col_blocks, row_blocks, chunk=768):
    width, tokens_in = left_t.shape
    columns = right.shape[1]
    rows = width // (2 * row_blocks)
    block = columns // col_blocks
    chunk = min(chunk, block)
    per = block // chunk

    def right_index(i, s):
        return (0, s[2 * row_blocks + i // per] // chunk + i % per)

    out_spec = pl.BlockSpec((1, row_blocks, rows, chunk), lambda i, *_: (i // per, 0, 0, i % per))
    return pl.pallas_call(
        outer_kernel,
        grid_spec=pltpu.PrefetchScalarGridSpec(
            num_scalar_prefetch=1,
            grid=(columns // chunk,),
            in_specs=[
                pl.BlockSpec((width, tokens_in), lambda i, *_: (0, 0)),
                pl.BlockSpec((tokens_in, chunk), right_index),
            ],
            out_specs=[out_spec] * 2,
            scratch_shapes=[pltpu.VMEM((width, chunk), f32)],
        ),
        out_shape=[jax.ShapeDtypeStruct((col_blocks, row_blocks, rows, block), bf16)] * 2,
        compiler_params=params(),
        cost_estimate=cost(
            2 * width * tokens_in * columns, 2 * (width + tokens_in) * columns + 2 * width * tokens_in
        ),
        name="outer",
    )(spots, left_t, right)


def token_kernel(slot_half, spots, grad_q, grad_k, grad_v, grad_one, own, other, keep, send, weight, sems):
    width = grad_one.shape[1]

    @pl.when(pl.program_id(0) == 0)
    def _():
        copies = piece_copies(own, other, spots, weight, sems)
        for copy in copies:
            copy.start()
        for copy in copies:
            copy.wait()

    total = grad_one[...]
    for part, grad in enumerate((grad_q, grad_k, grad_v)):
        total = total + dot(grad[...], weight[:, part * width : (part + 1) * width], NT)
    half = pl.program_id(0) * 2 // pl.num_programs(0)

    @pl.when(half == 0)
    def _():
        send[...] = total.astype(bf16)

    @pl.when(half == 1)
    def _():
        keep[...] = total


def token_gradient(slot_half, spots, grad_raw, grad_one, own, other, block=256):
    rows, width = grad_one.shape
    half = rows // 2
    halves = half // block

    def source(i, s):
        return (i + (1 - s[0]) * halves) % (2 * halves)

    return pl.pallas_call(
        token_kernel,
        grid_spec=pltpu.PrefetchScalarGridSpec(
            num_scalar_prefetch=2,
            grid=(2 * halves,),
            in_specs=[
                pl.BlockSpec((block, width), lambda i, s, *_: (source(i, s), 0)),
                pl.BlockSpec((block, width), lambda i, s, *_: (source(i, s), 0)),
                pl.BlockSpec((block, width), lambda i, s, *_: (source(i, s), 0)),
                pl.BlockSpec((block, width), lambda i, s, *_: (source(i, s), 0)),
                ANY,
                ANY,
            ],
            out_specs=[
                pl.BlockSpec((block, width), lambda i, *_: (jnp.maximum(i - halves, 0), 0)),
                pl.BlockSpec((block, width), lambda i, *_: (jnp.minimum(i, halves - 1), 0)),
            ],
            scratch_shapes=[
                pltpu.VMEM((width, 3 * width), bf16),
                pltpu.SemaphoreType.DMA((piece_count(own),)),
            ],
        ),
        out_shape=[
            jax.ShapeDtypeStruct((half, width), f32),
            jax.ShapeDtypeStruct((half, width), bf16),
        ],
        compiler_params=params(),
        cost_estimate=cost(6 * rows * width * width, 14 * rows * width + 6 * width * width),
        name="token_gradient",
    )(slot_half, spots, *grad_raw, grad_one, own, other)


class Transfers:
    def __init__(self, mesh):
        self.fsdp = mesh.shape["fsdp"]
        self.ctx = mesh.shape["ctx"]
        self.tp = mesh.shape["tp"]
        self.levels = self.fsdp // 2
        place = lax.axis_index("fsdp")
        self.z = place // 2
        self.core = place % 2
        self.x = lax.axis_index("ctx")
        self.y = lax.axis_index("tp")
        self.paired = self.ctx == 2 and self.tp == 2 and self.fsdp % 2 == 0

    def swap_slots(self, value):
        return lax.ppermute(value, "ctx", [(i, i ^ 1) for i in range(self.ctx)])

    def swap(self, value, axis):
        return lax.ppermute(value, axis, [(0, 1), (1, 0)])

    def swap_core(self, value):
        return lax.ppermute(value, "fsdp", [(i, i ^ 1) for i in range(self.fsdp)])

    def shift(self, value, step):
        pairs = [
            (2 * level + core, 2 * ((level + step) % self.levels) + core)
            for level in range(self.levels)
            for core in range(2)
        ]
        return lax.ppermute(value, "fsdp", pairs)

    def row_spots(self, rows, split, sign):
        spots = []
        for side in range(2):
            for part in range(2):
                for step in range(self.levels):
                    level = (self.z + sign * step + self.levels) % self.levels
                    block = 2 * level + jnp.bitwise_xor(self.core, side)
                    spots.append(2 * rows * block + rows * jnp.bitwise_xor(split, part))
        return spots

    def spots(self, rows, split, sign, width=None):
        found = self.row_spots(rows, split, sign)
        if width is None:
            found = found + [jnp.zeros((), jnp.int32)]
        else:
            found = found + [self.y * width, (1 - self.y) * width]
        return jnp.stack(found).astype(jnp.int32)

    def levels_of(self, block):
        return jnp.stack([block] + [self.shift(block, step) for step in range(1, self.levels)])

    def pair(self, block, axis, at):
        return jnp.stack([block, self.swap(block, axis)], at)

    def gather_attention(self, shard):
        half = shard.shape[0] // 2
        block = lax.dynamic_slice_in_dim(shard, self.y * half, half, 0)
        own = self.pair(self.levels_of(block), "tp", 0)
        own = own.reshape((1, 2 * self.levels) + block.shape)
        return own, self.swap_core(own)

    def gather_feed(self, shard, order):
        half = shard.shape[0] // 2
        block = lax.dynamic_slice_in_dim(shard, self.x * half, half, 0)
        own = self.levels_of(block)
        if order == "yx":
            own = self.pair(self.pair(own, "tp", 0), "ctx", 1)
        else:
            own = self.pair(self.pair(own, "ctx", 0), "tp", 0)
        own = own.reshape((2, 2 * self.levels) + block.shape)
        return own, self.swap_core(own)

    def add(self, left, right):
        return (left.astype(f32) + right.astype(f32)).astype(bf16)

    def finish(self, value):
        total = value[0].astype(f32)
        for step in range(1, self.levels):
            total = total + self.shift(value[step], step).astype(f32)
        total = total.astype(bf16)
        other = self.swap(total, "ctx")
        low = jnp.where(self.x == 0, total, other)
        high = jnp.where(self.x == 0, other, total)
        return low, high

    def reduce_feed(self, keep, send, order):
        rows, width = keep.shape[2:]
        value = self.add(keep, self.swap_core(send))
        value = value.reshape(2, 2, self.levels, rows, width)
        if order == "yx":
            value = self.add(value[0], self.swap(value[1], "tp"))
            value = self.add(value[0], self.swap(value[1], "ctx"))
        else:
            value = self.add(value[:, 0], self.swap(value[:, 1], "ctx"))
            value = self.add(value[0], self.swap(value[1], "tp"))
        return jnp.concatenate(self.finish(value), 0).astype(f32)

    def reduce_attention(self, keep, send):
        rows, width = keep.shape[2:]
        value = self.add(keep, self.swap_core(send))
        value = value.reshape(2, self.levels, rows, width)
        value = self.add(value[0], self.swap(value[1], "ctx"))
        value = self.add(value, self.swap(value, "tp"))
        return self.finish(value)

    def vector_pieces(self, vectors, rows, width):
        shard = vectors.shape[1] // self.fsdp
        value = vectors.astype(bf16).reshape(2, 2, self.levels, 2, shard)
        value = jnp.where(self.x == 0, value, value[::-1])
        value = lax.dynamic_slice_in_dim(
            jnp.concatenate([value, value], 2), self.z, self.levels, 2
        )
        value = jnp.where(self.core == 0, value, value[:, :, :, ::-1])
        value = value.transpose(3, 0, 2, 1, 4).reshape(2, 1, 2 * self.levels, 2, shard)
        value = jnp.pad(value, ((0, 0),) * 3 + ((0, rows - 2), (0, width - shard)))
        return value[0], value[1]


def on_device(
    mesh,
    tokens,
    query_key_value_weight,
    output_weight,
    gate_weight,
    up_weight,
    down_weight,
    gain_one,
    shift_one,
    gain_two,
    shift_two,
    lengths,
    positions,
    cotangent,
):
    move = Transfers(mesh)
    shard, model_width = query_key_value_weight.shape[0], tokens.shape[2]
    feed_width = gate_weight.shape[1]
    slot = move.x % 2
    half_rows = tokens.shape[1]

    def to_slot(value):
        keep = jnp.where(slot == 0, value[0], value[1])
        other = move.swap_slots(jnp.where(slot == 0, value[1], value[0]))
        first = jnp.where(slot == 0, keep, other)
        second = jnp.where(slot == 0, other, keep)
        return jnp.concatenate([first, second], 0)

    def from_slot(keep, other):
        return jnp.where(slot == 0, jnp.stack([keep, other]), jnp.stack([other, keep]))

    slot_tokens = to_slot(tokens)
    slot_places = to_slot(positions)
    length = jnp.where(slot == 0, lengths[0:1], lengths[1:2])
    slot_half = slot[None].astype(jnp.int32)
    norms = lax.all_gather(
        jnp.pad(jnp.stack([gain_one, shift_one, gain_two, shift_two]), ((0, 4), (0, 0))),
        "fsdp",
        axis=1,
        tiled=True,
    ).astype(f32)

    down_turned = down_weight.T
    if move.paired:
        half = shard // 2
        attn_in = move.spots(half, move.y, -1)
        attn_out = move.spots(half, move.x, 1)
        feed_in_spots = move.spots(half, move.x, -1, feed_width)
        feed_out_spots = move.spots(half, move.x, 1, feed_width)
        qkv_w = move.gather_attention(query_key_value_weight)
        out_w = move.gather_attention(output_weight)
        gate_w = move.gather_feed(gate_weight, "yx")
        up_w = move.gather_feed(up_weight, "xy")
        down_w = move.gather_feed(down_turned, "yx")
        attn_blocks, feed_cols, feed_blocks = 2 * move.levels, 2, 2 * move.levels
    else:
        middle = model_width // 2
        attn_in = jnp.asarray([0, middle, 0], jnp.int32)
        attn_out = feed_in_spots = feed_out_spots = attn_in

        def whole(value, axes):
            value = lax.all_gather(value, "fsdp", axis=0, tiled=True)
            if axes:
                value = lax.all_gather(value, "tp", axis=1, tiled=True)
            return value[None, None, :middle], value[None, None, middle:]

        qkv_w = whole(query_key_value_weight, False)
        out_w = whole(output_weight, False)
        gate_w = whole(gate_weight, True)
        up_w = whole(up_weight, True)
        down_w = whole(down_turned, True)
        attn_blocks, feed_cols, feed_blocks = 1, 1, 1

    cosine, sine = turn_tables(slot_places)
    queries, key_rows, values = project(attn_in, slot_tokens, cosine, sine, *qkv_w)
    mates = move.ctx // 2
    if mates > 1:
        groups = [[2 * j + s for j in range(mates)] for s in range(2)]

        def gather_rows(value):
            return lax.all_gather(value, "ctx", axis=0, tiled=True, axis_index_groups=groups)

        key_rows = gather_rows(key_rows)
        values = gather_rows(values)
        key_cos, key_sin = jnp.ones((key_rows.shape[0], PAIR), f32), jnp.zeros(
            (key_rows.shape[0], PAIR), f32
        )
    else:
        key_cos, key_sin = cosine, sine
    context, summit = attend(length, queries, key_rows, values)
    slot_cotangent = to_slot(cotangent)
    (
        mixed,
        hidden,
        grad_gate,
        grad_upper,
        feed_t,
        branch_t,
        context_t,
        tokens_t,
        grad_mix_one,
        grad_attn,
        grad_context,
        vectors,
    ) = feed_forward(
        slot_half,
        attn_in,
        feed_in_spots,
        slot_tokens,
        context,
        slot_cotangent,
        norms,
        out_w,
        gate_w,
        up_w,
        down_w,
    )
    mixed_out = from_slot(mixed[0], move.swap_slots(mixed[1]))
    pieces_down = outer(feed_out_spots, branch_t, hidden, feed_cols, feed_blocks)
    pieces_gate = outer(feed_out_spots, feed_t, grad_gate, feed_cols, feed_blocks)
    pieces_up = outer(feed_out_spots, feed_t, grad_upper, feed_cols, feed_blocks)
    pieces_out = outer(attn_out, context_t, grad_attn, 1, attn_blocks)
    grad_raw = attend_back(
        length,
        queries,
        key_rows,
        values,
        context,
        summit,
        grad_context,
        cosine,
        sine,
        key_cos,
        key_sin,
    )
    if mates > 1:
        rows = slot_tokens.shape[0]
        keys_part = lax.psum_scatter(
            jnp.stack(grad_raw[1:]).astype(f32),
            "ctx",
            scatter_dimension=1,
            axis_index_groups=groups,
            tiled=True,
        )
        turned_keys = keys_part[0].reshape(rows, HEADS, 2, HEAD_DIM // 2)
        cos_half = cosine[:, None, : HEAD_DIM // 2]
        sin_half = sine[:, None, HEAD_DIM // 2 : HEAD_DIM]
        first, second = turned_keys[:, :, 0], turned_keys[:, :, 1]
        turned_keys = jnp.stack(
            [first * cos_half + second * sin_half, second * cos_half - first * sin_half], 2
        ).reshape(rows, model_width)
        grad_raw = (grad_raw[0], turned_keys.astype(bf16), keys_part[1].astype(bf16))
    pieces_qkv = [outer(attn_out, tokens_t, grad_raw[part], 1, attn_blocks) for part in range(3)]
    keep_rows, send_rows = token_gradient(slot_half, attn_in, grad_raw, grad_mix_one, *qkv_w)
    grad_tokens = from_slot(keep_rows, move.swap_slots(send_rows).astype(f32))

    if move.paired:
        down_gradient = move.reduce_feed(*pieces_down, "xy").T
        gate_gradient = move.reduce_feed(*pieces_gate, "yx")
        up_gradient = move.reduce_feed(*pieces_up, "xy")
        extra = move.vector_pieces(vectors[:4], 16, model_width)
        low, high = move.reduce_attention(
            *[jnp.concatenate([piece, more], 2) for piece, more in zip(pieces_out, extra)]
        )
        out_gradient = jnp.concatenate([low[:half], high[:half]], 0).astype(f32)
        vector_grads = [
            row[half + place, :shard].astype(f32) for row in (low, high) for place in range(2)
        ]
        qkv_gradient = jnp.concatenate(
            [jnp.concatenate(move.reduce_attention(*pieces), 0) for pieces in pieces_qkv], 1
        ).astype(f32)
    else:

        def scatter(pieces, axes, other):
            value = jnp.concatenate([piece[0, 0] for piece in pieces], 0)
            value = lax.psum(value, axes)
            value = lax.psum_scatter(value, "fsdp", scatter_dimension=0, tiled=True)
            if other:
                value = lax.psum_scatter(value, "tp", scatter_dimension=1, tiled=True)
            return value.astype(f32)

        down_gradient = scatter(pieces_down, "ctx", True).T
        gate_gradient = scatter(pieces_gate, "ctx", True)
        up_gradient = scatter(pieces_up, "ctx", True)
        out_gradient = scatter(pieces_out, ("ctx", "tp"), False)
        qkv_gradient = jnp.concatenate(
            [scatter(pieces, ("ctx", "tp"), False) for pieces in pieces_qkv], 1
        )
        summed = lax.psum(vectors, ("ctx", "tp"))
        summed = lax.psum_scatter(summed, "fsdp", scatter_dimension=1, tiled=True)
        vector_grads = [summed[place] for place in range(4)]
    return (
        mixed_out,
        grad_tokens,
        qkv_gradient,
        out_gradient,
        gate_gradient,
        up_gradient,
        down_gradient,
        *vector_grads,
    )


def solution(mesh):
    in_specs = (
        P(("fsdp", "tp"), "ctx", None),
        P("fsdp", None),
        P("fsdp", None),
        P("fsdp", "tp"),
        P("fsdp", "tp"),
        P("tp", "fsdp"),
        P("fsdp"),
        P("fsdp"),
        P("fsdp"),
        P("fsdp"),
        P(("fsdp", "tp")),
        P(("fsdp", "tp"), "ctx"),
        P(("fsdp", "tp"), "ctx", None),
    )
    out_specs = (
        P(("fsdp", "tp"), "ctx", None),
        P(("fsdp", "tp"), "ctx", None),
        P("fsdp", None),
        P("fsdp", None),
        P("fsdp", "tp"),
        P("fsdp", "tp"),
        P("tp", "fsdp"),
        P("fsdp"),
        P("fsdp"),
        P("fsdp"),
        P("fsdp"),
    )
    return jax.shard_map(
        functools.partial(on_device, mesh),
        mesh=mesh,
        in_specs=in_specs,
        out_specs=out_specs,
        check_vma=False,
    )
```

```python
import functools

import jax
import jax.numpy as jnp
from jax import lax
from jax.experimental import pallas as pl
from jax.experimental.pallas import tpu as pltpu
from jax.sharding import PartitionSpec as P

HEADS = 12
HEAD_DIM = 64
PAIR = 2 * HEAD_DIM

norm_eps = 1e-05
rope_base = 1000.0
masked_bias = -1000000000.0

bf16 = jnp.bfloat16
f32 = jnp.float32
NN = (((1,), (0,)), ((), ()))
NT = (((1,), (1,)), ((), ()))
VMEM_LIMIT = 60 * 2**20
ANY = pl.BlockSpec(memory_space=pl.ANY)


def dot(left, right, dims=NN):
    return lax.dot_general(left, right, dims, preferred_element_type=f32)


def params():
    return pltpu.CompilerParams(vmem_limit_bytes=VMEM_LIMIT)


def cost(flops, moved, exps=0):
    return pl.CostEstimate(flops=int(flops), bytes_accessed=int(moved), transcendentals=int(exps))


def fence(*values):
    def nothing(*refs):
        pass

    return pl.pallas_call(
        nothing,
        in_specs=[ANY] * len(values),
        out_specs=[ANY] * len(values),
        out_shape=[jax.ShapeDtypeStruct(value.shape, value.dtype) for value in values],
        input_output_aliases={place: place for place in range(len(values))},
        compiler_params=params(),
        name="fence",
    )(*values)


def piece_copies(own, other, spots, full, sems):
    col_blocks, row_blocks, rows, width = own.shape
    copies = []
    for side, source in enumerate((own, other)):
        for row in range(row_blocks):
            for col in range(col_blocks):
                start = pl.multiple_of(spots[side * row_blocks + row], 16)
                left = pl.multiple_of(spots[2 * row_blocks + col], 128)
                copies.append(
                    pltpu.make_async_copy(
                        source.at[col, row],
                        full.at[pl.ds(start, rows), pl.ds(left, width)],
                        sems.at[(side * row_blocks + row) * col_blocks + col],
                    )
                )
    return copies


def piece_count(own):
    return 2 * own.shape[0] * own.shape[1]


def turned(block, cosine, sine):
    lane = lax.broadcasted_iota(jnp.int32, block.shape, 1)
    first = (lane % HEAD_DIM) < HEAD_DIM // 2
    partner = jnp.where(
        first, pltpu.roll(block, PAIR - HEAD_DIM // 2, 1), pltpu.roll(block, HEAD_DIM // 2, 1)
    )
    return block * cosine + partner * sine


def turn_tables(places):
    half_dim = HEAD_DIM // 2
    frequency = rope_base ** (-jnp.arange(half_dim, dtype=f32) * 2.0 / HEAD_DIM)
    angles = places.astype(f32)[:, None] * frequency
    cosine = jnp.cos(angles)
    sine = jnp.sin(angles)
    return jnp.concatenate([cosine] * 4, 1), jnp.concatenate([-sine, sine, -sine, sine], 1)


def project_kernel(spots, tokens, cosine, sine, own, other, q_out, k_out, v_out, weight, sems):
    width = q_out.shape[1]

    @pl.when(pl.program_id(0) == 0)
    def _():
        copies = piece_copies(own, other, spots, weight, sems)
        for copy in copies:
            copy.start()
        for copy in copies:
            copy.wait()

    rows = tokens[...]
    cos_part = cosine[...]
    sin_part = sine[...]
    for part, out in enumerate((q_out, k_out, v_out)):
        raw = dot(rows, weight[:, part * width : (part + 1) * width])
        for pair in range(width // PAIR):
            cols = slice(pair * PAIR, (pair + 1) * PAIR)
            block = raw[:, cols]
            if part < 2:
                block = turned(block, cos_part, sin_part)
            block = block.astype(bf16)
            if part == 0:
                block = block * jnp.asarray(HEAD_DIM**-0.5, bf16)
            out[:, cols] = block


def project(spots, tokens, cosine, sine, own, other, block=256):
    rows, width = tokens.shape
    total = own.shape[0] * own.shape[3]
    row_spec = pl.BlockSpec((block, width), lambda i, *_: (i, 0))
    table = pl.BlockSpec((block, PAIR), lambda i, *_: (i, 0))
    part = total // 3
    out_spec = pl.BlockSpec((block, part), lambda i, *_: (i, 0))
    return pl.pallas_call(
        project_kernel,
        grid_spec=pltpu.PrefetchScalarGridSpec(
            num_scalar_prefetch=1,
            grid=(rows // block,),
            in_specs=[row_spec, table, table, ANY, ANY],
            out_specs=[out_spec] * 3,
            scratch_shapes=[
                pltpu.VMEM((width, total), bf16),
                pltpu.SemaphoreType.DMA((piece_count(own),)),
            ],
        ),
        out_shape=[jax.ShapeDtypeStruct((rows, part), bf16)] * 3,
        compiler_params=params(),
        cost_estimate=cost(2 * rows * width * total, 4 * rows * total + 2 * width * total),
        name="project",
    )(spots, tokens, cosine, sine, own, other)


def lane_ids(shape):
    return lax.broadcasted_iota(jnp.int32, shape, 1)


def key_bias(length, shape):
    return jnp.where(lax.broadcasted_iota(jnp.int32, shape, 0) < length, 0.0, masked_bias).astype(
        bf16
    )


def attend_kernel(length, q_ref, k_ref, v_ref, out_ref, summit_ref):
    lane_q = lane_ids(q_ref.shape)
    lane_k = lane_ids(k_ref.shape)
    bias = key_bias(length[0], k_ref.shape)
    queries = q_ref[...]
    keys = k_ref[...]
    values = v_ref[...]
    one = jnp.ones((), bf16)
    zero = jnp.zeros((), bf16)
    outs = []
    summits = []
    for head in range(2):
        mine_q = (lane_q < HEAD_DIM) if head == 0 else (lane_q >= HEAD_DIM)
        mine_k = (lane_k < HEAD_DIM) if head == 0 else (lane_k >= HEAD_DIM)
        spare = HEAD_DIM * (1 - head)
        query = jnp.where(mine_q, queries, jnp.where(lane_q == spare, one, zero))
        key = jnp.where(mine_k, keys, bias)
        value = jnp.where(mine_k, values, one)
        scores = dot(query, key, NT)
        top = jnp.max(scores, axis=1, keepdims=True)
        summed = dot(jnp.exp(scores - top).astype(bf16), value)
        totals = pltpu.roll(summed, HEAD_DIM, 1)
        outs.append(summed / totals)
        summits.append(top + jnp.log(summed))
    low = lane_q < HEAD_DIM
    out_ref[...] = jnp.where(low, outs[0], outs[1]).astype(bf16)
    summit_ref[0] = jnp.where(low, summits[1], summits[0])


def attend(length, queries, keys, values):
    rows, width = queries.shape
    seq = keys.shape[0]
    pairs = width // PAIR
    q_spec = pl.BlockSpec((rows, PAIR), lambda h, *_: (0, h))
    k_spec = pl.BlockSpec((seq, PAIR), lambda h, *_: (0, h))
    return pl.pallas_call(
        attend_kernel,
        grid_spec=pltpu.PrefetchScalarGridSpec(
            num_scalar_prefetch=1,
            grid=(pairs,),
            in_specs=[q_spec, k_spec, k_spec],
            out_specs=[q_spec, pl.BlockSpec((1, rows, PAIR), lambda h, *_: (h, 0, 0))],
        ),
        out_shape=[
            jax.ShapeDtypeStruct((rows, width), bf16),
            jax.ShapeDtypeStruct((pairs, rows, PAIR), f32),
        ],
        compiler_params=params(),
        cost_estimate=cost(16 * rows * seq * width, 12 * rows * width),
        name="attend",
    )(length, queries, keys, values)


def three_parts(value):
    high = value.astype(bf16)
    rest = value - high.astype(f32)
    middle = rest.astype(bf16)
    return high, middle, (rest - middle.astype(f32)).astype(bf16)


def attend_back_kernel(
    length, q_ref, k_ref, v_ref, out_ref, summit_ref, grad_ref, cos_ref, sin_ref, kcos, ksin, *refs
):
    dq_ref, dk_ref, dv_ref = refs[-3:]
    rows = q_ref.shape[0]
    lane_q = lane_ids(q_ref.shape)
    lane_k = lane_ids(k_ref.shape)
    bias = key_bias(length[0], k_ref.shape)
    queries = q_ref[...]
    keys = k_ref[...]
    values = v_ref[...]
    grads = grad_ref[...]
    summit = three_parts(summit_ref[0])
    product = grads.astype(f32) * out_ref[...].astype(f32)
    one = jnp.ones((), bf16)
    zero = jnp.zeros((), bf16)
    grads_t = grads.T
    queries_t = queries.T
    dq, dk, dv = [], [], []
    for head in range(2):
        mine_q = (lane_q < HEAD_DIM) if head == 0 else (lane_q >= HEAD_DIM)
        mine_k = (lane_k < HEAD_DIM) if head == 0 else (lane_k >= HEAD_DIM)
        spare = HEAD_DIM * (1 - head)
        own = slice(HEAD_DIM * head, HEAD_DIM * (head + 1))
        row_dot = jnp.sum(jnp.where(mine_q, product, 0.0), axis=1, keepdims=True)
        row_dot = three_parts(jnp.broadcast_to(row_dot, (rows, PAIR)))

        def beside(main, mine, lane, parts, last):
            extra = jnp.where(lane == spare + 3, last, zero)
            for place in range(3):
                extra = jnp.where(lane == spare + place, parts[place], extra)
            return jnp.where(mine, main, extra)

        minus = (-one, -one, -one)
        query = beside(queries, mine_q, lane_q, summit, one)
        key = beside(keys, mine_k, lane_k, minus, bias)
        grad = beside(grads, mine_q, lane_q, row_dot, zero)
        value = beside(values, mine_k, lane_k, minus, zero)
        probs = jnp.exp(dot(query, key, NT))
        grad_scores = (probs * dot(grad, value, NT)).astype(bf16)
        dv.append(dot(grads_t[own], probs.astype(bf16)))
        dk.append(dot(queries_t[own], grad_scores))
        dq.append(dot(grad_scores, keys))
    grad_query = jnp.where(lane_q < HEAD_DIM, dq[0], dq[1]) * HEAD_DIM**-0.5
    grad_keys = jnp.concatenate(dk, 0).T
    dq_ref[...] = turned(grad_query, cos_ref[...], -sin_ref[...]).astype(bf16)
    dk_ref[...] = turned(grad_keys, kcos[...], -ksin[...]).astype(bf16)
    dv_ref[...] = jnp.concatenate(dv, 0).T.astype(bf16)


def attend_back(
    length, queries, keys, values, out, summit, grads, cosine, sine, kcos, ksin, first, pairs, before
):
    rows, width = queries.shape
    seq = keys.shape[0]
    q_spec = pl.BlockSpec((rows, PAIR), lambda h, *_: (0, h + first))
    k_spec = pl.BlockSpec((seq, PAIR), lambda h, *_: (0, h + first))
    q_table = pl.BlockSpec((rows, PAIR), lambda h, *_: (0, 0))
    k_table = pl.BlockSpec((seq, PAIR), lambda h, *_: (0, 0))
    return pl.pallas_call(
        attend_back_kernel,
        grid_spec=pltpu.PrefetchScalarGridSpec(
            num_scalar_prefetch=1,
            grid=(pairs,),
            in_specs=[
                q_spec,
                k_spec,
                k_spec,
                q_spec,
                pl.BlockSpec((1, rows, PAIR), lambda h, *_: (h + first, 0, 0)),
                q_spec,
                q_table,
                q_table,
                k_table,
                k_table,
            ]
            + [ANY] * len(before),
            out_specs=[q_spec, k_spec, k_spec],
        ),
        out_shape=[jax.ShapeDtypeStruct((count, width), bf16) for count in (rows, seq, seq)],
        input_output_aliases={11 + place: place for place in range(len(before))},
        compiler_params=params(),
        cost_estimate=cost(40 * rows * seq * PAIR * pairs, 16 * rows * PAIR * pairs),
        name="attend_back",
    )(length, queries, keys, values, out, summit, grads, cosine, sine, kcos, ksin, *before)


def row_mean(value):
    return jnp.mean(value, axis=-1, keepdims=True)


def normalize(value):
    centered = value - row_mean(value)
    inverse = lax.rsqrt(row_mean(centered * centered) + norm_eps)
    return centered * inverse, inverse


def normalize_back(normed, inverse, gain, upstream):
    scaled = upstream * gain
    return inverse * (scaled - row_mean(scaled) - normed * row_mean(scaled * normed))


def feed_kernel(plan, slot_half, spots, tokens, context, cotangent, norms, *refs, chunk=768):
    sources = refs[: plan["sources"]]
    (
        mixed,
        hidden,
        dgate,
        dupper,
        feed_t,
        branch_t,
        context_t,
        tokens_t,
        grad_mix_one,
        grad_attn,
        grad_context,
        vectors,
        w_out,
        w_gate,
        w_up,
        w_down,
        gate_pre,
        upper,
        sems,
    ) = refs[plan["sources"] :]
    step = pl.program_id(0)
    feed_total = w_gate.shape[1]
    loads = []
    for group, (weight, pieces) in enumerate(
        zip((w_out, w_gate, w_up, w_down), plan["pieces"])
    ):
        copies = []
        for place, (source, first, top, left, row, col, rows, cols) in enumerate(pieces):
            if isinstance(row, tuple):
                row = pl.multiple_of(spots[row[0]], 16)
                col = pl.multiple_of(spots[col[0]], 128)
            copies.append(
                pltpu.make_async_copy(
                    sources[source].at[first, pl.ds(top, rows), pl.ds(left, cols)],
                    weight.at[pl.ds(row, rows), pl.ds(col, cols)],
                    sems.at[group, place],
                )
            )
        loads.append(copies)

    @pl.when(step == 0)
    def _():
        for group in loads:
            for copy in group:
                copy.start()
        vectors[...] = jnp.zeros_like(vectors)

    def arrive(group):
        @pl.when(step == 0)
        def _():
            for copy in loads[group]:
                copy.wait()

    gain_one = norms[0:1, :]
    shift_one = norms[1:2, :]
    gain_two = norms[2:3, :]
    shift_two = norms[3:4, :]
    token_rows = tokens[...]
    context_rows = context[...]
    tokens_t[...] = token_rows.T
    context_t[...] = context_rows.T
    arrive(0)
    normed_one, inverse_one = normalize(
        token_rows.astype(f32) + dot(context_rows, w_out[...])
    )
    out_one = normed_one * gain_one + shift_one
    feed_in = out_one.astype(bf16)
    feed_t[...] = feed_in.T
    arrive(1)
    arrive(2)
    arrive(3)
    total = out_one
    for left in range(0, feed_total, chunk):
        cols = slice(left, left + chunk)
        gate = dot(feed_in, w_gate[:, cols])
        up = dot(feed_in, w_up[:, cols])
        gate_pre[:, cols] = gate
        upper[:, cols] = up
        hid = (gate * jax.nn.sigmoid(gate) * up).astype(bf16)
        hidden[:, cols] = hid
        total = total + dot(hid, w_down[:, cols], NT)
    normed_two, inverse_two = normalize(total)
    mixed[0] = (normed_two * gain_two + shift_two).astype(bf16)
    upstream = cotangent[...].astype(f32)
    grad_mix_two = normalize_back(normed_two, inverse_two, gain_two, upstream)
    grad_branch = grad_mix_two.astype(bf16)
    branch_t[...] = grad_branch.T
    grad_out_one = grad_mix_two
    for left in range(0, feed_total, chunk):
        cols = slice(left, left + chunk)
        grad_hidden = dot(grad_branch, w_down[:, cols])
        gate = gate_pre[:, cols]
        sig = jax.nn.sigmoid(gate)
        swish = gate * sig
        grad_gate = (grad_hidden * upper[:, cols] * (sig + swish * (1.0 - sig))).astype(bf16)
        grad_up = (grad_hidden * swish).astype(bf16)
        dgate[:, cols] = grad_gate
        dupper[:, cols] = grad_up
        grad_out_one = (
            grad_out_one + dot(grad_gate, w_gate[:, cols], NT) + dot(grad_up, w_up[:, cols], NT)
        )
    vectors[0:1, :] += jnp.sum(grad_out_one * normed_one, axis=0, keepdims=True)
    vectors[1:2, :] += jnp.sum(grad_out_one, axis=0, keepdims=True)
    vectors[2:3, :] += jnp.sum(upstream * normed_two, axis=0, keepdims=True)
    vectors[3:4, :] += jnp.sum(upstream, axis=0, keepdims=True)
    grad_one = normalize_back(normed_one, inverse_one, gain_one, grad_out_one)
    grad_mix_one[...] = grad_one
    grad_rows = grad_one.astype(bf16)
    grad_attn[...] = grad_rows
    grad_context[...] = dot(grad_rows, w_out[...], NT).astype(bf16)


def feed_forward(
    plan, sources, slot_half, spots, tokens, context, cotangent, norms, feed_total, block=256
):
    rows, width = tokens.shape
    half = rows // 2
    halves = half // block
    row_spec = pl.BlockSpec((block, width), lambda i, *_: (i, 0))
    wide_spec = pl.BlockSpec((block, feed_total), lambda i, *_: (i, 0))
    turned_spec = pl.BlockSpec((width, block), lambda i, *_: (0, i))
    mixed_spec = pl.BlockSpec(
        (1, block, width), lambda i, s, *_: ((i // halves + s[0]) % 2, i % halves, 0)
    )
    whole = pl.BlockSpec((8, width), lambda i, *_: (0, 0))
    vector_spec = pl.BlockSpec((PAIR, width), lambda i, *_: (0, 0))
    count = max(len(pieces) for pieces in plan["pieces"])
    return pl.pallas_call(
        functools.partial(feed_kernel, plan),
        grid_spec=pltpu.PrefetchScalarGridSpec(
            num_scalar_prefetch=2,
            grid=(rows // block,),
            in_specs=[row_spec, row_spec, row_spec, whole] + [ANY] * len(sources),
            out_specs=[mixed_spec]
            + [wide_spec] * 3
            + [turned_spec] * 4
            + [row_spec] * 3
            + [vector_spec],
            scratch_shapes=[
                pltpu.VMEM((width, width), bf16),
                pltpu.VMEM((width, feed_total), bf16),
                pltpu.VMEM((width, feed_total), bf16),
                pltpu.VMEM((width, feed_total), bf16),
                pltpu.VMEM((block, feed_total), f32),
                pltpu.VMEM((block, feed_total), f32),
                pltpu.SemaphoreType.DMA((4, count)),
            ],
        ),
        out_shape=[jax.ShapeDtypeStruct((2, half, width), bf16)]
        + [jax.ShapeDtypeStruct((rows, feed_total), bf16)] * 3
        + [jax.ShapeDtypeStruct((width, rows), bf16)] * 4
        + [
            jax.ShapeDtypeStruct((rows, width), f32),
            jax.ShapeDtypeStruct((rows, width), bf16),
            jax.ShapeDtypeStruct((rows, width), bf16),
            jax.ShapeDtypeStruct((PAIR, width), f32),
        ],
        compiler_params=params(),
        cost_estimate=cost(
            2 * rows * width * (6 * feed_total + 2 * width),
            rows * (6 * feed_total + 20 * width) + 6 * width * feed_total,
        ),
        name="feed_forward",
    )(slot_half, spots, tokens, context, cotangent, norms, *sources)


def outer_kernel(spots, left_t, right, keep, send, total):
    row_blocks, rows = keep.shape[1], keep.shape[2]
    total[...] = dot(left_t[...], right[...])
    for side, out in enumerate((keep, send)):
        for row in range(row_blocks):
            start = pl.multiple_of(spots[side * row_blocks + row], 16)
            out[0, row] = total[pl.ds(start, rows), :].astype(bf16)


def outer(spots, left_t, right, col_blocks, row_blocks, chunk=768, parts=1, part=0):
    width, tokens_in = left_t.shape
    columns = right.shape[1]
    rows = width // (2 * row_blocks)
    block = columns // col_blocks // parts
    chunk = min(chunk, block)
    per = block // chunk

    def right_index(i, s):
        return (0, s[2 * row_blocks + i // per] // chunk + part * per + i % per)

    out_spec = pl.BlockSpec((1, row_blocks, rows, chunk), lambda i, *_: (i // per, 0, 0, i % per))
    return pl.pallas_call(
        outer_kernel,
        grid_spec=pltpu.PrefetchScalarGridSpec(
            num_scalar_prefetch=1,
            grid=(col_blocks * per,),
            in_specs=[
                pl.BlockSpec((width, tokens_in), lambda i, *_: (0, 0)),
                pl.BlockSpec((tokens_in, chunk), right_index),
            ],
            out_specs=[out_spec] * 2,
            scratch_shapes=[pltpu.VMEM((width, chunk), f32)],
        ),
        out_shape=[jax.ShapeDtypeStruct((col_blocks, row_blocks, rows, block), bf16)] * 2,
        compiler_params=params(),
        cost_estimate=cost(
            2 * width * tokens_in * columns // parts,
            2 * (width + tokens_in) * columns // parts + 2 * width * tokens_in,
        ),
        name="outer",
    )(spots, left_t, right)


def outer_rows_kernel(tokens_t, *refs):
    out = refs[-1]
    parts = refs[:3]
    left = 0
    for part in parts:
        cols = slice(left, left + part.shape[1])
        out[:, cols] = dot(tokens_t[...], part[...]).astype(bf16)
        left += part.shape[1]
    if len(refs) > 4:
        context_t, grad_attn, vectors = refs[3:6]
        width = grad_attn.shape[1]
        out[:, left : left + width] = dot(context_t[...], grad_attn[...]).astype(bf16)
        out[:, left + width :] = vectors[...].astype(bf16).T


def outer_rows(tokens_t, parts, first, pairs, more=()):
    width, tokens_in = tokens_t.shape
    columns = pairs * PAIR
    total = 3 * columns + (width + PAIR if more else 0)
    part_spec = pl.BlockSpec((pl.Element(tokens_in), pl.Element(columns)), lambda i: (0, first * PAIR))
    whole = [pl.BlockSpec(value.shape, lambda i: (0, 0)) for value in more]
    return pl.pallas_call(
        outer_rows_kernel,
        grid=(1,),
        in_specs=[pl.BlockSpec((width, tokens_in), lambda i: (0, 0))] + [part_spec] * 3 + whole,
        out_specs=pl.BlockSpec((width, total), lambda i: (0, 0)),
        out_shape=jax.ShapeDtypeStruct((width, total), bf16),
        compiler_params=params(),
        cost_estimate=cost(2 * width * tokens_in * total, 2 * (width + tokens_in) * total),
        name="outer_rows",
    )(tokens_t, *parts, *more)


def token_kernel(slot_half, spots, grad_q, grad_k, grad_v, grad_one, own, other, keep, send, weight, sems):
    width = grad_one.shape[1]

    @pl.when(pl.program_id(0) == 0)
    def _():
        copies = piece_copies(own, other, spots, weight, sems)
        for copy in copies:
            copy.start()
        for copy in copies:
            copy.wait()

    total = grad_one[...]
    for part, grad in enumerate((grad_q, grad_k, grad_v)):
        total = total + dot(grad[...], weight[:, part * width : (part + 1) * width], NT)
    half = pl.program_id(0) * 2 // pl.num_programs(0)

    @pl.when(half == 0)
    def _():
        send[...] = total.astype(bf16)

    @pl.when(half == 1)
    def _():
        keep[...] = total


def token_gradient(slot_half, spots, grad_raw, grad_one, own, other, block=256):
    rows, width = grad_one.shape
    half = rows // 2
    halves = half // block

    def source(i, s):
        return (i + (1 - s[0]) * halves) % (2 * halves)

    return pl.pallas_call(
        token_kernel,
        grid_spec=pltpu.PrefetchScalarGridSpec(
            num_scalar_prefetch=2,
            grid=(2 * halves,),
            in_specs=[
                pl.BlockSpec((block, width), lambda i, s, *_: (source(i, s), 0)),
                pl.BlockSpec((block, width), lambda i, s, *_: (source(i, s), 0)),
                pl.BlockSpec((block, width), lambda i, s, *_: (source(i, s), 0)),
                pl.BlockSpec((block, width), lambda i, s, *_: (source(i, s), 0)),
                ANY,
                ANY,
            ],
            out_specs=[
                pl.BlockSpec((block, width), lambda i, *_: (jnp.maximum(i - halves, 0), 0)),
                pl.BlockSpec((block, width), lambda i, *_: (jnp.minimum(i, halves - 1), 0)),
            ],
            scratch_shapes=[
                pltpu.VMEM((width, 3 * width), bf16),
                pltpu.SemaphoreType.DMA((piece_count(own),)),
            ],
        ),
        out_shape=[
            jax.ShapeDtypeStruct((half, width), f32),
            jax.ShapeDtypeStruct((half, width), bf16),
        ],
        compiler_params=params(),
        cost_estimate=cost(6 * rows * width * width, 14 * rows * width + 6 * width * width),
        name="token_gradient",
    )(slot_half, spots, *grad_raw, grad_one, own, other)


class Transfers:
    def __init__(self, mesh):
        self.fsdp = mesh.shape["fsdp"]
        self.ctx = mesh.shape["ctx"]
        self.tp = mesh.shape["tp"]
        self.levels = self.fsdp // 2
        place = lax.axis_index("fsdp")
        self.z = place // 2
        self.core = place % 2
        self.x = lax.axis_index("ctx")
        self.y = lax.axis_index("tp")
        self.paired = self.ctx == 2 and self.tp == 2 and self.fsdp % 2 == 0

    def swap_slots(self, value):
        return lax.ppermute(value, "ctx", [(i, i ^ 1) for i in range(self.ctx)])

    def swap(self, value, axis):
        return lax.ppermute(value, axis, [(0, 1), (1, 0)])

    def swap_core(self, value):
        return lax.ppermute(value, "fsdp", [(i, i ^ 1) for i in range(self.fsdp)])

    def shift(self, value, step):
        pairs = [
            (2 * level + core, 2 * ((level + step) % self.levels) + core)
            for level in range(self.levels)
            for core in range(2)
        ]
        return lax.ppermute(value, "fsdp", pairs)

    def spots(self, rows, sign, width=None):
        found = []
        for side in range(2):
            for part in range(2):
                for step in range(self.levels):
                    level = (self.z + sign * step + self.levels) % self.levels
                    block = 2 * level + jnp.bitwise_xor(self.core, side)
                    found.append(2 * rows * block + rows * jnp.bitwise_xor(self.x, part))
        if width is None:
            found = found + [jnp.zeros((), jnp.int32)]
        else:
            found = found + [self.y * width, (1 - self.y) * width]
        return jnp.stack(found).astype(jnp.int32)

    def mine(self, shard):
        half = shard.shape[0] // 2
        return lax.dynamic_slice_in_dim(shard, self.x * half, half, 0)

    def shifts(self, block):
        return [self.shift(block, step) for step in range(1, self.levels)]

    def gather_feed(self, gate, up, out, norms):
        rows, width = gate.shape
        model = out.shape[1]
        share = rows // self.tp
        block = lax.dynamic_slice_in_dim(out, self.y * share, share, 0)
        tail = jnp.concatenate([block[16 * j : 16 * (j + 1)] for j in range(share // 16)], 1)
        norm_tail = jnp.pad(norms, ((0, 16 - norms.shape[0]), (0, 2 * width - tail.shape[1] - rows)))
        packed = jnp.concatenate(
            [jnp.concatenate([gate, up], 1), jnp.concatenate([tail, norm_tail], 1)], 0
        )
        packed = lax.all_gather(packed, ("fsdp", "tp"), axis=0)
        pieces = [[], [], [], []]
        for place in range(self.fsdp * self.tp):
            row, col = rows * (place // self.tp), width * (place % self.tp)
            for group in range(2):
                pieces[1 + group].append((0, place, 0, group * width, row, col, rows, width))
            for j in range(share // 16):
                row = rows * (place // self.tp) + share * (place % self.tp) + 16 * j
                pieces[0].append((0, place, rows, model * j, row, 0, 16, model))
        blocks = 2 * self.levels
        for side in range(2):
            for col in range(2):
                for row in range(blocks):
                    pieces[3].append(
                        (
                            1 + side,
                            col * blocks + row,
                            0,
                            0,
                            (side * blocks + row,),
                            (2 * blocks + col,),
                            rows // 2,
                            width,
                        )
                    )
        left = model * (share // 16)
        norms = packed[:: self.tp, rows : rows + norms.shape[0], left : left + rows]
        norms = norms.transpose(1, 0, 2).reshape(norms.shape[1], -1)
        return {"sources": 3, "pieces": pieces}, packed, norms

    def add(self, left, right):
        return (left.astype(f32) + right.astype(f32)).astype(bf16)

    def level_shifts(self, value):
        return [self.shift(value[step], step) for step in range(1, self.levels)]

    def sum_shifts(self, value, shifts):
        total = value.astype(f32)
        for other in shifts:
            total = total + other.astype(f32)
        return total.astype(bf16)

    def sum_shards(self, value):
        return lax.psum_scatter(value, "fsdp", scatter_dimension=0, tiled=True)

    def both(self, value, axis, index):
        other = self.swap(value, axis)
        return jnp.where(index == 0, value, other), jnp.where(index == 0, other, value)


def on_device(
    mesh,
    tokens,
    query_key_value_weight,
    output_weight,
    gate_weight,
    up_weight,
    down_weight,
    gain_one,
    shift_one,
    gain_two,
    shift_two,
    lengths,
    positions,
    cotangent,
):
    move = Transfers(mesh)
    shard, model_width = query_key_value_weight.shape[0], tokens.shape[2]
    feed_width = gate_weight.shape[1]
    slot = move.x % 2
    half_rows = tokens.shape[1]

    def sent(value):
        return jnp.where(slot == 0, value[1], value[0])

    def to_slot(value, other):
        keep = jnp.where(slot == 0, value[0], value[1])
        first = jnp.where(slot == 0, keep, other)
        second = jnp.where(slot == 0, other, keep)
        return jnp.concatenate([first, second], 0)

    def from_slot(keep, other):
        return jnp.where(slot == 0, jnp.stack([keep, other]), jnp.stack([other, keep]))

    other_places = move.swap_slots(sent(positions))
    other_tokens = move.swap_slots(sent(tokens))
    other_cotangent = move.swap_slots(sent(cotangent))
    length = jnp.where(slot == 0, lengths[0:1], lengths[1:2])
    slot_half = slot[None].astype(jnp.int32)
    norms = jnp.stack([gain_one, shift_one, gain_two, shift_two])
    feed_total = feed_width * move.tp
    down_turned = down_weight.T
    half = shard // 2
    if move.paired:
        levels = move.levels
        blocks = (2, 2 * levels, half)
        attn_in = move.spots(half, -1)
        feed_in = move.spots(half, -1, feed_width)
        feed_out = move.spots(half, 1, feed_width)
        plan, packed, norms = move.gather_feed(gate_weight, up_weight, output_weight, norms)
        qkv = move.mine(query_key_value_weight)
        other_tokens, other_cotangent, down, qkv, *parts = fence(
            other_tokens, other_cotangent, move.mine(down_turned), qkv, *move.shifts(qkv)
        )
        qkv = jnp.stack([qkv] + parts)
        qkv_x = move.swap(qkv, "ctx")
        qkv, qkv_x, down, *parts = fence(qkv, qkv_x, down, *move.shifts(down))
        qkv = jnp.stack([qkv, qkv_x]).reshape(1, 2 * levels, half, -1)
        qkv_w = qkv, move.swap_core(qkv)
        down = jnp.stack([down] + parts)
        down_y = move.swap(down, "tp")
    else:
        middle = model_width // 2
        attn_in = jnp.asarray([0, middle, 0], jnp.int32)
        feed_in = attn_in

        def whole(value, axes):
            value = lax.all_gather(value, "fsdp", axis=0, tiled=True)
            if axes:
                value = lax.all_gather(value, "tp", axis=1, tiled=True)
            return value[None]

        sources = [
            whole(output_weight, False),
            whole(gate_weight, True),
            whole(up_weight, True),
            whole(down_turned, True),
        ]
        plan = {
            "sources": 4,
            "pieces": [
                [(place, 0, 0, 0, 0, 0) + source.shape[1:]] for place, source in enumerate(sources)
            ],
        }
        qkv_all = whole(query_key_value_weight, False)
        qkv_w = qkv_all[None, :, :middle], qkv_all[None, :, middle:]
        norms = lax.all_gather(norms, "fsdp", axis=1, tiled=True)
    norms = jnp.pad(norms.astype(f32), ((0, 4), (0, 0)))

    slot_tokens = to_slot(tokens, other_tokens)
    cosine, sine = turn_tables(to_slot(positions, other_places))
    queries, key_rows, values = project(attn_in, slot_tokens, cosine, sine, *qkv_w)
    if move.paired:
        queries, down, down_y = fence(queries, down, down_y)
        down = jnp.stack([down, down_y])
        down_x = move.swap(down, "ctx")
    mates = move.ctx // 2
    if mates > 1:
        groups = [[2 * j + s for j in range(mates)] for s in range(2)]

        def gather_rows(value):
            return lax.all_gather(value, "ctx", axis=0, tiled=True, axis_index_groups=groups)

        key_rows = gather_rows(key_rows)
        values = gather_rows(values)
        key_cos, key_sin = jnp.ones((key_rows.shape[0], PAIR), f32), jnp.zeros(
            (key_rows.shape[0], PAIR), f32
        )
    else:
        key_cos, key_sin = cosine, sine
    context, summit = attend(length, queries, key_rows, values)
    if move.paired:
        context, down, down_x = fence(context, down, down_x)
        down = jnp.stack([down, down_x], 1).reshape(4 * levels, half, feed_width)
        down = down.reshape((2 * 2 * levels, half, feed_width))
        sources = [packed, down, move.swap_core(down)]
    slot_cotangent = to_slot(cotangent, other_cotangent)
    (
        mixed,
        hidden,
        grad_gate,
        grad_upper,
        feed_t,
        branch_t,
        context_t,
        tokens_t,
        grad_mix_one,
        grad_attn,
        grad_context,
        vectors,
    ) = feed_forward(
        plan, sources, slot_half, feed_in, slot_tokens, context, slot_cotangent, norms, feed_total
    )

    def back(grads, first, pairs, before):
        return attend_back(
            length,
            queries,
            key_rows,
            values,
            context,
            summit,
            grads,
            cosine,
            sine,
            key_cos,
            key_sin,
            first,
            pairs,
            before,
        )

    pairs = model_width // PAIR
    if move.paired:
        def outer_feed(left_t, right, parts=1, part=0):
            return outer(feed_out, left_t, right, 2, 2 * levels, parts=parts, part=part)

        def grouped(value):
            return value.reshape((2, 2, levels) + value.shape[2:])

        third = pairs // 3
        down, down_core = outer_feed(branch_t, hidden)
        down, down_core, grad_gate, send_mixed = fence(down, down_core, grad_gate, mixed[1])
        down_core = move.swap_core(down_core)
        other_mixed = move.swap_slots(send_mixed)
        gate, gate_core = outer_feed(feed_t, grad_gate)

        gate, gate_core, down, down_core, grad_context, grad_upper = fence(
            gate, gate_core, down, down_core, grad_context, grad_upper
        )
        down = grouped(move.add(down, down_core))
        down_x = move.swap(down[:, 1], "ctx")
        gate_core = move.swap_core(gate_core)
        grad_raw = back(grad_context, 0, third, ())

        *grad_raw, gate, gate_core, grad_context, grad_upper, vectors = fence(
            *grad_raw, gate, gate_core, grad_context, grad_upper, vectors
        )
        gate = grouped(move.add(gate, gate_core))
        gate_y = move.swap(gate[1], "tp")
        attn_a = outer_rows(tokens_t, grad_raw, 0, third, (context_t, grad_attn, vectors))
        attn_a = move.sum_shards(attn_a)
        up_a, up_a_core = outer_feed(feed_t, grad_upper, 2, 0)
        up_b, up_b_core = outer_feed(feed_t, grad_upper, 2, 1)

        *grad_raw, up_a, up_a_core, up_b, up_b_core, down, down_x, grad_context = fence(
            *grad_raw, up_a, up_a_core, up_b, up_b_core, down[:, 0], down_x, grad_context
        )
        down = move.add(down, down_x)
        down_y = move.swap(down[1], "tp")
        up_a_core = move.swap_core(up_a_core)
        up_b_core = move.swap_core(up_b_core)
        grad_raw = back(grad_context, third, third, grad_raw)

        *grad_raw, up_a, up_a_core, up_b, up_b_core, gate, gate_y, grad_context = fence(
            *grad_raw, up_a, up_a_core, up_b, up_b_core, gate[0], gate_y, grad_context
        )
        gate = move.add(gate, gate_y)
        up_a = grouped(move.add(up_a, up_a_core))
        up_b = grouped(move.add(up_b, up_b_core))
        gate_x = move.swap(gate[1], "ctx")
        up_a_x = move.swap(up_a[:, 1], "ctx")
        up_b_y = move.swap(up_b[1], "tp")
        grad_raw = back(grad_context, 2 * third, pairs - 2 * third, grad_raw)

        *grad_raw, down, down_y, gate, gate_x = fence(
            *grad_raw, down[0], down_y, gate[0], gate_x
        )
        attn_b = outer_rows(tokens_t, grad_raw, third, 2 * third, ())
        attn_b = move.sum_shards(attn_b)
        feed_a = jnp.concatenate([move.add(down, down_y), move.add(gate, gate_x)], 2)
        shifts_a = move.level_shifts(feed_a)
        keep_rows, send_rows = token_gradient(
            slot_half, attn_in, grad_raw, grad_mix_one, *qkv_w
        )

        keep_rows, send_rows, up_a, up_a_x, up_b, up_b_y, attn_a = fence(
            keep_rows, send_rows, up_a[:, 0], up_a_x, up_b[0], up_b_y, attn_a
        )
        up_a = move.add(up_a, up_a_x)
        up_b = move.add(up_b, up_b_y)
        up_a_y = move.swap(up_a[1], "tp")
        up_b_x = move.swap(up_b[1], "ctx")
        attn_a_x = move.swap(attn_a, "ctx")

        send_rows, up_a, up_a_y, up_b, up_b_x, attn_a, attn_a_x, feed_a, *shifts_a = fence(
            send_rows, up_a[0], up_a_y, up_b[0], up_b_x, attn_a, attn_a_x, feed_a[0], *shifts_a
        )
        up = jnp.concatenate([move.add(up_a, up_a_y), move.add(up_b, up_b_x)], 2)
        shifts_up = move.level_shifts(up)
        other_rows = move.swap_slots(send_rows)
        attn_a = move.add(attn_a, attn_a_x)
        attn_a_y = move.swap(attn_a, "tp")
        feed_a = move.sum_shifts(feed_a, shifts_a)

        other_rows, feed_a, up, attn_a, attn_a_y, attn_b, *shifts_up = fence(
            other_rows, feed_a, up[0], attn_a, attn_a_y, attn_b, *shifts_up
        )
        attn_a = move.add(attn_a, attn_a_y)
        attn_b_x = move.swap(attn_b, "ctx")
        feed = jnp.concatenate([feed_a, move.sum_shifts(up, shifts_up)], 1)
        low, high = move.both(feed, "ctx", move.x)
        feed = jnp.concatenate([low, high], 0).astype(f32)
        mixed_out = from_slot(mixed[0], other_mixed)
        attn_b = move.add(attn_b, attn_b_x)
        attn_b = move.add(attn_b, move.swap(attn_b, "tp"))
        down_gradient = feed[:, :feed_width].T
        gate_gradient = feed[:, feed_width : 2 * feed_width]
        up_gradient = feed[:, 2 * feed_width :]
        columns = third * PAIR
        qkv_gradient = jnp.concatenate(
            [
                value[:, part * size : (part + 1) * size]
                for part in range(3)
                for value, size in ((attn_a, columns), (attn_b, 2 * columns))
            ],
            1,
        ).astype(f32)
        out_gradient = attn_a[:, 3 * columns : 3 * columns + model_width].astype(f32)
        left = 3 * columns + model_width
        vector_grads = [attn_a[:, left + place].astype(f32) for place in range(4)]
        grad_tokens = from_slot(keep_rows, other_rows.astype(f32))
    else:
        grad_raw = back(grad_context, 0, pairs, ())
        mixed_out = from_slot(mixed[0], move.swap_slots(mixed[1]))
        if mates > 1:
            rows = slot_tokens.shape[0]
            keys_part = lax.psum_scatter(
                jnp.stack(grad_raw[1:]).astype(f32),
                "ctx",
                scatter_dimension=1,
                axis_index_groups=groups,
                tiled=True,
            )
            turned_keys = keys_part[0].reshape(rows, HEADS, 2, HEAD_DIM // 2)
            cos_half = cosine[:, None, : HEAD_DIM // 2]
            sin_half = sine[:, None, HEAD_DIM // 2 : HEAD_DIM]
            ahead, behind = turned_keys[:, :, 0], turned_keys[:, :, 1]
            turned_keys = jnp.stack(
                [ahead * cos_half + behind * sin_half, behind * cos_half - ahead * sin_half], 2
            ).reshape(rows, model_width)
            grad_raw = (grad_raw[0], turned_keys.astype(bf16), keys_part[1].astype(bf16))
        keep_rows, send_rows = token_gradient(
            slot_half, attn_in, grad_raw, grad_mix_one, *qkv_w
        )
        grad_tokens = from_slot(keep_rows, move.swap_slots(send_rows).astype(f32))

        def scatter(left_t, right, axes, split):
            pieces = outer(attn_in, left_t, right, 1, 1)
            value = jnp.concatenate([piece[0, 0] for piece in pieces], 0)
            value = lax.psum(value, axes)
            value = lax.psum_scatter(value, "fsdp", scatter_dimension=0, tiled=True)
            if split:
                start = move.y * feed_width
                value = lax.dynamic_slice_in_dim(value, start, feed_width, 1)
            return value.astype(f32)

        every = ("ctx", "tp")
        down_gradient = scatter(branch_t, hidden, every, True).T
        gate_gradient = scatter(feed_t, grad_gate, every, True)
        up_gradient = scatter(feed_t, grad_upper, every, True)
        out_gradient = scatter(context_t, grad_attn, every, False)
        qkv_gradient = jnp.concatenate(
            [scatter(tokens_t, part, every, False) for part in grad_raw], 1
        )
        summed = lax.psum(vectors, every)
        summed = lax.psum_scatter(summed, "fsdp", scatter_dimension=1, tiled=True)
        vector_grads = [summed[place] for place in range(4)]
    return (
        mixed_out,
        grad_tokens,
        qkv_gradient,
        out_gradient,
        gate_gradient,
        up_gradient,
        down_gradient,
        *vector_grads,
    )


def solution(mesh):
    in_specs = (
        P(("fsdp", "tp"), "ctx", None),
        P("fsdp", None),
        P("fsdp", None),
        P("fsdp", "tp"),
        P("fsdp", "tp"),
        P("tp", "fsdp"),
        P("fsdp"),
        P("fsdp"),
        P("fsdp"),
        P("fsdp"),
        P(("fsdp", "tp")),
        P(("fsdp", "tp"), "ctx"),
        P(("fsdp", "tp"), "ctx", None),
    )
    out_specs = (
        P(("fsdp", "tp"), "ctx", None),
        P(("fsdp", "tp"), "ctx", None),
        P("fsdp", None),
        P("fsdp", None),
        P("fsdp", "tp"),
        P("fsdp", "tp"),
        P("tp", "fsdp"),
        P("fsdp"),
        P("fsdp"),
        P("fsdp"),
        P("fsdp"),
    )
    return jax.shard_map(
        functools.partial(on_device, mesh),
        mesh=mesh,
        in_specs=in_specs,
        out_specs=out_specs,
        check_vma=False,
    )
```

```python
import functools

import jax
import jax.numpy as jnp
from jax import lax
from jax.experimental import pallas as pl
from jax.experimental.pallas import tpu as pltpu
from jax.sharding import PartitionSpec as P

HEADS = 12
HEAD_DIM = 64
PAIR = 2 * HEAD_DIM

norm_eps = 1e-05
rope_base = 1000.0
masked_bias = -1000000000.0

bf16 = jnp.bfloat16
f32 = jnp.float32
NN = (((1,), (0,)), ((), ()))
NT = (((1,), (1,)), ((), ()))
VMEM_LIMIT = 60 * 2**20
ANY = pl.BlockSpec(memory_space=pl.ANY)


def dot(left, right, dims=NN):
    return lax.dot_general(left, right, dims, preferred_element_type=f32)


def params():
    return pltpu.CompilerParams(vmem_limit_bytes=VMEM_LIMIT)


def cost(flops, moved, exps=0):
    return pl.CostEstimate(flops=int(flops), bytes_accessed=int(moved), transcendentals=int(exps))


def fence(*values, waits=()):
    def nothing(*refs):
        pass

    return pl.pallas_call(
        nothing,
        in_specs=[ANY] * (len(values) + len(waits)),
        out_specs=[ANY] * len(values),
        out_shape=[jax.ShapeDtypeStruct(value.shape, value.dtype) for value in values],
        input_output_aliases={place: place for place in range(len(values))},
        compiler_params=params(),
        name="fence",
    )(*values, *waits)


def piece_copies(own, other, spots, full, sems):
    col_blocks, row_blocks, rows, width = own.shape
    copies = []
    for side, source in enumerate((own, other)):
        for row in range(row_blocks):
            for col in range(col_blocks):
                start = pl.multiple_of(spots[side * row_blocks + row], 16)
                left = pl.multiple_of(spots[2 * row_blocks + col], 128)
                copies.append(
                    pltpu.make_async_copy(
                        source.at[col, row],
                        full.at[pl.ds(start, rows), pl.ds(left, width)],
                        sems.at[(side * row_blocks + row) * col_blocks + col],
                    )
                )
    return copies


def piece_count(own):
    return 2 * own.shape[0] * own.shape[1]


def turned(block, cosine, sine):
    lane = lax.broadcasted_iota(jnp.int32, block.shape, 1)
    first = (lane % HEAD_DIM) < HEAD_DIM // 2
    partner = jnp.where(
        first, pltpu.roll(block, PAIR - HEAD_DIM // 2, 1), pltpu.roll(block, HEAD_DIM // 2, 1)
    )
    return block * cosine + partner * sine


def turn_tables(places):
    half_dim = HEAD_DIM // 2
    frequency = rope_base ** (-jnp.arange(half_dim, dtype=f32) * 2.0 / HEAD_DIM)
    angles = places.astype(f32)[:, None] * frequency
    cosine = jnp.cos(angles)
    sine = jnp.sin(angles)
    return jnp.concatenate([cosine] * 4, 1), jnp.concatenate([-sine, sine, -sine, sine], 1)


def project_kernel(
    spots, tokens, cosine, sine, own, other, q_out, k_out, v_out, tokens_t, weight, sems
):
    width = q_out.shape[1]

    @pl.when(pl.program_id(0) == 0)
    def _():
        copies = piece_copies(own, other, spots, weight, sems)
        for copy in copies:
            copy.start()
        for copy in copies:
            copy.wait()

    rows = tokens[...]
    tokens_t[...] = rows.T
    cos_part = cosine[...]
    sin_part = sine[...]
    for part, out in enumerate((q_out, k_out, v_out)):
        raw = dot(rows, weight[:, part * width : (part + 1) * width])
        for pair in range(width // PAIR):
            cols = slice(pair * PAIR, (pair + 1) * PAIR)
            block = raw[:, cols]
            if part < 2:
                block = turned(block, cos_part, sin_part)
            block = block.astype(bf16)
            if part == 0:
                block = block * jnp.asarray(HEAD_DIM**-0.5, bf16)
            out[:, cols] = block


def project(spots, tokens, cosine, sine, own, other, block=256):
    rows, width = tokens.shape
    total = own.shape[0] * own.shape[3]
    row_spec = pl.BlockSpec((block, width), lambda i, *_: (i, 0))
    table = pl.BlockSpec((block, PAIR), lambda i, *_: (i, 0))
    part = total // 3
    out_spec = pl.BlockSpec((block, part), lambda i, *_: (i, 0))
    return pl.pallas_call(
        project_kernel,
        grid_spec=pltpu.PrefetchScalarGridSpec(
            num_scalar_prefetch=1,
            grid=(rows // block,),
            in_specs=[row_spec, table, table, ANY, ANY],
            out_specs=[out_spec] * 3 + [pl.BlockSpec((width, block), lambda i, *_: (0, i))],
            scratch_shapes=[
                pltpu.VMEM((width, total), bf16),
                pltpu.SemaphoreType.DMA((piece_count(own),)),
            ],
        ),
        out_shape=[jax.ShapeDtypeStruct((rows, part), bf16)] * 3
        + [jax.ShapeDtypeStruct((width, rows), bf16)],
        compiler_params=params(),
        cost_estimate=cost(2 * rows * width * total, 4 * rows * total + 2 * width * total),
        name="project",
    )(spots, tokens, cosine, sine, own, other)


def lane_ids(shape):
    return lax.broadcasted_iota(jnp.int32, shape, 1)


def key_bias(length, shape):
    return jnp.where(lax.broadcasted_iota(jnp.int32, shape, 0) < length, 0.0, masked_bias).astype(
        bf16
    )


def attend_kernel(length, q_ref, k_ref, v_ref, out_ref, summit_ref):
    lane_q = lane_ids(q_ref.shape)
    lane_k = lane_ids(k_ref.shape)
    bias = key_bias(length[0], k_ref.shape)
    queries = q_ref[...]
    keys = k_ref[...]
    values = v_ref[...]
    one = jnp.ones((), bf16)
    zero = jnp.zeros((), bf16)
    outs = []
    summits = []
    for head in range(2):
        mine_q = (lane_q < HEAD_DIM) if head == 0 else (lane_q >= HEAD_DIM)
        mine_k = (lane_k < HEAD_DIM) if head == 0 else (lane_k >= HEAD_DIM)
        spare = HEAD_DIM * (1 - head)
        query = jnp.where(mine_q, queries, jnp.where(lane_q == spare, one, zero))
        key = jnp.where(mine_k, keys, bias)
        value = jnp.where(mine_k, values, one)
        scores = dot(query, key, NT)
        top = jnp.max(scores, axis=1, keepdims=True)
        summed = dot(jnp.exp(scores - top).astype(bf16), value)
        totals = pltpu.roll(summed, HEAD_DIM, 1)
        outs.append(summed / totals)
        summits.append(top + jnp.log(summed))
    low = lane_q < HEAD_DIM
    out_ref[...] = jnp.where(low, outs[0], outs[1]).astype(bf16)
    summit_ref[0] = jnp.where(low, summits[1], summits[0])


def attend(length, queries, keys, values):
    rows, width = queries.shape
    seq = keys.shape[0]
    pairs = width // PAIR
    q_spec = pl.BlockSpec((rows, PAIR), lambda h, *_: (0, h))
    k_spec = pl.BlockSpec((seq, PAIR), lambda h, *_: (0, h))
    return pl.pallas_call(
        attend_kernel,
        grid_spec=pltpu.PrefetchScalarGridSpec(
            num_scalar_prefetch=1,
            grid=(pairs,),
            in_specs=[q_spec, k_spec, k_spec],
            out_specs=[q_spec, pl.BlockSpec((1, rows, PAIR), lambda h, *_: (h, 0, 0))],
        ),
        out_shape=[
            jax.ShapeDtypeStruct((rows, width), bf16),
            jax.ShapeDtypeStruct((pairs, rows, PAIR), f32),
        ],
        compiler_params=params(),
        cost_estimate=cost(16 * rows * seq * width, 12 * rows * width),
        name="attend",
    )(length, queries, keys, values)


def three_parts(value):
    high = value.astype(bf16)
    rest = value - high.astype(f32)
    middle = rest.astype(bf16)
    return high, middle, (rest - middle.astype(f32)).astype(bf16)


def pair_back(length, q_ref, k_ref, v_ref, out_ref, summit_ref, grad_ref):
    rows = q_ref.shape[0]
    lane_q = lane_ids(q_ref.shape)
    lane_k = lane_ids(k_ref.shape)
    bias = key_bias(length[0], k_ref.shape)
    queries = q_ref[...]
    keys = k_ref[...]
    values = v_ref[...]
    grads = grad_ref[...]
    summit = three_parts(summit_ref[0])
    product = grads.astype(f32) * out_ref[...].astype(f32)
    one = jnp.ones((), bf16)
    zero = jnp.zeros((), bf16)
    grads_t = grads.T
    queries_t = queries.T
    dq, dk, dv = [], [], []
    for head in range(2):
        mine_q = (lane_q < HEAD_DIM) if head == 0 else (lane_q >= HEAD_DIM)
        mine_k = (lane_k < HEAD_DIM) if head == 0 else (lane_k >= HEAD_DIM)
        spare = HEAD_DIM * (1 - head)
        own = slice(HEAD_DIM * head, HEAD_DIM * (head + 1))
        row_dot = jnp.sum(jnp.where(mine_q, product, 0.0), axis=1, keepdims=True)
        row_dot = three_parts(jnp.broadcast_to(row_dot, (rows, PAIR)))

        def beside(main, mine, lane, parts, last):
            extra = jnp.where(lane == spare + 3, last, zero)
            for place in range(3):
                extra = jnp.where(lane == spare + place, parts[place], extra)
            return jnp.where(mine, main, extra)

        minus = (-one, -one, -one)
        query = beside(queries, mine_q, lane_q, summit, one)
        key = beside(keys, mine_k, lane_k, minus, bias)
        grad = beside(grads, mine_q, lane_q, row_dot, zero)
        value = beside(values, mine_k, lane_k, minus, zero)
        probs = jnp.exp(dot(query, key, NT))
        grad_scores = (probs * dot(grad, value, NT)).astype(bf16)
        dv.append(dot(grads_t[own], probs.astype(bf16)))
        dk.append(dot(queries_t[own], grad_scores))
        dq.append(dot(grad_scores, keys))
    grad_query = jnp.where(lane_q < HEAD_DIM, dq[0], dq[1]) * HEAD_DIM**-0.5
    return grad_query, jnp.concatenate(dk, 0).T, jnp.concatenate(dv, 0).T


def attend_back_kernel(
    waits,
    length,
    first,
    q_ref,
    k_ref,
    v_ref,
    out_ref,
    summit_ref,
    grad_ref,
    cos_ref,
    sin_ref,
    tokens_t,
    *refs,
):
    outer_ref, raw_ref = refs[waits:]
    grad_query, grad_keys, grad_values = pair_back(
        length, q_ref, k_ref, v_ref, out_ref, summit_ref, grad_ref
    )
    cosine = cos_ref[...]
    sine = sin_ref[...]
    raw = jnp.concatenate(
        [
            turned(grad_query, cosine, -sine).astype(bf16),
            turned(grad_keys, cosine, -sine).astype(bf16),
            grad_values.astype(bf16),
        ],
        1,
    )
    outer_ref[...] = dot(tokens_t[...], raw).astype(bf16)
    raw_ref[...] = raw


def attend_back(
    length,
    queries,
    keys,
    values,
    out,
    summit,
    grads,
    cosine,
    sine,
    tokens_t,
    first,
    pairs,
    waits=(),
):
    rows, width = queries.shape
    q_spec = pl.BlockSpec((rows, PAIR), lambda h, length, first: (0, h + first[0]))
    table = pl.BlockSpec((rows, PAIR), lambda h, *_: (0, 0))
    columns = 3 * PAIR
    return pl.pallas_call(
        functools.partial(attend_back_kernel, len(waits)),
        grid_spec=pltpu.PrefetchScalarGridSpec(
            num_scalar_prefetch=2,
            grid=(pairs,),
            in_specs=[
                q_spec,
                q_spec,
                q_spec,
                q_spec,
                pl.BlockSpec((1, rows, PAIR), lambda h, length, first: (h + first[0], 0, 0)),
                q_spec,
                table,
                table,
                pl.BlockSpec(tokens_t.shape, lambda h, *_: (0, 0)),
            ]
            + [ANY] * len(waits),
            out_specs=[
                pl.BlockSpec((width, columns), lambda h, *_: (0, h)),
                pl.BlockSpec((rows, columns), lambda h, *_: (0, h)),
            ],
        ),
        out_shape=[
            jax.ShapeDtypeStruct((width, columns * pairs), bf16),
            jax.ShapeDtypeStruct((rows, columns * pairs), bf16),
        ],
        compiler_params=params(),
        cost_estimate=cost(46 * rows * rows * PAIR * pairs, 16 * rows * PAIR * pairs),
        name="attend_back",
    )(
        length,
        jnp.full((1,), first, jnp.int32),
        queries,
        keys,
        values,
        out,
        summit,
        grads,
        cosine,
        sine,
        tokens_t,
        *waits,
    )


def token_kernel(count, slot_half, spots, *refs):
    raws = refs[:count]
    total_ref, own, other = refs[count : count + 3]
    keep, send, weight, sems = refs[-4:]
    width = total_ref.shape[1]
    step = pl.program_id(0)

    @pl.when(step == 0)
    def _():
        copies = piece_copies(own, other, spots, weight, sems)
        for copy in copies:
            copy.start()
        for copy in copies:
            copy.wait()

    order = [part * width + pair * PAIR for pair in range(width // PAIR) for part in range(3)]
    used = jnp.concatenate([weight[:, left : left + PAIR] for left in order], 1)
    total = total_ref[...]
    left = 0
    for raw in raws:
        size = raw.shape[1]
        total = total + dot(raw[...], used[:, left : left + size], NT)
        left += size

    @pl.when(step < pl.num_programs(0) // 2)
    def _():
        send[...] = total.astype(bf16)

    @pl.when(step >= pl.num_programs(0) // 2)
    def _():
        keep[...] = total


def token_gradient(slot_half, spots, raws, total, own, other, waits=(), block=256):
    rows, width = total.shape
    halves = rows // 2 // block

    def source(i, s):
        return (i + (1 - s[0]) * halves) % (2 * halves)

    def rows_of(value):
        return pl.BlockSpec((block, value.shape[1]), lambda i, s, *_: (source(i, s), 0))

    return pl.pallas_call(
        functools.partial(token_kernel, len(raws)),
        grid_spec=pltpu.PrefetchScalarGridSpec(
            num_scalar_prefetch=2,
            grid=(2 * halves,),
            in_specs=[rows_of(raw) for raw in raws]
            + [rows_of(total), ANY, ANY]
            + [ANY] * len(waits),
            out_specs=[
                pl.BlockSpec((block, width), lambda i, *_: (jnp.maximum(i - halves, 0), 0)),
                pl.BlockSpec((block, width), lambda i, *_: (jnp.minimum(i, halves - 1), 0)),
            ],
            scratch_shapes=[
                pltpu.VMEM((width, 3 * width), bf16),
                pltpu.SemaphoreType.DMA((piece_count(own),)),
            ],
        ),
        out_shape=[
            jax.ShapeDtypeStruct((rows // 2, width), f32),
            jax.ShapeDtypeStruct((rows // 2, width), bf16),
        ],
        compiler_params=params(),
        cost_estimate=cost(6 * rows * width * width, 14 * rows * width + 6 * width * width),
        name="token_gradient",
    )(slot_half, spots, *raws, total, own, other, *waits)


def attend_back_plain_kernel(
    length, q_ref, k_ref, v_ref, out_ref, summit_ref, grad_ref, dq_ref, dk_ref, dv_ref
):
    dq_ref[...], dk_ref[...], dv_ref[...] = pair_back(
        length, q_ref, k_ref, v_ref, out_ref, summit_ref, grad_ref
    )


def attend_back_plain(length, queries, keys, values, out, summit, grads):
    rows, width = queries.shape
    seq = keys.shape[0]
    q_spec = pl.BlockSpec((rows, PAIR), lambda h, *_: (0, h))
    k_spec = pl.BlockSpec((seq, PAIR), lambda h, *_: (0, h))
    return pl.pallas_call(
        attend_back_plain_kernel,
        grid_spec=pltpu.PrefetchScalarGridSpec(
            num_scalar_prefetch=1,
            grid=(width // PAIR,),
            in_specs=[
                q_spec,
                k_spec,
                k_spec,
                q_spec,
                pl.BlockSpec((1, rows, PAIR), lambda h, *_: (h, 0, 0)),
                q_spec,
            ],
            out_specs=[q_spec, k_spec, k_spec],
        ),
        out_shape=[jax.ShapeDtypeStruct((count, width), f32) for count in (rows, seq, seq)],
        compiler_params=params(),
        cost_estimate=cost(40 * rows * seq * width, 16 * rows * width),
        name="attend_back_plain",
    )(length, queries, keys, values, out, summit, grads)


def row_mean(value):
    return jnp.mean(value, axis=-1, keepdims=True)


def normalize(value):
    centered = value - row_mean(value)
    inverse = lax.rsqrt(row_mean(centered * centered) + norm_eps)
    return centered * inverse, inverse


def normalize_back(normed, inverse, gain, upstream):
    scaled = upstream * gain
    return inverse * (scaled - row_mean(scaled) - normed * row_mean(scaled * normed))


def weight_copies(plan, group, sources, weight, spots, sems, chunk):
    copies = [[] for _ in range(weight.shape[1] // chunk)]
    count = 0
    for source, first, top, left, row, col, rows, cols in plan["pieces"][group]:
        dynamic = isinstance(row, tuple)
        if dynamic:
            row = pl.multiple_of(spots[row[0]], 16)
            col = pl.multiple_of(spots[col[0]], 128)
        width = cols if dynamic else min(cols, chunk)
        for inside in range(0, cols, width):
            copy = pltpu.make_async_copy(
                sources[source].at[first, pl.ds(top, rows), pl.ds(left + inside, width)],
                weight.at[pl.ds(row, rows), pl.ds(col + inside, width)],
                sems.at[group, count],
            )
            copies[0 if dynamic else (col + inside) // chunk].append(copy)
            count += 1
    return copies


def weight_copy_count(plan):
    counts = []
    for pieces in plan["pieces"]:
        counts.append(
            sum(
                1 if isinstance(row, tuple) else -(-cols // plan["chunk"])
                for _, _, _, _, row, _, _, cols in pieces
            )
        )
    return max(counts)


def feed_kernel(plan, slot_half, spots_in, spots_out, tokens, context, cotangent, norms, *refs):
    sources = refs[: plan["sources"]]
    (
        mixed_keep,
        mixed_send,
        grad_mix_one,
        grad_context,
        out_ref,
        keep,
        send,
        w_out,
        w_gate,
        w_up,
        w_down,
        slopes,
        known,
        lefts,
        context_t,
        attn_rows,
        vectors,
        stage,
        sems,
        out_sems,
    ) = refs[plan["sources"] :]
    chunk = plan["chunk"]
    rows, width = tokens.shape
    steps = known.shape[1] // rows
    step = pl.program_id(0)
    feed_total = w_gate.shape[1]
    chunks = feed_total // chunk
    weights = (w_out, w_gate, w_up, w_down)
    loads = [
        weight_copies(plan, group, sources, weight, spots_in, sems, min(chunk, weight.shape[1]))
        for group, weight in enumerate(weights)
    ]

    @pl.when(step == 0)
    def _():
        order = [loads[0][0]]
        for place in range(chunks):
            order += [loads[1][place], loads[2][place], loads[3][place]]
        for group in order:
            for copy in group:
                copy.start()
        vectors[...] = jnp.zeros_like(vectors)

    def arrive(*groups):
        @pl.when(step == 0)
        def _():
            for group in groups:
                for copy in group:
                    copy.wait()

    @pl.when(step < steps)
    def _():
        here = pl.ds(pl.multiple_of(step * rows, rows), rows)
        gain_one = norms[0:1, :]
        shift_one = norms[1:2, :]
        gain_two = norms[2:3, :]
        shift_two = norms[3:4, :]
        arrive(loads[0][0])
        context_rows = context[...]
        context_t[:, here] = context_rows.T
        normed_one, inverse_one = normalize(
            tokens[...].astype(f32) + dot(context_rows, w_out[...])
        )
        out_one = normed_one * gain_one + shift_one
        feed_in = out_one.astype(bf16)
        lefts[1, :, here] = feed_in.T
        total = out_one
        for place in range(chunks):
            cols = slice(place * chunk, (place + 1) * chunk)
            arrive(loads[1][place], loads[2][place], loads[3][place])
            gate = dot(feed_in, w_gate[:, cols])
            up = dot(feed_in, w_up[:, cols])
            sig = jax.nn.sigmoid(gate)
            swish = gate * sig
            hid = (swish * up).astype(bf16)
            known[0, here, cols] = hid
            slopes[0, :, cols] = swish.astype(bf16)
            slopes[1, :, cols] = (up * (sig + swish * (1.0 - sig))).astype(bf16)
            total = total + dot(hid, w_down[:, cols], NT)
        normed_two, inverse_two = normalize(total)
        mixed = (normed_two * gain_two + shift_two).astype(bf16)

        @pl.when(step < steps // 2)
        def _():
            mixed_send[...] = mixed

        @pl.when(step >= steps // 2)
        def _():
            mixed_keep[...] = mixed

        upstream = cotangent[...].astype(f32)
        grad_mix_two = normalize_back(normed_two, inverse_two, gain_two, upstream)
        branch = grad_mix_two.astype(bf16)
        lefts[0, :, here] = branch.T
        grad_out_one = grad_mix_two
        for place in range(chunks):
            cols = slice(place * chunk, (place + 1) * chunk)
            grad_hidden = dot(branch, w_down[:, cols])
            grad_gate = (grad_hidden * slopes[1, :, cols].astype(f32)).astype(bf16)
            grad_up = (grad_hidden * slopes[0, :, cols].astype(f32)).astype(bf16)
            known[1, here, cols] = grad_gate
            known[2, here, cols] = grad_up
            grad_out_one = (
                grad_out_one
                + dot(grad_gate, w_gate[:, cols], NT)
                + dot(grad_up, w_up[:, cols], NT)
            )
        vectors[0:1, :] += jnp.sum(grad_out_one * normed_one, axis=0, keepdims=True)
        vectors[1:2, :] += jnp.sum(grad_out_one, axis=0, keepdims=True)
        vectors[2:3, :] += jnp.sum(upstream * normed_two, axis=0, keepdims=True)
        vectors[3:4, :] += jnp.sum(upstream, axis=0, keepdims=True)
        grad_one = normalize_back(normed_one, inverse_one, gain_one, grad_out_one)
        grad_mix_one[...] = grad_one
        grad_rows = grad_one.astype(bf16)
        attn_rows[here, :] = grad_rows
        grad_context[...] = dot(grad_rows, w_out[...], NT).astype(bf16)

    _, col_blocks, row_blocks, piece_rows, _ = keep.shape
    per = chunks // col_blocks

    def piece_moves(place):
        job, inside = place // chunks, place % chunks
        col, left = inside // per, inside % per * chunk
        slot = place % 2
        moves = []
        for side, out in enumerate((keep, send)):
            for row in range(row_blocks):
                start = pl.multiple_of(spots_out[side * row_blocks + row], 16)
                moves.append(
                    pltpu.make_async_copy(
                        stage.at[slot, pl.ds(start, piece_rows), :],
                        out.at[job, col, row, :, pl.ds(pl.multiple_of(left, 128), chunk)],
                        out_sems.at[slot, side * row_blocks + row],
                    )
                )
        return moves

    @pl.when(step >= steps)
    def _():
        place = step - steps

        @pl.when(place >= 2)
        def _():
            for move in piece_moves(place - 2):
                move.wait()

        job, inside = place // chunks, place % chunks
        start = spots_out[2 * row_blocks + inside // per] + inside % per * chunk
        cols = pl.ds(pl.multiple_of(start, 128), chunk)
        left_t = lefts[jnp.minimum(job, 1)]
        stage[place % 2] = dot(left_t, known[job, :, cols]).astype(bf16)
        for move in piece_moves(place):
            move.start()

    @pl.when(step == pl.num_programs(0) - 1)
    def _():
        out_ref[:, :width] = dot(context_t[...], attn_rows[...]).astype(bf16)
        out_ref[:, width:] = vectors[...].astype(bf16).T
        for place in (3 * chunks - 2, 3 * chunks - 1):
            for move in piece_moves(place):
                move.wait()


def feed_forward(
    plan,
    sources,
    slot_half,
    spots_in,
    spots_out,
    tokens,
    context,
    cotangent,
    norms,
    feed_total,
    pieces,
    block=256,
):
    rows, width = tokens.shape
    half = rows // 2
    halves = half // block
    chunk = plan["chunk"]
    chunks = 3 * feed_total // chunk

    def source(i, s):
        return (jnp.minimum(i, 2 * halves - 1) + (1 - s[0]) * halves) % (2 * halves)

    row_spec = pl.BlockSpec((block, width), lambda i, s, *_: (source(i, s), 0))
    keep_spec = pl.BlockSpec((block, width), lambda i, *_: (jnp.clip(i - halves, 0, halves - 1), 0))
    send_spec = pl.BlockSpec((block, width), lambda i, *_: (jnp.minimum(i, halves - 1), 0))
    whole = pl.BlockSpec((8, width), lambda i, *_: (0, 0))
    return pl.pallas_call(
        functools.partial(feed_kernel, plan),
        grid_spec=pltpu.PrefetchScalarGridSpec(
            num_scalar_prefetch=3,
            grid=(rows // block + chunks,),
            in_specs=[row_spec, row_spec, row_spec, whole] + [ANY] * len(sources),
            out_specs=[
                keep_spec,
                send_spec,
                row_spec,
                row_spec,
                pl.BlockSpec((width, width + PAIR), lambda i, *_: (0, 0)),
            ]
            + [ANY] * 2,
            scratch_shapes=[pltpu.VMEM((width, width), bf16)]
            + [pltpu.VMEM((width, feed_total), bf16)] * 3
            + [
                pltpu.VMEM((2, block, feed_total), bf16),
                pltpu.VMEM((3, rows, feed_total), bf16),
                pltpu.VMEM((2, width, rows), bf16),
                pltpu.VMEM((width, rows), bf16),
                pltpu.VMEM((rows, width), bf16),
                pltpu.VMEM((PAIR, width), f32),
                pltpu.VMEM((2, width, chunk), bf16),
                pltpu.SemaphoreType.DMA((4, weight_copy_count(plan))),
                pltpu.SemaphoreType.DMA((2, 2 * pieces[1])),
            ],
        ),
        out_shape=[
            jax.ShapeDtypeStruct((half, width), bf16),
            jax.ShapeDtypeStruct((half, width), bf16),
            jax.ShapeDtypeStruct((rows, width), f32),
            jax.ShapeDtypeStruct((rows, width), bf16),
            jax.ShapeDtypeStruct((width, width + PAIR), bf16),
        ]
        + [jax.ShapeDtypeStruct((3,) + pieces, bf16)] * 2,
        compiler_params=pltpu.CompilerParams(vmem_limit_bytes=62 * 2**20),
        cost_estimate=cost(
            2 * rows * width * (9 * feed_total + 3 * width),
            rows * 24 * width + 12 * width * feed_total,
        ),
        name="feed_forward",
    )(slot_half, spots_in, spots_out, tokens, context, cotangent, norms, *sources)


class Transfers:
    def __init__(self, mesh):
        self.fsdp = mesh.shape["fsdp"]
        self.ctx = mesh.shape["ctx"]
        self.tp = mesh.shape["tp"]
        self.levels = self.fsdp // 2
        place = lax.axis_index("fsdp")
        self.z = place // 2
        self.core = place % 2
        self.x = lax.axis_index("ctx")
        self.y = lax.axis_index("tp")
        self.paired = self.ctx == 2 and self.tp == 2 and self.fsdp % 2 == 0

    def swap_slots(self, value):
        return lax.ppermute(value, "ctx", [(i, i ^ 1) for i in range(self.ctx)])

    def swap(self, value, axis):
        return lax.ppermute(value, axis, [(0, 1), (1, 0)])

    def swap_core(self, value):
        return lax.ppermute(value, "fsdp", [(i, i ^ 1) for i in range(self.fsdp)])

    def shift(self, value, step):
        pairs = [
            (2 * level + core, 2 * ((level + step) % self.levels) + core)
            for level in range(self.levels)
            for core in range(2)
        ]
        return lax.ppermute(value, "fsdp", pairs)

    def spots(self, rows, sign, width=None):
        found = []
        for side in range(2):
            for part in range(2):
                for step in range(self.levels):
                    level = (self.z + sign * step + self.levels) % self.levels
                    block = 2 * level + jnp.bitwise_xor(self.core, side)
                    found.append(2 * rows * block + rows * jnp.bitwise_xor(self.x, part))
        if width is None:
            found = found + [jnp.zeros((), jnp.int32)]
        else:
            found = found + [self.y * width, (1 - self.y) * width]
        return jnp.stack(found).astype(jnp.int32)

    def mine(self, shard):
        half = shard.shape[0] // 2
        return lax.dynamic_slice_in_dim(shard, self.x * half, half, 0)

    def shifts(self, block):
        return [self.shift(block, step) for step in range(1, self.levels)]

    def gather_feed(self, gate, up, out, norms):
        rows, width = gate.shape
        model = out.shape[1]
        share = rows // self.tp
        block = lax.dynamic_slice_in_dim(out, self.y * share, share, 0)
        tail = jnp.concatenate([block[16 * j : 16 * (j + 1)] for j in range(share // 16)], 1)
        norm_tail = jnp.pad(norms, ((0, 16 - norms.shape[0]), (0, 2 * width - tail.shape[1] - rows)))
        packed = jnp.concatenate(
            [jnp.concatenate([gate, up], 1), jnp.concatenate([tail, norm_tail], 1)], 0
        )
        packed = lax.all_gather(packed, ("fsdp", "tp"), axis=0)
        pieces = [[], [], [], []]
        for place in range(self.fsdp * self.tp):
            row, col = rows * (place // self.tp), width * (place % self.tp)
            for group in range(2):
                pieces[1 + group].append((0, place, 0, group * width, row, col, rows, width))
            for j in range(share // 16):
                row = rows * (place // self.tp) + share * (place % self.tp) + 16 * j
                pieces[0].append((0, place, rows, model * j, row, 0, 16, model))
        blocks = 2 * self.levels
        for side in range(2):
            for col in range(2):
                for row in range(blocks):
                    pieces[3].append(
                        (
                            1 + side,
                            col * blocks + row,
                            0,
                            0,
                            (side * blocks + row,),
                            (2 * blocks + col,),
                            rows // 2,
                            width,
                        )
                    )
        left = model * (share // 16)
        norms = packed[:: self.tp, rows : rows + norms.shape[0], left : left + rows]
        norms = norms.transpose(1, 0, 2).reshape(norms.shape[1], -1)
        return {"sources": 3, "pieces": pieces, "chunk": 768}, packed, norms

    def add(self, left, right):
        return (left.astype(f32) + right.astype(f32)).astype(bf16)

    def level_shifts(self, value):
        return [self.shift(value[step], step) for step in range(1, self.levels)]

    def sum_shifts(self, value, shifts):
        total = value.astype(f32)
        for other in shifts:
            total = total + other.astype(f32)
        return total.astype(bf16)

    def sum_shards(self, value):
        return lax.psum_scatter(value, "fsdp", scatter_dimension=0, tiled=True)

    def both(self, value, axis, index):
        other = self.swap(value, axis)
        return jnp.where(index == 0, value, other), jnp.where(index == 0, other, value)


def on_device(
    mesh,
    tokens,
    query_key_value_weight,
    output_weight,
    gate_weight,
    up_weight,
    down_weight,
    gain_one,
    shift_one,
    gain_two,
    shift_two,
    lengths,
    positions,
    cotangent,
):
    move = Transfers(mesh)
    shard, model_width = query_key_value_weight.shape[0], tokens.shape[2]
    feed_width = gate_weight.shape[1]
    slot = move.x % 2
    half_rows = tokens.shape[1]

    def sent(value):
        return lax.dynamic_index_in_dim(value, 1 - slot, 0, keepdims=False)

    def to_slot(value, other):
        keep = lax.dynamic_index_in_dim(value, slot, 0, keepdims=False)
        first = jnp.where(slot == 0, keep, other)
        second = jnp.where(slot == 0, other, keep)
        return jnp.concatenate([first, second], 0)

    def from_slot(keep, other):
        return jnp.where(slot == 0, jnp.stack([keep, other]), jnp.stack([other, keep]))

    other_places = move.swap_slots(sent(positions))
    other_tokens = move.swap_slots(sent(tokens))
    length = jnp.where(slot == 0, lengths[0:1], lengths[1:2])
    slot_half = slot[None].astype(jnp.int32)
    norms = jnp.stack([gain_one, shift_one, gain_two, shift_two])
    feed_total = feed_width * move.tp
    down_turned = down_weight.T
    half = shard // 2
    if move.paired:
        levels = move.levels
        blocks = (2, 2 * levels, half)
        attn_in = move.spots(half, -1)
        feed_in = move.spots(half, -1, feed_width)
        qkv = move.mine(query_key_value_weight)
        other_tokens, down, qkv, send_cotangent, norms, *parts = fence(
            other_tokens, move.mine(down_turned), qkv, sent(cotangent), norms, *move.shifts(qkv)
        )
        plan, packed, norms = move.gather_feed(gate_weight, up_weight, output_weight, norms)
        qkv = jnp.stack([qkv] + parts)
        qkv_x = move.swap(qkv, "ctx")
        slot_tokens = to_slot(tokens, other_tokens)
        cosine, sine = turn_tables(to_slot(positions, other_places))
        qkv, qkv_x, send_cotangent, slot_tokens, cosine, sine, down, *parts = fence(
            qkv, qkv_x, send_cotangent, slot_tokens, cosine, sine, down, *move.shifts(down)
        )
        other_cotangent = move.swap_slots(send_cotangent)
        qkv = jnp.stack([qkv, qkv_x]).reshape(1, 2 * levels, half, -1)
        qkv_w = qkv, move.swap_core(qkv)
        down = jnp.stack([down] + parts)
        down_y = move.swap(down, "tp")
    else:
        middle = model_width // 2
        attn_in = jnp.asarray([0, middle, 0], jnp.int32)
        feed_in = attn_in

        def whole(value, axes):
            value = lax.all_gather(value, "fsdp", axis=0, tiled=True)
            if axes:
                value = lax.all_gather(value, "tp", axis=1, tiled=True)
            return value[None]

        sources = [
            whole(output_weight, False),
            whole(gate_weight, True),
            whole(up_weight, True),
            whole(down_turned, True),
        ]
        plan = {
            "sources": 4,
            "chunk": 768,
            "pieces": [
                [(place, 0, 0, 0, 0, 0) + source.shape[1:]] for place, source in enumerate(sources)
            ],
        }
        qkv_all = whole(query_key_value_weight, False)
        qkv_w = qkv_all[None, :, :middle], qkv_all[None, :, middle:]
        norms = lax.all_gather(norms, "fsdp", axis=1, tiled=True)
        other_cotangent = move.swap_slots(sent(cotangent))
        slot_tokens = to_slot(tokens, other_tokens)
        cosine, sine = turn_tables(to_slot(positions, other_places))
    norms = jnp.pad(norms.astype(f32), ((0, 4), (0, 0)))

    queries, key_rows, values, tokens_t = project(attn_in, slot_tokens, cosine, sine, *qkv_w)
    if move.paired:
        queries, down, down_y = fence(queries, down, down_y)
        down = jnp.stack([down, down_y])
        down_x = move.swap(down, "ctx")
    mates = move.ctx // 2
    if mates > 1:
        groups = [[2 * j + s for j in range(mates)] for s in range(2)]

        def gather_rows(value):
            return lax.all_gather(value, "ctx", axis=0, tiled=True, axis_index_groups=groups)

        key_rows = gather_rows(key_rows)
        values = gather_rows(values)
    context, summit = attend(length, queries, key_rows, values)
    if move.paired:
        context, down, down_x, other_cotangent = fence(context, down, down_x, other_cotangent)
        down = jnp.stack([down, down_x], 1).reshape(4 * levels, half, feed_width)
        down = down.reshape((2 * 2 * levels, half, feed_width))
        sources = [packed, down, move.swap_core(down)]
    slot_cotangent = to_slot(cotangent, other_cotangent)
    pieces = (2, 2 * levels, half, feed_width) if move.paired else (1, 1, middle, feed_total)
    feed_out = move.spots(half, 1, feed_width) if move.paired else attn_in
    (
        mixed_keep,
        mixed_send,
        grad_mix_one,
        grad_context,
        attn_o,
        feed_keep,
        feed_send,
    ) = feed_forward(
        plan,
        sources,
        slot_half,
        feed_in,
        feed_out,
        slot_tokens,
        context,
        slot_cotangent,
        norms,
        feed_total,
        pieces,
    )

    pairs = model_width // PAIR
    if move.paired:
        def back(first, count, grads, waits=()):
            return attend_back(
                length,
                queries,
                key_rows,
                values,
                context,
                summit,
                grads,
                cosine,
                sine,
                tokens_t,
                first,
                count,
                waits,
            )

        feed_core = move.swap_core(feed_send)
        other_mixed = move.swap_slots(mixed_send)
        attn_0, raw_0 = back(0, 2, grad_context)

        raw_0, feed_keep, grad_context = fence(
            raw_0, feed_keep, grad_context, waits=(feed_core, other_mixed)
        )
        width = feed_width // 2
        shape = (3, 2, 2, levels, half, feed_width)
        feed_keep, feed_core = feed_keep.reshape(shape), feed_core.reshape(shape)

        def joined(job, place):
            return move.add(feed_keep[job][place], feed_core[job][place])

        every = slice(None)
        first, last = (..., slice(0, width)), (..., slice(width, None))
        down_send = joined(0, (every, 1))
        down_x = move.swap(down_send, "ctx")
        gate_send = joined(1, (1,))
        gate_y = move.swap(gate_send, "tp")
        up_a_send = joined(2, (every, 1) + first)
        up_a_x = move.swap(up_a_send, "ctx")
        up_b_send = joined(2, (1,) + last)
        up_b_y = move.swap(up_b_send, "tp")
        down, gate = joined(0, (every, 0)), joined(1, (0,))
        up_a, up_b = joined(2, (every, 0) + first), joined(2, (0,) + last)
        sends = (down_send, gate_send, up_a_send, up_b_send)
        attn_1, raw_1 = back(2, 2, grad_context, (raw_0, *sends))

        raw_1, attn_1, grad_context, down, gate = fence(
            raw_1, attn_1, grad_context, down, gate, waits=(down_x, gate_y)
        )
        attn_a = move.sum_shards(jnp.concatenate([attn_o, attn_0, attn_1], 1))
        down_send, down = move.add(down[1], down_x[1]), move.add(down[0], down_x[0])
        gate_send, gate = move.add(gate[1], gate_y[1]), move.add(gate[0], gate_y[0])
        down_y = move.swap(down_send, "tp")
        gate_x = move.swap(gate_send, "ctx")
        attn_c, raw_2 = back(4, 2, grad_context, (down_send, gate_send))

        raw_2, attn_c, down, gate, up_a, up_b = fence(
            raw_2, attn_c, down, gate, up_a, up_b, waits=(down_y, gate_x, up_a_x, up_b_y)
        )
        attn_c = move.sum_shards(attn_c)
        up_a_send, up_a = move.add(up_a[1], up_a_x[1]), move.add(up_a[0], up_a_x[0])
        up_b_send, up_b = move.add(up_b[1], up_b_y[1]), move.add(up_b[0], up_b_y[0])
        up_a_y = move.swap(up_a_send, "tp")
        up_b_x = move.swap(up_b_send, "ctx")
        some = jnp.concatenate([move.add(down, down_y), move.add(gate, gate_x)], 2)
        some_shifts = move.level_shifts(some)
        keep_rows, send_rows = token_gradient(
            slot_half,
            attn_in,
            (raw_0, raw_1, raw_2),
            grad_mix_one,
            *qkv_w,
            (up_a_send, up_b_send, some),
        )

        send_rows, up_a, up_b, attn_a, some = fence(
            send_rows, up_a, up_b, attn_a, some[0], waits=(up_a_y, up_b_x)
        )
        attn_x = move.swap(attn_a, "ctx")
        other_rows = move.swap_slots(send_rows)
        up = jnp.concatenate([move.add(up_a, up_a_y), move.add(up_b, up_b_x)], 2)

        up, attn_a, some = fence(up, attn_a, some, waits=(attn_x, *some_shifts))
        up_shifts = move.level_shifts(up)
        some = move.sum_shifts(some, some_shifts)
        attn_a = move.add(attn_a, attn_x)
        attn_y = move.swap(attn_a, "tp")

        up, attn_a, attn_c, some = fence(
            up[0], attn_a, attn_c, some, waits=(attn_y, *up_shifts)
        )
        feed = jnp.concatenate([some, move.sum_shifts(up, up_shifts)], 1)
        feed_x = move.swap(feed, "ctx")
        attn_c_x = move.swap(attn_c, "ctx")
        attn_a = move.add(attn_a, attn_y)
        attn_c = move.add(attn_c, attn_c_x)
        attn_c_y = move.swap(attn_c, "tp")
        low = jnp.where(move.x == 0, feed, feed_x)
        high = jnp.where(move.x == 0, feed_x, feed)
        feed = jnp.concatenate([low, high], 0).astype(f32)
        attn_c = move.add(attn_c, attn_c_y)
        attn = attn_a
        down_gradient = feed[:, :feed_width].T
        gate_gradient = feed[:, feed_width : 2 * feed_width]
        up_gradient = feed[:, 2 * feed_width :]
        out_gradient = attn[:, :model_width].astype(f32)
        vector_grads = [attn[:, model_width + place].astype(f32) for place in range(4)]
        attn = jnp.concatenate([attn[:, model_width + PAIR :], attn_c], 1)
        qkv_gradient = attn.reshape(shard, pairs, 3, PAIR).transpose(0, 2, 1, 3)
        qkv_gradient = qkv_gradient.reshape(shard, 3 * model_width).astype(f32)
        mixed_out = from_slot(mixed_keep, other_mixed)
        grad_tokens = from_slot(keep_rows, other_rows.astype(f32))
    else:
        mixed_out = from_slot(mixed_keep, move.swap_slots(mixed_send))
        grad_query, grad_keys, grad_values = attend_back_plain(
            length, queries, key_rows, values, context, summit, grad_context
        )
        if mates > 1:

            def scatter_rows(value):
                return lax.psum_scatter(
                    value, "ctx", scatter_dimension=0, axis_index_groups=groups, tiled=True
                )

            grad_keys, grad_values = scatter_rows(grad_keys), scatter_rows(grad_values)

        def turn_back(value):
            value = value.reshape(-1, HEADS, 2, HEAD_DIM // 2)
            ahead, behind = value[:, :, 0], value[:, :, 1]
            cos_half = cosine[:, None, : HEAD_DIM // 2]
            sin_half = sine[:, None, HEAD_DIM // 2 : HEAD_DIM]
            value = jnp.stack(
                [ahead * cos_half + behind * sin_half, behind * cos_half - ahead * sin_half], 2
            )
            return value.reshape(-1, model_width)

        grad_raw = jnp.concatenate(
            [turn_back(grad_query), turn_back(grad_keys), grad_values], 1
        ).astype(bf16)
        total = grad_mix_one + dot(grad_raw, qkv_all[0], NT)
        first = lax.dynamic_slice_in_dim(total, slot * half_rows, half_rows, 0)
        second = lax.dynamic_slice_in_dim(total, (1 - slot) * half_rows, half_rows, 0)
        other_rows = move.swap_slots(second.astype(bf16))
        grad_tokens = from_slot(first, other_rows.astype(f32))
        every = ("ctx", "tp")

        def scatter(value, split):
            value = lax.psum(value, every)
            value = lax.psum_scatter(value, "fsdp", scatter_dimension=0, tiled=True)
            if split:
                value = lax.dynamic_slice_in_dim(value, move.y * feed_width, feed_width, 1)
            return value.astype(f32)

        feed = jnp.concatenate([feed_keep[:, 0, 0], feed_send[:, 0, 0]], 1)
        down_gradient = scatter(feed[0], True).T
        gate_gradient = scatter(feed[1], True)
        up_gradient = scatter(feed[2], True)
        outer = dot(slot_tokens, grad_raw, (((0,), (0,)), ((), ())))
        qkv_gradient = scatter(outer.astype(bf16), False)
        attn_o = scatter(attn_o, False)
        out_gradient = attn_o[:, :model_width]
        vector_grads = [attn_o[:, model_width + place] for place in range(4)]
    return (
        mixed_out,
        grad_tokens,
        qkv_gradient,
        out_gradient,
        gate_gradient,
        up_gradient,
        down_gradient,
        *vector_grads,
    )


def solution(mesh):
    in_specs = (
        P(("fsdp", "tp"), "ctx", None),
        P("fsdp", None),
        P("fsdp", None),
        P("fsdp", "tp"),
        P("fsdp", "tp"),
        P("tp", "fsdp"),
        P("fsdp"),
        P("fsdp"),
        P("fsdp"),
        P("fsdp"),
        P(("fsdp", "tp")),
        P(("fsdp", "tp"), "ctx"),
        P(("fsdp", "tp"), "ctx", None),
    )
    out_specs = (
        P(("fsdp", "tp"), "ctx", None),
        P(("fsdp", "tp"), "ctx", None),
        P("fsdp", None),
        P("fsdp", None),
        P("fsdp", "tp"),
        P("fsdp", "tp"),
        P("tp", "fsdp"),
        P("fsdp"),
        P("fsdp"),
        P("fsdp"),
        P("fsdp"),
    )
    return jax.shard_map(
        functools.partial(on_device, mesh),
        mesh=mesh,
        in_specs=in_specs,
        out_specs=out_specs,
        check_vma=False,
    )
```

```python
import functools

import jax
import jax.numpy as jnp
from jax import lax
from jax.experimental import pallas as pl
from jax.experimental.pallas import tpu as pltpu
from jax.sharding import PartitionSpec as P

HEADS = 12
HEAD_DIM = 64
PAIR = 2 * HEAD_DIM

norm_eps = 1e-05
rope_base = 1000.0
masked_bias = -1000000000.0

bf16 = jnp.bfloat16
f32 = jnp.float32
NN = (((1,), (0,)), ((), ()))
NT = (((1,), (1,)), ((), ()))
ANY = pl.BlockSpec(memory_space=pl.ANY)


def dot(left, right, dims=NN):
    return lax.dot_general(left, right, dims, preferred_element_type=f32)


def params(limit=60):
    return pltpu.CompilerParams(vmem_limit_bytes=limit * 2**20)


def cost(flops, moved, exps=0):
    return pl.CostEstimate(flops=int(flops), bytes_accessed=int(moved), transcendentals=int(exps))


def fence(*values, waits=()):
    def nothing(*refs):
        pass

    return pl.pallas_call(
        nothing,
        in_specs=[ANY] * (len(values) + len(waits)),
        out_specs=[ANY] * len(values),
        out_shape=[jax.ShapeDtypeStruct(value.shape, value.dtype) for value in values],
        input_output_aliases={place: place for place in range(len(values))},
        compiler_params=params(),
        name="fence",
    )(*values, *waits)


def piece_copies(own, other, spots, full, sems):
    col_blocks, row_blocks, rows, width = own.shape
    copies = []
    for side, source in enumerate((own, other)):
        for row in range(row_blocks):
            for col in range(col_blocks):
                start = pl.multiple_of(spots[side * row_blocks + row], 16)
                left = pl.multiple_of(spots[2 * row_blocks + col], 128)
                copies.append(
                    pltpu.make_async_copy(
                        source.at[col, row],
                        full.at[pl.ds(start, rows), pl.ds(left, width)],
                        sems.at[(side * row_blocks + row) * col_blocks + col],
                    )
                )
    return copies


def piece_count(own):
    return 2 * own.shape[0] * own.shape[1]


def turned(block, cosine, sine):
    lane = lax.broadcasted_iota(jnp.int32, block.shape, 1)
    first = (lane % HEAD_DIM) < HEAD_DIM // 2
    partner = jnp.where(
        first, pltpu.roll(block, PAIR - HEAD_DIM // 2, 1), pltpu.roll(block, HEAD_DIM // 2, 1)
    )
    return block * cosine + partner * sine


def turn_tables(places):
    half_dim = HEAD_DIM // 2
    frequency = rope_base ** (-jnp.arange(half_dim, dtype=f32) * 2.0 / HEAD_DIM)
    angles = places.astype(f32)[:, None] * frequency
    cosine = jnp.cos(angles)
    sine = jnp.sin(angles)
    return jnp.concatenate([cosine] * 4, 1), jnp.concatenate([-sine, sine, -sine, sine], 1)


def project_kernel(
    spots, tokens, cosine, sine, own, other, q_out, k_out, v_out, tokens_t, weight, sems
):
    width = q_out.shape[1]

    @pl.when(pl.program_id(0) == 0)
    def _():
        copies = piece_copies(own, other, spots, weight, sems)
        for copy in copies:
            copy.start()
        for copy in copies:
            copy.wait()

    rows = tokens[...]
    tokens_t[...] = rows.T
    cos_part = cosine[...]
    sin_part = sine[...]
    for part, out in enumerate((q_out, k_out, v_out)):
        raw = dot(rows, weight[:, part * width : (part + 1) * width])
        for pair in range(width // PAIR):
            cols = slice(pair * PAIR, (pair + 1) * PAIR)
            block = raw[:, cols]
            if part < 2:
                block = turned(block, cos_part, sin_part)
            block = block.astype(bf16)
            if part == 0:
                block = block * jnp.asarray(HEAD_DIM**-0.5, bf16)
            out[:, cols] = block


def project(spots, tokens, cosine, sine, own, other, block=256):
    rows, width = tokens.shape
    total = own.shape[0] * own.shape[3]
    row_spec = pl.BlockSpec((block, width), lambda i, *_: (i, 0))
    table = pl.BlockSpec((block, PAIR), lambda i, *_: (i, 0))
    part = total // 3
    out_spec = pl.BlockSpec((block, part), lambda i, *_: (i, 0))
    return pl.pallas_call(
        project_kernel,
        grid_spec=pltpu.PrefetchScalarGridSpec(
            num_scalar_prefetch=1,
            grid=(rows // block,),
            in_specs=[row_spec, table, table, ANY, ANY],
            out_specs=[out_spec] * 3 + [pl.BlockSpec((width, block), lambda i, *_: (0, i))],
            scratch_shapes=[
                pltpu.VMEM((width, total), bf16),
                pltpu.SemaphoreType.DMA((piece_count(own),)),
            ],
        ),
        out_shape=[jax.ShapeDtypeStruct((rows, part), bf16)] * 3
        + [jax.ShapeDtypeStruct((width, rows), bf16)],
        compiler_params=params(),
        cost_estimate=cost(2 * rows * width * total, 4 * rows * total + 2 * width * total),
        name="project",
    )(spots, tokens, cosine, sine, own, other)


def lane_ids(shape):
    return lax.broadcasted_iota(jnp.int32, shape, 1)


def key_bias(length, shape):
    return jnp.where(lax.broadcasted_iota(jnp.int32, shape, 0) < length, 0.0, masked_bias).astype(
        bf16
    )


def attend_kernel(length, q_ref, k_ref, v_ref, out_ref, summit_ref):
    lane_q = lane_ids(q_ref.shape)
    lane_k = lane_ids(k_ref.shape)
    bias = key_bias(length[0], k_ref.shape)
    queries = q_ref[...]
    keys = k_ref[...]
    values = v_ref[...]
    one = jnp.ones((), bf16)
    zero = jnp.zeros((), bf16)
    outs = []
    summits = []
    for head in range(2):
        mine_q = (lane_q < HEAD_DIM) if head == 0 else (lane_q >= HEAD_DIM)
        mine_k = (lane_k < HEAD_DIM) if head == 0 else (lane_k >= HEAD_DIM)
        spare = HEAD_DIM * (1 - head)
        query = jnp.where(mine_q, queries, jnp.where(lane_q == spare, one, zero))
        key = jnp.where(mine_k, keys, bias)
        value = jnp.where(mine_k, values, one)
        scores = dot(query, key, NT)
        top = jnp.max(scores, axis=1, keepdims=True)
        summed = dot(jnp.exp(scores - top).astype(bf16), value)
        totals = pltpu.roll(summed, HEAD_DIM, 1)
        outs.append(summed / totals)
        summits.append(top + jnp.log(summed))
    low = lane_q < HEAD_DIM
    out_ref[...] = jnp.where(low, outs[0], outs[1]).astype(bf16)
    summit_ref[0] = jnp.where(low, summits[1], summits[0])


def attend(length, queries, keys, values):
    rows, width = queries.shape
    seq = keys.shape[0]
    pairs = width // PAIR
    q_spec = pl.BlockSpec((rows, PAIR), lambda h, *_: (0, h))
    k_spec = pl.BlockSpec((seq, PAIR), lambda h, *_: (0, h))
    return pl.pallas_call(
        attend_kernel,
        grid_spec=pltpu.PrefetchScalarGridSpec(
            num_scalar_prefetch=1,
            grid=(pairs,),
            in_specs=[q_spec, k_spec, k_spec],
            out_specs=[q_spec, pl.BlockSpec((1, rows, PAIR), lambda h, *_: (h, 0, 0))],
        ),
        out_shape=[
            jax.ShapeDtypeStruct((rows, width), bf16),
            jax.ShapeDtypeStruct((pairs, rows, PAIR), f32),
        ],
        compiler_params=params(),
        cost_estimate=cost(16 * rows * seq * width, 12 * rows * width),
        name="attend",
    )(length, queries, keys, values)


def three_parts(value):
    high = value.astype(bf16)
    rest = value - high.astype(f32)
    middle = rest.astype(bf16)
    return high, middle, (rest - middle.astype(f32)).astype(bf16)


def pair_back(length, q_ref, k_ref, v_ref, out_ref, summit_ref, grad_ref):
    rows = q_ref.shape[0]
    lane_q = lane_ids(q_ref.shape)
    lane_k = lane_ids(k_ref.shape)
    bias = key_bias(length[0], k_ref.shape)
    queries = q_ref[...]
    keys = k_ref[...]
    values = v_ref[...]
    grads = grad_ref[...]
    summit = three_parts(summit_ref[0])
    product = grads.astype(f32) * out_ref[...].astype(f32)
    one = jnp.ones((), bf16)
    zero = jnp.zeros((), bf16)
    grads_t = grads.T
    queries_t = queries.T
    dq, dk, dv = [], [], []
    for head in range(2):
        mine_q = (lane_q < HEAD_DIM) if head == 0 else (lane_q >= HEAD_DIM)
        mine_k = (lane_k < HEAD_DIM) if head == 0 else (lane_k >= HEAD_DIM)
        spare = HEAD_DIM * (1 - head)
        own = slice(HEAD_DIM * head, HEAD_DIM * (head + 1))
        row_dot = jnp.sum(jnp.where(mine_q, product, 0.0), axis=1, keepdims=True)
        row_dot = three_parts(jnp.broadcast_to(row_dot, (rows, PAIR)))

        def beside(main, mine, lane, parts, last):
            extra = jnp.where(lane == spare + 3, last, zero)
            for place in range(3):
                extra = jnp.where(lane == spare + place, parts[place], extra)
            return jnp.where(mine, main, extra)

        minus = (-one, -one, -one)
        query = beside(queries, mine_q, lane_q, summit, one)
        key = beside(keys, mine_k, lane_k, minus, bias)
        grad = beside(grads, mine_q, lane_q, row_dot, zero)
        value = beside(values, mine_k, lane_k, minus, zero)
        probs = jnp.exp(dot(query, key, NT))
        grad_scores = (probs * dot(grad, value, NT)).astype(bf16)
        dv.append(dot(grads_t[own], probs.astype(bf16)))
        dk.append(dot(queries_t[own], grad_scores))
        dq.append(dot(grad_scores, keys))
    grad_query = jnp.where(lane_q < HEAD_DIM, dq[0], dq[1]) * HEAD_DIM**-0.5
    return grad_query, jnp.concatenate(dk, 0).T, jnp.concatenate(dv, 0).T


def attend_back_kernel(
    waits,
    length,
    first,
    q_ref,
    k_ref,
    v_ref,
    out_ref,
    summit_ref,
    grad_ref,
    cos_ref,
    sin_ref,
    tokens_t,
    *refs,
):
    outer_ref, raw_ref = refs[-2:]
    grad_query, grad_keys, grad_values = pair_back(
        length, q_ref, k_ref, v_ref, out_ref, summit_ref, grad_ref
    )
    cosine = cos_ref[...]
    sine = sin_ref[...]
    raw = jnp.concatenate(
        [
            turned(grad_query, cosine, -sine).astype(bf16),
            turned(grad_keys, cosine, -sine).astype(bf16),
            grad_values.astype(bf16),
        ],
        1,
    )
    outer_ref[...] = dot(tokens_t[...], raw).astype(bf16)
    raw_ref[...] = raw


def attend_back(
    length,
    queries,
    keys,
    values,
    out,
    summit,
    grads,
    cosine,
    sine,
    tokens_t,
    first,
    pairs,
    waits=(),
    base=None,
):
    rows, width = queries.shape
    q_spec = pl.BlockSpec((rows, PAIR), lambda h, length, first: (0, h + first[0]))
    table = pl.BlockSpec((rows, PAIR), lambda h, *_: (0, 0))
    columns = 3 * PAIR
    if base is None:
        extra, shape, aliases = list(waits), (width, columns * pairs), {}
        outer_spec = pl.BlockSpec((width, columns), lambda h, *_: (0, h))
    else:
        extra, shape = [base] + list(waits), base.shape
        aliases = {11: 0}
        outer_spec = pl.BlockSpec(
            (pl.Element(width), pl.Element(columns)),
            lambda h, length, first: (
                0,
                pl.multiple_of(width + PAIR + (first[0] + h) * columns, PAIR),
            ),
        )
    return pl.pallas_call(
        functools.partial(attend_back_kernel, len(waits)),
        grid_spec=pltpu.PrefetchScalarGridSpec(
            num_scalar_prefetch=2,
            grid=(pairs,),
            in_specs=[
                q_spec,
                q_spec,
                q_spec,
                q_spec,
                pl.BlockSpec((1, rows, PAIR), lambda h, length, first: (h + first[0], 0, 0)),
                q_spec,
                table,
                table,
                pl.BlockSpec(tokens_t.shape, lambda h, *_: (0, 0)),
            ]
            + [ANY] * len(extra),
            out_specs=[
                outer_spec,
                pl.BlockSpec((rows, columns), lambda h, *_: (0, h)),
            ],
        ),
        out_shape=[
            jax.ShapeDtypeStruct(shape, bf16),
            jax.ShapeDtypeStruct((rows, columns * pairs), bf16),
        ],
        input_output_aliases=aliases,
        compiler_params=params(),
        cost_estimate=cost(46 * rows * rows * PAIR * pairs, 16 * rows * PAIR * pairs),
        name="attend_back",
    )(
        length,
        jnp.full((1,), first, jnp.int32),
        queries,
        keys,
        values,
        out,
        summit,
        grads,
        cosine,
        sine,
        tokens_t,
        *extra,
    )


def token_kernel(count, slot_half, spots, *refs):
    raws = refs[:count]
    total_ref, own, other = refs[count : count + 3]
    keep, send, weight, sems = refs[-4:]
    width = total_ref.shape[1]
    step = pl.program_id(0)

    @pl.when(step == 0)
    def _():
        copies = piece_copies(own, other, spots, weight, sems)
        for copy in copies:
            copy.start()
        for copy in copies:
            copy.wait()

    order = [part * width + pair * PAIR for pair in range(width // PAIR) for part in range(3)]
    used = jnp.concatenate([weight[:, left : left + PAIR] for left in order], 1)
    total = total_ref[...]
    left = 0
    for raw in raws:
        size = raw.shape[1]
        total = total + dot(raw[...], used[:, left : left + size], NT)
        left += size

    @pl.when(step < pl.num_programs(0) // 2)
    def _():
        send[...] = total.astype(bf16)

    @pl.when(step >= pl.num_programs(0) // 2)
    def _():
        keep[...] = total


def token_gradient(slot_half, spots, raws, total, own, other, waits=(), block=256):
    rows, width = total.shape
    halves = rows // 2 // block

    def source(i, s):
        return (i + (1 - s[0]) * halves) % (2 * halves)

    def rows_of(value):
        return pl.BlockSpec((block, value.shape[1]), lambda i, s, *_: (source(i, s), 0))

    return pl.pallas_call(
        functools.partial(token_kernel, len(raws)),
        grid_spec=pltpu.PrefetchScalarGridSpec(
            num_scalar_prefetch=2,
            grid=(2 * halves,),
            in_specs=[rows_of(raw) for raw in raws]
            + [rows_of(total), ANY, ANY]
            + [ANY] * len(waits),
            out_specs=[
                pl.BlockSpec((block, width), lambda i, *_: (jnp.maximum(i - halves, 0), 0)),
                pl.BlockSpec((block, width), lambda i, *_: (jnp.minimum(i, halves - 1), 0)),
            ],
            scratch_shapes=[
                pltpu.VMEM((width, 3 * width), bf16),
                pltpu.SemaphoreType.DMA((piece_count(own),)),
            ],
        ),
        out_shape=[
            jax.ShapeDtypeStruct((rows // 2, width), f32),
            jax.ShapeDtypeStruct((rows // 2, width), bf16),
        ],
        compiler_params=params(),
        cost_estimate=cost(6 * rows * width * width, 14 * rows * width + 6 * width * width),
        name="token_gradient",
    )(slot_half, spots, *raws, total, own, other, *waits)


def attend_back_plain_kernel(
    length, q_ref, k_ref, v_ref, out_ref, summit_ref, grad_ref, dq_ref, dk_ref, dv_ref
):
    dq_ref[...], dk_ref[...], dv_ref[...] = pair_back(
        length, q_ref, k_ref, v_ref, out_ref, summit_ref, grad_ref
    )


def attend_back_plain(length, queries, keys, values, out, summit, grads):
    rows, width = queries.shape
    seq = keys.shape[0]
    q_spec = pl.BlockSpec((rows, PAIR), lambda h, *_: (0, h))
    k_spec = pl.BlockSpec((seq, PAIR), lambda h, *_: (0, h))
    return pl.pallas_call(
        attend_back_plain_kernel,
        grid_spec=pltpu.PrefetchScalarGridSpec(
            num_scalar_prefetch=1,
            grid=(width // PAIR,),
            in_specs=[
                q_spec,
                k_spec,
                k_spec,
                q_spec,
                pl.BlockSpec((1, rows, PAIR), lambda h, *_: (h, 0, 0)),
                q_spec,
            ],
            out_specs=[q_spec, k_spec, k_spec],
        ),
        out_shape=[jax.ShapeDtypeStruct((count, width), f32) for count in (rows, seq, seq)],
        compiler_params=params(),
        cost_estimate=cost(40 * rows * seq * width, 16 * rows * width),
        name="attend_back_plain",
    )(length, queries, keys, values, out, summit, grads)


def row_mean(value):
    return jnp.mean(value, axis=-1, keepdims=True)


def normalize(value):
    centered = value - row_mean(value)
    inverse = lax.rsqrt(row_mean(centered * centered) + norm_eps)
    return centered * inverse, inverse


def normalize_back(normed, inverse, gain, upstream):
    scaled = upstream * gain
    return inverse * (scaled - row_mean(scaled) - normed * row_mean(scaled * normed))


def weight_copies(plan, group, sources, weight, spots, sems, chunk):
    copies = [[] for _ in range(weight.shape[1] // chunk)]
    count = 0
    for source, first, top, left, row, col, rows, cols in plan["pieces"][group]:
        dynamic = isinstance(row, tuple)
        if dynamic:
            row = pl.multiple_of(spots[row[0]], 16)
            col = pl.multiple_of(spots[col[0]], 128)
        width = cols if dynamic else min(cols, chunk)
        for inside in range(0, cols, width):
            copy = pltpu.make_async_copy(
                sources[source].at[first, pl.ds(top, rows), pl.ds(left + inside, width)],
                weight.at[pl.ds(row, rows), pl.ds(col + inside, width)],
                sems.at[group, count],
            )
            copies[0 if dynamic else (col + inside) // chunk].append(copy)
            count += 1
    return copies


def weight_copy_count(plan):
    counts = []
    for pieces in plan["pieces"]:
        counts.append(
            sum(
                1 if isinstance(row, tuple) else -(-cols // plan["chunk"])
                for _, _, _, _, row, _, _, cols in pieces
            )
        )
    return max(counts)


def feed_kernel(plan, slot_half, spots_in, spots_out, tokens, context, cotangent, norms, *refs):
    sources = refs[: plan["sources"]]
    (
        mixed_keep,
        mixed_send,
        grad_mix_one,
        grad_context,
        out_ref,
        keep,
        send,
        w_out,
        w_gate,
        w_up,
        w_down,
        slopes,
        known,
        lefts,
        context_t,
        attn_rows,
        vectors,
        stage,
        out_stage,
        sems,
        out_sems,
        out_sem,
    ) = refs[plan["sources"] :]
    chunk = plan["chunk"]
    rows, width = tokens.shape
    steps = known.shape[1] // rows
    step = pl.program_id(0)
    feed_total = w_gate.shape[1]
    chunks = feed_total // chunk
    weights = (w_out, w_gate, w_up, w_down)
    loads = [
        weight_copies(plan, group, sources, weight, spots_in, sems, min(chunk, weight.shape[1]))
        for group, weight in enumerate(weights)
    ]

    @pl.when(step == 0)
    def _():
        order = [loads[0][0]]
        for place in range(chunks):
            order += [loads[1][place], loads[2][place], loads[3][place]]
        for group in order:
            for copy in group:
                copy.start()
        vectors[...] = jnp.zeros_like(vectors)

    def arrive(*groups):
        @pl.when(step == 0)
        def _():
            for group in groups:
                for copy in group:
                    copy.wait()

    @pl.when(step < steps)
    def _():
        here = pl.ds(pl.multiple_of(step * rows, rows), rows)
        gain_one = norms[0:1, :]
        shift_one = norms[1:2, :]
        gain_two = norms[2:3, :]
        shift_two = norms[3:4, :]
        arrive(loads[0][0])
        context_rows = context[...]
        context_t[:, here] = context_rows.T
        normed_one, inverse_one = normalize(
            tokens[...].astype(f32) + dot(context_rows, w_out[...])
        )
        out_one = normed_one * gain_one + shift_one
        feed_in = out_one.astype(bf16)
        lefts[1, :, here] = feed_in.T
        total = out_one
        for place in range(chunks):
            cols = slice(place * chunk, (place + 1) * chunk)
            arrive(loads[1][place], loads[2][place], loads[3][place])
            gate = dot(feed_in, w_gate[:, cols])
            up = dot(feed_in, w_up[:, cols])
            sig = jax.nn.sigmoid(gate)
            swish = gate * sig
            hid = (swish * up).astype(bf16)
            known[0, here, cols] = hid
            slopes[0, :, cols] = swish.astype(bf16)
            slopes[1, :, cols] = (up * (sig + swish * (1.0 - sig))).astype(bf16)
            total = total + dot(hid, w_down[:, cols], NT)
        normed_two, inverse_two = normalize(total)
        mixed = (normed_two * gain_two + shift_two).astype(bf16)

        @pl.when(step < steps // 2)
        def _():
            mixed_send[...] = mixed

        @pl.when(step >= steps // 2)
        def _():
            mixed_keep[...] = mixed

        upstream = cotangent[...].astype(f32)
        grad_mix_two = normalize_back(normed_two, inverse_two, gain_two, upstream)
        branch = grad_mix_two.astype(bf16)
        lefts[0, :, here] = branch.T
        grad_out_one = grad_mix_two
        for place in range(chunks):
            cols = slice(place * chunk, (place + 1) * chunk)
            grad_hidden = dot(branch, w_down[:, cols])
            grad_gate = (grad_hidden * slopes[1, :, cols].astype(f32)).astype(bf16)
            grad_up = (grad_hidden * slopes[0, :, cols].astype(f32)).astype(bf16)
            known[1, here, cols] = grad_gate
            known[2, here, cols] = grad_up
            grad_out_one = (
                grad_out_one
                + dot(grad_gate, w_gate[:, cols], NT)
                + dot(grad_up, w_up[:, cols], NT)
            )
        vectors[0:1, :] += jnp.sum(grad_out_one * normed_one, axis=0, keepdims=True)
        vectors[1:2, :] += jnp.sum(grad_out_one, axis=0, keepdims=True)
        vectors[2:3, :] += jnp.sum(upstream * normed_two, axis=0, keepdims=True)
        vectors[3:4, :] += jnp.sum(upstream, axis=0, keepdims=True)
        grad_one = normalize_back(normed_one, inverse_one, gain_one, grad_out_one)
        grad_mix_one[...] = grad_one
        grad_rows = grad_one.astype(bf16)
        attn_rows[here, :] = grad_rows
        grad_context[...] = dot(grad_rows, w_out[...], NT).astype(bf16)

    _, col_blocks, row_blocks, piece_rows, _ = keep.shape
    per = chunks // col_blocks

    def piece_moves(place):
        job, inside = place // chunks, place % chunks
        col, left = inside // per, inside % per * chunk
        slot = place % 2
        moves = []
        for side, out in enumerate((keep, send)):
            for row in range(row_blocks):
                start = pl.multiple_of(spots_out[side * row_blocks + row], 16)
                moves.append(
                    pltpu.make_async_copy(
                        stage.at[slot, pl.ds(start, piece_rows), :],
                        out.at[job, col, row, :, pl.ds(pl.multiple_of(left, 128), chunk)],
                        out_sems.at[slot, side * row_blocks + row],
                    )
                )
        return moves

    @pl.when(step >= steps)
    def _():
        place = step - steps

        @pl.when(place >= 2)
        def _():
            for move in piece_moves(place - 2):
                move.wait()

        job, inside = place // chunks, place % chunks
        start = spots_out[2 * row_blocks + inside // per] + inside % per * chunk
        cols = pl.ds(pl.multiple_of(start, 128), chunk)
        left_t = lefts[jnp.minimum(job, 1)]
        stage[place % 2] = dot(left_t, known[job, :, cols]).astype(bf16)
        for move in piece_moves(place):
            move.start()

    @pl.when(step == pl.num_programs(0) - 1)
    def _():
        out_stage[:, :width] = dot(context_t[...], attn_rows[...]).astype(bf16)
        out_stage[:, width:] = vectors[...].astype(bf16).T
        move = pltpu.make_async_copy(out_stage, out_ref.at[:, pl.ds(0, width + PAIR)], out_sem)
        move.start()
        move.wait()
        for place in (3 * chunks - 2, 3 * chunks - 1):
            for move in piece_moves(place):
                move.wait()


def feed_forward(
    plan,
    sources,
    slot_half,
    spots_in,
    spots_out,
    tokens,
    context,
    cotangent,
    norms,
    feed_total,
    pieces,
    more,
    block=256,
):
    rows, width = tokens.shape
    half = rows // 2
    halves = half // block
    chunk = plan["chunk"]
    chunks = 3 * feed_total // chunk

    def source(i, s):
        return (jnp.minimum(i, 2 * halves - 1) + (1 - s[0]) * halves) % (2 * halves)

    row_spec = pl.BlockSpec((block, width), lambda i, s, *_: (source(i, s), 0))
    keep_spec = pl.BlockSpec((block, width), lambda i, *_: (jnp.clip(i - halves, 0, halves - 1), 0))
    send_spec = pl.BlockSpec((block, width), lambda i, *_: (jnp.minimum(i, halves - 1), 0))
    whole = pl.BlockSpec((8, width), lambda i, *_: (0, 0))
    return pl.pallas_call(
        functools.partial(feed_kernel, plan),
        grid_spec=pltpu.PrefetchScalarGridSpec(
            num_scalar_prefetch=3,
            grid=(rows // block + chunks,),
            in_specs=[row_spec, row_spec, row_spec, whole] + [ANY] * len(sources),
            out_specs=[
                keep_spec,
                send_spec,
                row_spec,
                row_spec,
                ANY,
            ]
            + [ANY] * 2,
            scratch_shapes=[pltpu.VMEM((width, width), bf16)]
            + [pltpu.VMEM((width, feed_total), bf16)] * 3
            + [
                pltpu.VMEM((2, block, feed_total), bf16),
                pltpu.VMEM((3, rows, feed_total), bf16),
                pltpu.VMEM((2, width, rows), bf16),
                pltpu.VMEM((width, rows), bf16),
                pltpu.VMEM((rows, width), bf16),
                pltpu.VMEM((PAIR, width), f32),
                pltpu.VMEM((2, width, chunk), bf16),
                pltpu.VMEM((width, width + PAIR), bf16),
                pltpu.SemaphoreType.DMA((4, weight_copy_count(plan))),
                pltpu.SemaphoreType.DMA((2, 2 * pieces[1])),
                pltpu.SemaphoreType.DMA,
            ],
        ),
        out_shape=[
            jax.ShapeDtypeStruct((half, width), bf16),
            jax.ShapeDtypeStruct((half, width), bf16),
            jax.ShapeDtypeStruct((rows, width), f32),
            jax.ShapeDtypeStruct((rows, width), bf16),
            jax.ShapeDtypeStruct((width, width + PAIR + more), bf16),
        ]
        + [jax.ShapeDtypeStruct((3,) + pieces, bf16)] * 2,
        compiler_params=pltpu.CompilerParams(vmem_limit_bytes=62 * 2**20),
        cost_estimate=cost(
            2 * rows * width * (9 * feed_total + 3 * width),
            rows * 24 * width + 12 * width * feed_total,
        ),
        name="feed_forward",
    )(slot_half, spots_in, spots_out, tokens, context, cotangent, norms, *sources)


class Transfers:
    def __init__(self, mesh):
        self.fsdp = mesh.shape["fsdp"]
        self.ctx = mesh.shape["ctx"]
        self.tp = mesh.shape["tp"]
        self.levels = self.fsdp // 2
        place = lax.axis_index("fsdp")
        self.z = place // 2
        self.core = place % 2
        self.x = lax.axis_index("ctx")
        self.y = lax.axis_index("tp")
        self.paired = self.ctx == 2 and self.tp == 2 and self.fsdp % 2 == 0

    def swap_slots(self, value):
        return lax.ppermute(value, "ctx", [(i, i ^ 1) for i in range(self.ctx)])

    def swap(self, value, axis):
        return lax.ppermute(value, axis, [(0, 1), (1, 0)])

    def swap_core(self, value):
        return lax.ppermute(value, "fsdp", [(i, i ^ 1) for i in range(self.fsdp)])

    def shift(self, value, step):
        pairs = [
            (2 * level + core, 2 * ((level + step) % self.levels) + core)
            for level in range(self.levels)
            for core in range(2)
        ]
        return lax.ppermute(value, "fsdp", pairs)

    def spots(self, rows, sign, width=None):
        found = []
        for side in range(2):
            for part in range(2):
                for step in range(self.levels):
                    level = (self.z + sign * step + self.levels) % self.levels
                    block = 2 * level + jnp.bitwise_xor(self.core, side)
                    found.append(2 * rows * block + rows * jnp.bitwise_xor(self.x, part))
        if width is None:
            found = found + [jnp.zeros((), jnp.int32)]
        else:
            found = found + [self.y * width, (1 - self.y) * width]
        return jnp.stack(found).astype(jnp.int32)

    def mine(self, shard):
        half = shard.shape[0] // 2
        return lax.dynamic_slice_in_dim(shard, self.x * half, half, 0)

    def shifts(self, block):
        return [self.shift(block, step) for step in range(1, self.levels)]

    def gather_feed(self, gate, up, out, norms):
        rows, width = gate.shape
        model = out.shape[1]
        share = rows // self.tp
        block = lax.dynamic_slice_in_dim(out, self.y * share, share, 0)
        tail = jnp.concatenate([block[16 * j : 16 * (j + 1)] for j in range(share // 16)], 1)
        norm_tail = jnp.pad(norms, ((0, 16 - norms.shape[0]), (0, 2 * width - tail.shape[1] - rows)))
        packed = jnp.concatenate(
            [jnp.concatenate([gate, up], 1), jnp.concatenate([tail, norm_tail], 1)], 0
        )
        packed = lax.all_gather(packed, ("fsdp", "tp"), axis=0)
        pieces = [[], [], [], []]
        for place in range(self.fsdp * self.tp):
            row, col = rows * (place // self.tp), width * (place % self.tp)
            for group in range(2):
                pieces[1 + group].append((0, place, 0, group * width, row, col, rows, width))
            for j in range(share // 16):
                row = rows * (place // self.tp) + share * (place % self.tp) + 16 * j
                pieces[0].append((0, place, rows, model * j, row, 0, 16, model))
        blocks = 2 * self.levels
        for side in range(2):
            for col in range(2):
                for row in range(blocks):
                    pieces[3].append(
                        (
                            1 + side,
                            col * blocks + row,
                            0,
                            0,
                            (side * blocks + row,),
                            (2 * blocks + col,),
                            rows // 2,
                            width,
                        )
                    )
        left = model * (share // 16)
        norms = packed[:: self.tp, rows : rows + norms.shape[0], left : left + rows]
        norms = norms.transpose(1, 0, 2).reshape(norms.shape[1], -1)
        return {"sources": 3, "pieces": pieces, "chunk": 768}, packed, norms

    def add(self, left, right):
        return (left.astype(f32) + right.astype(f32)).astype(bf16)

    def level_shifts(self, value):
        return [self.shift(value[step], step) for step in range(1, self.levels)]

    def sum_shifts(self, value, shifts):
        total = value.astype(f32)
        for other in shifts:
            total = total + other.astype(f32)
        return total.astype(bf16)

    def sum_shards(self, value):
        return lax.psum_scatter(value, "fsdp", scatter_dimension=0, tiled=True)

    def sum_all(self, value):
        corners = [(i, i ^ 3) for i in range(4)]
        over_y = self.swap(value, "tp")
        over_x = self.swap(value, "ctx")
        across = lax.ppermute(value, ("ctx", "tp"), corners)
        here = value.astype(f32) + over_y.astype(f32)
        there = over_x.astype(f32) + across.astype(f32)
        return (here + there).astype(bf16)

    def both(self, value, axis, index):
        other = self.swap(value, axis)
        return jnp.where(index == 0, value, other), jnp.where(index == 0, other, value)


def on_device(
    mesh,
    tokens,
    query_key_value_weight,
    output_weight,
    gate_weight,
    up_weight,
    down_weight,
    gain_one,
    shift_one,
    gain_two,
    shift_two,
    lengths,
    positions,
    cotangent,
):
    move = Transfers(mesh)
    shard, model_width = query_key_value_weight.shape[0], tokens.shape[2]
    feed_width = gate_weight.shape[1]
    slot = move.x % 2
    half_rows = tokens.shape[1]

    def sent(value):
        return lax.dynamic_index_in_dim(value, 1 - slot, 0, keepdims=False)

    def to_slot(value, other):
        keep = lax.dynamic_index_in_dim(value, slot, 0, keepdims=False)
        first = jnp.where(slot == 0, keep, other)
        second = jnp.where(slot == 0, other, keep)
        return jnp.concatenate([first, second], 0)

    def from_slot(keep, other):
        return jnp.where(slot == 0, jnp.stack([keep, other]), jnp.stack([other, keep]))

    other_places = move.swap_slots(sent(positions))
    other_tokens = move.swap_slots(sent(tokens))
    length = jnp.where(slot == 0, lengths[0:1], lengths[1:2])
    slot_half = slot[None].astype(jnp.int32)
    norms = jnp.stack([gain_one, shift_one, gain_two, shift_two])
    feed_total = feed_width * move.tp
    down_turned = down_weight.T
    half = shard // 2
    if move.paired:
        levels = move.levels
        blocks = (2, 2 * levels, half)
        narrow = query_key_value_weight.shape[1] // 2
        attn_in = move.spots(half, -1, narrow)
        feed_in = move.spots(half, -1, feed_width)
        plan, packed, norms = move.gather_feed(gate_weight, up_weight, output_weight, norms)
        qkv = lax.dynamic_slice_in_dim(
            move.mine(query_key_value_weight), move.y * narrow, narrow, 1
        )
        down, qkv, send_cotangent, *parts = fence(
            move.mine(down_turned), qkv, sent(cotangent), *move.shifts(qkv)
        )
        qkv = jnp.stack([qkv] + parts)
        qkv_y = move.swap(qkv, "tp")
        down_parts = move.shifts(down)
        slot_tokens = to_slot(tokens, other_tokens)
        cosine, sine = turn_tables(to_slot(positions, other_places))
        qkv, qkv_y, slot_tokens, cosine, sine = fence(qkv, qkv_y, slot_tokens, cosine, sine)
        qkv = jnp.stack([qkv, qkv_y])
        qkv_x = move.swap(qkv, "ctx")
        qkv, qkv_x, send_cotangent, down, *down_parts = fence(
            qkv, qkv_x, send_cotangent, down, *down_parts
        )
        other_cotangent = move.swap_slots(send_cotangent)
        qkv = jnp.stack([qkv, qkv_x], 1).reshape(2, 2 * levels, half, narrow)
        qkv_w = qkv, move.swap_core(qkv)
        down = jnp.stack([down] + down_parts)
        down_y = move.swap(down, "tp")
    else:
        middle = model_width // 2
        attn_in = jnp.asarray([0, middle, 0], jnp.int32)
        feed_in = attn_in

        def whole(value, axes):
            value = lax.all_gather(value, "fsdp", axis=0, tiled=True)
            if axes:
                value = lax.all_gather(value, "tp", axis=1, tiled=True)
            return value[None]

        sources = [
            whole(output_weight, False),
            whole(gate_weight, True),
            whole(up_weight, True),
            whole(down_turned, True),
        ]
        plan = {
            "sources": 4,
            "chunk": 768,
            "pieces": [
                [(place, 0, 0, 0, 0, 0) + source.shape[1:]] for place, source in enumerate(sources)
            ],
        }
        qkv_all = whole(query_key_value_weight, False)
        qkv_w = qkv_all[None, :, :middle], qkv_all[None, :, middle:]
        norms = lax.all_gather(norms, "fsdp", axis=1, tiled=True)
        other_cotangent = move.swap_slots(sent(cotangent))
        slot_tokens = to_slot(tokens, other_tokens)
        cosine, sine = turn_tables(to_slot(positions, other_places))
    norms = jnp.pad(norms.astype(f32), ((0, 4), (0, 0)))

    queries, key_rows, values, tokens_t = project(attn_in, slot_tokens, cosine, sine, *qkv_w)
    if move.paired:
        queries, down, down_y = fence(queries, down, down_y)
        down = jnp.stack([down, down_y])
        down_x = move.swap(down, "ctx")
    mates = move.ctx // 2
    if mates > 1:
        groups = [[2 * j + s for j in range(mates)] for s in range(2)]

        def gather_rows(value):
            return lax.all_gather(value, "ctx", axis=0, tiled=True, axis_index_groups=groups)

        key_rows = gather_rows(key_rows)
        values = gather_rows(values)
    context, summit = attend(length, queries, key_rows, values)
    if move.paired:
        context, down, down_x, other_cotangent = fence(context, down, down_x, other_cotangent)
        down = jnp.stack([down, down_x], 1).reshape(4 * levels, half, feed_width)
        down = down.reshape((2 * 2 * levels, half, feed_width))
        sources = [packed, down, move.swap_core(down)]
    slot_cotangent = to_slot(cotangent, other_cotangent)
    pieces = (2, 2 * levels, half, feed_width) if move.paired else (1, 1, middle, feed_total)
    feed_out = move.spots(half, 1, feed_width) if move.paired else attn_in
    (
        mixed_keep,
        mixed_send,
        grad_mix_one,
        grad_context,
        attn_o,
        feed_keep,
        feed_send,
    ) = feed_forward(
        plan,
        sources,
        slot_half,
        feed_in,
        feed_out,
        slot_tokens,
        context,
        slot_cotangent,
        norms,
        feed_total,
        pieces,
        4 * 3 * PAIR if move.paired else 0,
    )

    pairs = model_width // PAIR
    if move.paired:
        def back(first, count, grads, waits=(), base=None):
            return attend_back(
                length,
                queries,
                key_rows,
                values,
                context,
                summit,
                grads,
                cosine,
                sine,
                tokens_t,
                first,
                count,
                waits,
                base,
            )

        feed_core = move.swap_core(feed_send)
        other_mixed = move.swap_slots(mixed_send)
        attn_a, raw_0 = back(0, 2, grad_context, (), attn_o)

        raw_0, feed_keep, grad_context = fence(
            raw_0, feed_keep, grad_context, waits=(feed_core, other_mixed)
        )
        width = feed_width // 2
        shape = (3, 2, 2, levels, half, feed_width)
        feed_keep, feed_core = feed_keep.reshape(shape), feed_core.reshape(shape)

        def joined(job, place):
            return move.add(feed_keep[job][place], feed_core[job][place])

        every = slice(None)
        first, last = (..., slice(0, width)), (..., slice(width, None))
        down_send = joined(0, (every, 1))
        down_x = move.swap(down_send, "ctx")
        gate_send = joined(1, (1,))
        gate_y = move.swap(gate_send, "tp")
        up_a_send = joined(2, (every, 1) + first)
        up_a_x = move.swap(up_a_send, "ctx")
        up_b_send = joined(2, (1,) + last)
        up_b_y = move.swap(up_b_send, "tp")
        down, gate = joined(0, (every, 0)), joined(1, (0,))
        up_a, up_b = joined(2, (every, 0) + first), joined(2, (0,) + last)
        sends = (down_send, gate_send, up_a_send, up_b_send)
        attn_a, raw_1 = back(2, 2, grad_context, (raw_0, *sends), attn_a)

        raw_1, attn_a, grad_context, down, gate = fence(
            raw_1, attn_a, grad_context, down, gate, waits=(down_x, gate_y)
        )
        attn_a = move.sum_shards(attn_a)
        down_send, down = move.add(down[1], down_x[1]), move.add(down[0], down_x[0])
        gate_send, gate = move.add(gate[1], gate_y[1]), move.add(gate[0], gate_y[0])
        down_y = move.swap(down_send, "tp")
        gate_x = move.swap(gate_send, "ctx")
        attn_c, raw_2 = back(4, 2, grad_context, (down_send, gate_send))

        raw_2, attn_c, down, gate, up_a, up_b = fence(
            raw_2, attn_c, down, gate, up_a, up_b, waits=(down_y, gate_x, up_a_x, up_b_y)
        )
        attn_c = move.sum_shards(attn_c)
        up_a_send, up_a = move.add(up_a[1], up_a_x[1]), move.add(up_a[0], up_a_x[0])
        up_b_send, up_b = move.add(up_b[1], up_b_y[1]), move.add(up_b[0], up_b_y[0])
        up_a_y = move.swap(up_a_send, "tp")
        up_b_x = move.swap(up_b_send, "ctx")
        some = jnp.concatenate([move.add(down, down_y), move.add(gate, gate_x)], 2)
        some_shifts = move.level_shifts(some)
        keep_rows, send_rows = token_gradient(
            slot_half,
            attn_in,
            (raw_0, raw_1, raw_2),
            grad_mix_one,
            *qkv_w,
            (up_a_send, up_b_send, some),
        )

        send_rows, up_a, up_b, attn_a, some = fence(
            send_rows, up_a, up_b, attn_a, some[0], waits=(up_a_y, up_b_x)
        )
        attn_x = move.swap(attn_a, "ctx")
        other_rows = move.swap_slots(send_rows)
        up = jnp.concatenate([move.add(up_a, up_a_y), move.add(up_b, up_b_x)], 2)

        up, attn_a, some = fence(up, attn_a, some, waits=(attn_x, *some_shifts))
        up_shifts = move.level_shifts(up)
        some = move.sum_shifts(some, some_shifts)
        attn_a = move.add(attn_a, attn_x)
        attn_y = move.swap(attn_a, "tp")

        up, attn_a, attn_c, some = fence(
            up[0], attn_a, attn_c, some, waits=(attn_y, *up_shifts)
        )
        feed = jnp.concatenate([some, move.sum_shifts(up, up_shifts)], 1)
        feed_x = move.swap(feed, "ctx")
        attn_a = move.add(attn_a, attn_y)
        attn_c = move.sum_all(attn_c)
        low = jnp.where(move.x == 0, feed, feed_x)
        high = jnp.where(move.x == 0, feed_x, feed)
        feed = jnp.concatenate([low, high], 0).astype(f32)
        attn = attn_a
        down_gradient = feed[:, :feed_width].T
        gate_gradient = feed[:, feed_width : 2 * feed_width]
        up_gradient = feed[:, 2 * feed_width :]
        out_gradient = attn[:, :model_width].astype(f32)
        vector_grads = [attn[:, model_width + place].astype(f32) for place in range(4)]
        attn = jnp.concatenate([attn[:, model_width + PAIR :], attn_c], 1)
        qkv_gradient = attn.reshape(shard, pairs, 3, PAIR).transpose(0, 2, 1, 3)
        qkv_gradient = qkv_gradient.reshape(shard, 3 * model_width).astype(f32)
        mixed_out = from_slot(mixed_keep, other_mixed)
        grad_tokens = from_slot(keep_rows, other_rows.astype(f32))
    else:
        mixed_out = from_slot(mixed_keep, move.swap_slots(mixed_send))
        grad_query, grad_keys, grad_values = attend_back_plain(
            length, queries, key_rows, values, context, summit, grad_context
        )
        if mates > 1:

            def scatter_rows(value):
                return lax.psum_scatter(
                    value, "ctx", scatter_dimension=0, axis_index_groups=groups, tiled=True
                )

            grad_keys, grad_values = scatter_rows(grad_keys), scatter_rows(grad_values)

        def turn_back(value):
            value = value.reshape(-1, HEADS, 2, HEAD_DIM // 2)
            ahead, behind = value[:, :, 0], value[:, :, 1]
            cos_half = cosine[:, None, : HEAD_DIM // 2]
            sin_half = sine[:, None, HEAD_DIM // 2 : HEAD_DIM]
            value = jnp.stack(
                [ahead * cos_half + behind * sin_half, behind * cos_half - ahead * sin_half], 2
            )
            return value.reshape(-1, model_width)

        grad_raw = jnp.concatenate(
            [turn_back(grad_query), turn_back(grad_keys), grad_values], 1
        ).astype(bf16)
        total = grad_mix_one + dot(grad_raw, qkv_all[0], NT)
        first = lax.dynamic_slice_in_dim(total, slot * half_rows, half_rows, 0)
        second = lax.dynamic_slice_in_dim(total, (1 - slot) * half_rows, half_rows, 0)
        other_rows = move.swap_slots(second.astype(bf16))
        grad_tokens = from_slot(first, other_rows.astype(f32))
        every = ("ctx", "tp")

        def scatter(value, split):
            value = lax.psum(value, every)
            value = lax.psum_scatter(value, "fsdp", scatter_dimension=0, tiled=True)
            if split:
                value = lax.dynamic_slice_in_dim(value, move.y * feed_width, feed_width, 1)
            return value.astype(f32)

        feed = jnp.concatenate([feed_keep[:, 0, 0], feed_send[:, 0, 0]], 1)
        down_gradient = scatter(feed[0], True).T
        gate_gradient = scatter(feed[1], True)
        up_gradient = scatter(feed[2], True)
        outer = dot(slot_tokens, grad_raw, (((0,), (0,)), ((), ())))
        qkv_gradient = scatter(outer.astype(bf16), False)
        attn_o = scatter(attn_o, False)
        out_gradient = attn_o[:, :model_width]
        vector_grads = [attn_o[:, model_width + place] for place in range(4)]
    return (
        mixed_out,
        grad_tokens,
        qkv_gradient,
        out_gradient,
        gate_gradient,
        up_gradient,
        down_gradient,
        *vector_grads,
    )


def solution(mesh):
    in_specs = (
        P(("fsdp", "tp"), "ctx", None),
        P("fsdp", None),
        P("fsdp", None),
        P("fsdp", "tp"),
        P("fsdp", "tp"),
        P("tp", "fsdp"),
        P("fsdp"),
        P("fsdp"),
        P("fsdp"),
        P("fsdp"),
        P(("fsdp", "tp")),
        P(("fsdp", "tp"), "ctx"),
        P(("fsdp", "tp"), "ctx", None),
    )
    out_specs = (
        P(("fsdp", "tp"), "ctx", None),
        P(("fsdp", "tp"), "ctx", None),
        P("fsdp", None),
        P("fsdp", None),
        P("fsdp", "tp"),
        P("fsdp", "tp"),
        P("tp", "fsdp"),
        P("fsdp"),
        P("fsdp"),
        P("fsdp"),
        P("fsdp"),
    )
    return jax.shard_map(
        functools.partial(on_device, mesh),
        mesh=mesh,
        in_specs=in_specs,
        out_specs=out_specs,
        check_vma=False,
    )
```

```python
import functools

import jax
import jax.numpy as jnp
from jax import lax
from jax.experimental import pallas as pl
from jax.experimental.pallas import tpu as pltpu
from jax.sharding import PartitionSpec as P

HEADS = 12
HEAD_DIM = 64
PAIR = 2 * HEAD_DIM

norm_eps = 1e-05
rope_base = 1000.0
masked_bias = -1000000000.0

bf16 = jnp.bfloat16
f32 = jnp.float32
NN = (((1,), (0,)), ((), ()))
NT = (((1,), (1,)), ((), ()))
ANY = pl.BlockSpec(memory_space=pl.ANY)


def dot(left, right, dims=NN):
    return lax.dot_general(left, right, dims, preferred_element_type=f32)


def params(limit=60):
    return pltpu.CompilerParams(vmem_limit_bytes=limit * 2**20)


def cost(flops, moved, exps=0):
    return pl.CostEstimate(flops=int(flops), bytes_accessed=int(moved), transcendentals=int(exps))


def fence(*values, waits=()):
    def nothing(*refs):
        pass

    return pl.pallas_call(
        nothing,
        in_specs=[ANY] * (len(values) + len(waits)),
        out_specs=[ANY] * len(values),
        out_shape=[jax.ShapeDtypeStruct(value.shape, value.dtype) for value in values],
        input_output_aliases={place: place for place in range(len(values))},
        compiler_params=params(),
        name="fence",
    )(*values, *waits)


def piece_copies(own, other, spots, full, sems):
    col_blocks, row_blocks, rows, width = own.shape
    copies = []
    for side, source in enumerate((own, other)):
        for row in range(row_blocks):
            for col in range(col_blocks):
                start = pl.multiple_of(spots[side * row_blocks + row], 16)
                left = pl.multiple_of(spots[2 * row_blocks + col], 128)
                copies.append(
                    pltpu.make_async_copy(
                        source.at[col, row],
                        full.at[pl.ds(start, rows), pl.ds(left, width)],
                        sems.at[(side * row_blocks + row) * col_blocks + col],
                    )
                )
    return copies


def piece_count(own):
    return 2 * own.shape[0] * own.shape[1]


def turned(block, cosine, sine):
    lane = lax.broadcasted_iota(jnp.int32, block.shape, 1)
    first = (lane % HEAD_DIM) < HEAD_DIM // 2
    partner = jnp.where(
        first, pltpu.roll(block, PAIR - HEAD_DIM // 2, 1), pltpu.roll(block, HEAD_DIM // 2, 1)
    )
    return block * cosine + partner * sine


def turn_tables(places):
    half_dim = HEAD_DIM // 2
    frequency = rope_base ** (-jnp.arange(half_dim, dtype=f32) * 2.0 / HEAD_DIM)
    angles = places.astype(f32)[:, None] * frequency
    cosine = jnp.cos(angles)
    sine = jnp.sin(angles)
    return jnp.concatenate([cosine] * 4, 1), jnp.concatenate([-sine, sine, -sine, sine], 1)


def project_kernel(
    spots, tokens, cosine, sine, own, other, q_out, k_out, v_out, tokens_t, weight, sems
):
    width = q_out.shape[1]

    @pl.when(pl.program_id(0) == 0)
    def _():
        copies = piece_copies(own, other, spots, weight, sems)
        for copy in copies:
            copy.start()
        for copy in copies:
            copy.wait()

    rows = tokens[...]
    tokens_t[...] = rows.T
    cos_part = cosine[...]
    sin_part = sine[...]
    for part, out in enumerate((q_out, k_out, v_out)):
        raw = dot(rows, weight[:, part * width : (part + 1) * width])
        for pair in range(width // PAIR):
            cols = slice(pair * PAIR, (pair + 1) * PAIR)
            block = raw[:, cols]
            if part < 2:
                block = turned(block, cos_part, sin_part)
            block = block.astype(bf16)
            if part == 0:
                block = block * jnp.asarray(HEAD_DIM**-0.5, bf16)
            out[:, cols] = block


def project(spots, tokens, cosine, sine, own, other, block=256):
    rows, width = tokens.shape
    total = own.shape[0] * own.shape[3]
    row_spec = pl.BlockSpec((block, width), lambda i, *_: (i, 0))
    table = pl.BlockSpec((block, PAIR), lambda i, *_: (i, 0))
    part = total // 3
    out_spec = pl.BlockSpec((block, part), lambda i, *_: (i, 0))
    return pl.pallas_call(
        project_kernel,
        grid_spec=pltpu.PrefetchScalarGridSpec(
            num_scalar_prefetch=1,
            grid=(rows // block,),
            in_specs=[row_spec, table, table, ANY, ANY],
            out_specs=[out_spec] * 3 + [pl.BlockSpec((width, block), lambda i, *_: (0, i))],
            scratch_shapes=[
                pltpu.VMEM((width, total), bf16),
                pltpu.SemaphoreType.DMA((piece_count(own),)),
            ],
        ),
        out_shape=[jax.ShapeDtypeStruct((rows, part), bf16)] * 3
        + [jax.ShapeDtypeStruct((width, rows), bf16)],
        compiler_params=params(),
        cost_estimate=cost(2 * rows * width * total, 4 * rows * total + 2 * width * total),
        name="project",
    )(spots, tokens, cosine, sine, own, other)


def lane_ids(shape):
    return lax.broadcasted_iota(jnp.int32, shape, 1)


def key_bias(length, shape):
    return jnp.where(lax.broadcasted_iota(jnp.int32, shape, 0) < length, 0.0, masked_bias).astype(
        bf16
    )


def attend_kernel(length, q_ref, k_ref, v_ref, out_ref, summit_ref):
    lane_q = lane_ids(q_ref.shape)
    lane_k = lane_ids(k_ref.shape)
    bias = key_bias(length[0], k_ref.shape)
    queries = q_ref[...]
    keys = k_ref[...]
    values = v_ref[...]
    one = jnp.ones((), bf16)
    zero = jnp.zeros((), bf16)
    outs = []
    summits = []
    for head in range(2):
        mine_q = (lane_q < HEAD_DIM) if head == 0 else (lane_q >= HEAD_DIM)
        mine_k = (lane_k < HEAD_DIM) if head == 0 else (lane_k >= HEAD_DIM)
        spare = HEAD_DIM * (1 - head)
        query = jnp.where(mine_q, queries, jnp.where(lane_q == spare, one, zero))
        key = jnp.where(mine_k, keys, bias)
        value = jnp.where(mine_k, values, one)
        scores = dot(query, key, NT)
        top = jnp.max(scores, axis=1, keepdims=True)
        summed = dot(jnp.exp(scores - top).astype(bf16), value)
        totals = pltpu.roll(summed, HEAD_DIM, 1)
        outs.append(summed / totals)
        summits.append(top + jnp.log(summed))
    low = lane_q < HEAD_DIM
    out_ref[...] = jnp.where(low, outs[0], outs[1]).astype(bf16)
    summit_ref[0] = jnp.where(low, summits[1], summits[0])


def attend(length, queries, keys, values):
    rows, width = queries.shape
    seq = keys.shape[0]
    pairs = width // PAIR
    q_spec = pl.BlockSpec((rows, PAIR), lambda h, *_: (0, h))
    k_spec = pl.BlockSpec((seq, PAIR), lambda h, *_: (0, h))
    return pl.pallas_call(
        attend_kernel,
        grid_spec=pltpu.PrefetchScalarGridSpec(
            num_scalar_prefetch=1,
            grid=(pairs,),
            in_specs=[q_spec, k_spec, k_spec],
            out_specs=[q_spec, pl.BlockSpec((1, rows, PAIR), lambda h, *_: (h, 0, 0))],
        ),
        out_shape=[
            jax.ShapeDtypeStruct((rows, width), bf16),
            jax.ShapeDtypeStruct((pairs, rows, PAIR), f32),
        ],
        compiler_params=params(),
        cost_estimate=cost(16 * rows * seq * width, 12 * rows * width),
        name="attend",
    )(length, queries, keys, values)


def three_parts(value):
    high = value.astype(bf16)
    rest = value - high.astype(f32)
    middle = rest.astype(bf16)
    return high, middle, (rest - middle.astype(f32)).astype(bf16)


def pair_back(length, q_ref, k_ref, v_ref, out_ref, summit_ref, grad_ref):
    rows = q_ref.shape[0]
    lane_q = lane_ids(q_ref.shape)
    lane_k = lane_ids(k_ref.shape)
    bias = key_bias(length[0], k_ref.shape)
    queries = q_ref[...]
    keys = k_ref[...]
    values = v_ref[...]
    grads = grad_ref[...]
    summit = three_parts(summit_ref[0])
    product = grads.astype(f32) * out_ref[...].astype(f32)
    one = jnp.ones((), bf16)
    zero = jnp.zeros((), bf16)
    grads_t = grads.T
    queries_t = queries.T
    dq, dk, dv = [], [], []
    for head in range(2):
        mine_q = (lane_q < HEAD_DIM) if head == 0 else (lane_q >= HEAD_DIM)
        mine_k = (lane_k < HEAD_DIM) if head == 0 else (lane_k >= HEAD_DIM)
        spare = HEAD_DIM * (1 - head)
        own = slice(HEAD_DIM * head, HEAD_DIM * (head + 1))
        row_dot = jnp.sum(jnp.where(mine_q, product, 0.0), axis=1, keepdims=True)
        row_dot = three_parts(jnp.broadcast_to(row_dot, (rows, PAIR)))

        def beside(main, mine, lane, parts, last):
            extra = jnp.where(lane == spare + 3, last, zero)
            for place in range(3):
                extra = jnp.where(lane == spare + place, parts[place], extra)
            return jnp.where(mine, main, extra)

        minus = (-one, -one, -one)
        query = beside(queries, mine_q, lane_q, summit, one)
        key = beside(keys, mine_k, lane_k, minus, bias)
        grad = beside(grads, mine_q, lane_q, row_dot, zero)
        value = beside(values, mine_k, lane_k, minus, zero)
        probs = jnp.exp(dot(query, key, NT))
        grad_scores = (probs * dot(grad, value, NT)).astype(bf16)
        dv.append(dot(grads_t[own], probs.astype(bf16)))
        dk.append(dot(queries_t[own], grad_scores))
        dq.append(dot(grad_scores, keys))
    grad_query = jnp.where(lane_q < HEAD_DIM, dq[0], dq[1]) * HEAD_DIM**-0.5
    return grad_query, jnp.concatenate(dk, 0).T, jnp.concatenate(dv, 0).T


def attend_back_kernel(
    waits,
    length,
    first,
    q_ref,
    k_ref,
    v_ref,
    out_ref,
    summit_ref,
    grad_ref,
    cos_ref,
    sin_ref,
    tokens_t,
    *refs,
):
    outer_ref, raw_ref = refs[-2:]
    grad_query, grad_keys, grad_values = pair_back(
        length, q_ref, k_ref, v_ref, out_ref, summit_ref, grad_ref
    )
    cosine = cos_ref[...]
    sine = sin_ref[...]
    raw = jnp.concatenate(
        [
            turned(grad_query, cosine, -sine).astype(bf16),
            turned(grad_keys, cosine, -sine).astype(bf16),
            grad_values.astype(bf16),
        ],
        1,
    )
    outer_ref[...] = dot(tokens_t[...], raw).astype(bf16)
    raw_ref[...] = raw


def attend_back(
    length,
    queries,
    keys,
    values,
    out,
    summit,
    grads,
    cosine,
    sine,
    tokens_t,
    first,
    pairs,
    waits=(),
    base=None,
):
    rows, width = queries.shape
    q_spec = pl.BlockSpec((rows, PAIR), lambda h, length, first: (0, h + first[0]))
    table = pl.BlockSpec((rows, PAIR), lambda h, *_: (0, 0))
    columns = 3 * PAIR
    if base is None:
        extra, shape, aliases = list(waits), (width, columns * pairs), {}
        outer_spec = pl.BlockSpec((width, columns), lambda h, *_: (0, h))
    else:
        extra, shape = [base] + list(waits), base.shape
        aliases = {11: 0}
        outer_spec = pl.BlockSpec(
            (pl.Element(width), pl.Element(columns)),
            lambda h, length, first: (
                0,
                pl.multiple_of(width + PAIR + (first[0] + h) * columns, PAIR),
            ),
        )
    return pl.pallas_call(
        functools.partial(attend_back_kernel, len(waits)),
        grid_spec=pltpu.PrefetchScalarGridSpec(
            num_scalar_prefetch=2,
            grid=(pairs,),
            in_specs=[
                q_spec,
                q_spec,
                q_spec,
                q_spec,
                pl.BlockSpec((1, rows, PAIR), lambda h, length, first: (h + first[0], 0, 0)),
                q_spec,
                table,
                table,
                pl.BlockSpec(tokens_t.shape, lambda h, *_: (0, 0)),
            ]
            + [ANY] * len(extra),
            out_specs=[
                outer_spec,
                pl.BlockSpec((rows, columns), lambda h, *_: (0, h)),
            ],
        ),
        out_shape=[
            jax.ShapeDtypeStruct(shape, bf16),
            jax.ShapeDtypeStruct((rows, columns * pairs), bf16),
        ],
        input_output_aliases=aliases,
        compiler_params=params(),
        cost_estimate=cost(46 * rows * rows * PAIR * pairs, 16 * rows * PAIR * pairs),
        name="attend_back",
    )(
        length,
        jnp.full((1,), first, jnp.int32),
        queries,
        keys,
        values,
        out,
        summit,
        grads,
        cosine,
        sine,
        tokens_t,
        *extra,
    )


def token_kernel(count, slot_half, spots, *refs):
    raws = refs[:count]
    total_ref, own, other = refs[count : count + 3]
    keep, send, weight, sems = refs[-4:]
    width = total_ref.shape[1]
    step = pl.program_id(0)

    @pl.when(step == 0)
    def _():
        copies = piece_copies(own, other, spots, weight, sems)
        for copy in copies:
            copy.start()
        for copy in copies:
            copy.wait()

    order = [part * width + pair * PAIR for pair in range(width // PAIR) for part in range(3)]
    used = jnp.concatenate([weight[:, left : left + PAIR] for left in order], 1)
    total = total_ref[...]
    left = 0
    for raw in raws:
        size = raw.shape[1]
        total = total + dot(raw[...], used[:, left : left + size], NT)
        left += size

    @pl.when(step < pl.num_programs(0) // 2)
    def _():
        send[...] = total.astype(bf16)

    @pl.when(step >= pl.num_programs(0) // 2)
    def _():
        keep[...] = total


def token_gradient(slot_half, spots, raws, total, own, other, waits=(), block=256):
    rows, width = total.shape
    halves = rows // 2 // block

    def source(i, s):
        return (i + (1 - s[0]) * halves) % (2 * halves)

    def rows_of(value):
        return pl.BlockSpec((block, value.shape[1]), lambda i, s, *_: (source(i, s), 0))

    return pl.pallas_call(
        functools.partial(token_kernel, len(raws)),
        grid_spec=pltpu.PrefetchScalarGridSpec(
            num_scalar_prefetch=2,
            grid=(2 * halves,),
            in_specs=[rows_of(raw) for raw in raws]
            + [rows_of(total), ANY, ANY]
            + [ANY] * len(waits),
            out_specs=[
                pl.BlockSpec((block, width), lambda i, *_: (jnp.maximum(i - halves, 0), 0)),
                pl.BlockSpec((block, width), lambda i, *_: (jnp.minimum(i, halves - 1), 0)),
            ],
            scratch_shapes=[
                pltpu.VMEM((width, 3 * width), bf16),
                pltpu.SemaphoreType.DMA((piece_count(own),)),
            ],
        ),
        out_shape=[
            jax.ShapeDtypeStruct((rows // 2, width), f32),
            jax.ShapeDtypeStruct((rows // 2, width), bf16),
        ],
        compiler_params=params(),
        cost_estimate=cost(6 * rows * width * width, 14 * rows * width + 6 * width * width),
        name="token_gradient",
    )(slot_half, spots, *raws, total, own, other, *waits)


def attend_back_plain_kernel(
    length, q_ref, k_ref, v_ref, out_ref, summit_ref, grad_ref, dq_ref, dk_ref, dv_ref
):
    dq_ref[...], dk_ref[...], dv_ref[...] = pair_back(
        length, q_ref, k_ref, v_ref, out_ref, summit_ref, grad_ref
    )


def attend_back_plain(length, queries, keys, values, out, summit, grads):
    rows, width = queries.shape
    seq = keys.shape[0]
    q_spec = pl.BlockSpec((rows, PAIR), lambda h, *_: (0, h))
    k_spec = pl.BlockSpec((seq, PAIR), lambda h, *_: (0, h))
    return pl.pallas_call(
        attend_back_plain_kernel,
        grid_spec=pltpu.PrefetchScalarGridSpec(
            num_scalar_prefetch=1,
            grid=(width // PAIR,),
            in_specs=[
                q_spec,
                k_spec,
                k_spec,
                q_spec,
                pl.BlockSpec((1, rows, PAIR), lambda h, *_: (h, 0, 0)),
                q_spec,
            ],
            out_specs=[q_spec, k_spec, k_spec],
        ),
        out_shape=[jax.ShapeDtypeStruct((count, width), f32) for count in (rows, seq, seq)],
        compiler_params=params(),
        cost_estimate=cost(40 * rows * seq * width, 16 * rows * width),
        name="attend_back_plain",
    )(length, queries, keys, values, out, summit, grads)


def row_mean(value):
    return jnp.mean(value, axis=-1, keepdims=True)


def normalize(value):
    centered = value - row_mean(value)
    inverse = lax.rsqrt(row_mean(centered * centered) + norm_eps)
    return centered * inverse, inverse


def normalize_back(normed, inverse, gain, upstream):
    scaled = upstream * gain
    return inverse * (scaled - row_mean(scaled) - normed * row_mean(scaled * normed))


def weight_copies(plan, group, sources, weight, spots, sems, chunk):
    copies = [[] for _ in range(weight.shape[1] // chunk)]
    count = 0
    for source, first, top, left, row, col, rows, cols in plan["pieces"][group]:
        dynamic = isinstance(row, tuple)
        if dynamic:
            row = pl.multiple_of(spots[row[0]], 16)
            col = pl.multiple_of(spots[col[0]], 128)
        width = cols if dynamic else min(cols, chunk)
        for inside in range(0, cols, width):
            copy = pltpu.make_async_copy(
                sources[source].at[first, pl.ds(top, rows), pl.ds(left + inside, width)],
                weight.at[pl.ds(row, rows), pl.ds(col + inside, width)],
                sems.at[group, count],
            )
            copies[0 if dynamic else (col + inside) // chunk].append(copy)
            count += 1
    return copies


def weight_copy_count(plan):
    counts = []
    for pieces in plan["pieces"]:
        counts.append(
            sum(
                1 if isinstance(row, tuple) else -(-cols // plan["chunk"])
                for _, _, _, _, row, _, _, cols in pieces
            )
        )
    return max(counts)


def feed_kernel(plan, slot_half, spots_in, spots_out, tokens, context, cotangent, norms, *refs):
    sources = refs[: plan["sources"]]
    (
        mixed_keep,
        mixed_send,
        grad_mix_one,
        grad_context,
        out_ref,
        keep,
        send,
        w_out,
        w_gate,
        w_up,
        w_down,
        slopes,
        known,
        lefts,
        context_t,
        attn_rows,
        vectors,
        stage,
        out_stage,
        sems,
        out_sems,
        out_sem,
    ) = refs[plan["sources"] :]
    chunk = plan["chunk"]
    rows, width = tokens.shape
    steps = known.shape[1] // rows
    step = pl.program_id(0)
    feed_total = w_gate.shape[1]
    chunks = feed_total // chunk
    weights = (w_out, w_gate, w_up, w_down)
    loads = [
        weight_copies(plan, group, sources, weight, spots_in, sems, min(chunk, weight.shape[1]))
        for group, weight in enumerate(weights)
    ]

    @pl.when(step == 0)
    def _():
        order = [loads[0][0]]
        for place in range(chunks):
            order += [loads[1][place], loads[2][place], loads[3][place]]
        for group in order:
            for copy in group:
                copy.start()
        vectors[...] = jnp.zeros_like(vectors)

    def arrive(*groups):
        @pl.when(step == 0)
        def _():
            for group in groups:
                for copy in group:
                    copy.wait()

    @pl.when(step < steps)
    def _():
        here = pl.ds(pl.multiple_of(step * rows, rows), rows)
        gain_one = norms[0:1, :]
        shift_one = norms[1:2, :]
        gain_two = norms[2:3, :]
        shift_two = norms[3:4, :]
        arrive(loads[0][0])
        context_rows = context[...]
        context_t[:, here] = context_rows.T
        normed_one, inverse_one = normalize(
            tokens[...].astype(f32) + dot(context_rows, w_out[...])
        )
        out_one = normed_one * gain_one + shift_one
        feed_in = out_one.astype(bf16)
        lefts[1, :, here] = feed_in.T
        total = out_one
        for place in range(chunks):
            cols = slice(place * chunk, (place + 1) * chunk)
            arrive(loads[1][place], loads[2][place], loads[3][place])
            gate = dot(feed_in, w_gate[:, cols])
            up = dot(feed_in, w_up[:, cols])
            sig = jax.nn.sigmoid(gate)
            swish = gate * sig
            hid = (swish * up).astype(bf16)
            known[0, here, cols] = hid
            slopes[0, :, cols] = swish.astype(bf16)
            slopes[1, :, cols] = (up * (sig + swish * (1.0 - sig))).astype(bf16)
            total = total + dot(hid, w_down[:, cols], NT)
        normed_two, inverse_two = normalize(total)
        mixed = (normed_two * gain_two + shift_two).astype(bf16)

        @pl.when(step < steps // 2)
        def _():
            mixed_send[...] = mixed

        @pl.when(step >= steps // 2)
        def _():
            mixed_keep[...] = mixed

        upstream = cotangent[...].astype(f32)
        grad_mix_two = normalize_back(normed_two, inverse_two, gain_two, upstream)
        branch = grad_mix_two.astype(bf16)
        lefts[0, :, here] = branch.T
        grad_out_one = grad_mix_two
        for place in range(chunks):
            cols = slice(place * chunk, (place + 1) * chunk)
            grad_hidden = dot(branch, w_down[:, cols])
            grad_gate = (grad_hidden * slopes[1, :, cols].astype(f32)).astype(bf16)
            grad_up = (grad_hidden * slopes[0, :, cols].astype(f32)).astype(bf16)
            known[1, here, cols] = grad_gate
            known[2, here, cols] = grad_up
            grad_out_one = (
                grad_out_one
                + dot(grad_gate, w_gate[:, cols], NT)
                + dot(grad_up, w_up[:, cols], NT)
            )
        vectors[0:1, :] += jnp.sum(grad_out_one * normed_one, axis=0, keepdims=True)
        vectors[1:2, :] += jnp.sum(grad_out_one, axis=0, keepdims=True)
        vectors[2:3, :] += jnp.sum(upstream * normed_two, axis=0, keepdims=True)
        vectors[3:4, :] += jnp.sum(upstream, axis=0, keepdims=True)
        grad_one = normalize_back(normed_one, inverse_one, gain_one, grad_out_one)
        grad_mix_one[...] = grad_one
        grad_rows = grad_one.astype(bf16)
        attn_rows[here, :] = grad_rows
        grad_context[...] = dot(grad_rows, w_out[...], NT).astype(bf16)

    _, col_blocks, row_blocks, piece_rows, _ = keep.shape
    per = chunks // col_blocks

    def piece_moves(place):
        job, inside = place // chunks, place % chunks
        col, left = inside // per, inside % per * chunk
        slot = place % 2
        moves = []
        for side, out in enumerate((keep, send)):
            for row in range(row_blocks):
                start = pl.multiple_of(spots_out[side * row_blocks + row], 16)
                moves.append(
                    pltpu.make_async_copy(
                        stage.at[slot, pl.ds(start, piece_rows), :],
                        out.at[job, col, row, :, pl.ds(pl.multiple_of(left, 128), chunk)],
                        out_sems.at[slot, side * row_blocks + row],
                    )
                )
        return moves

    @pl.when(step >= steps)
    def _():
        place = step - steps

        @pl.when(place >= 2)
        def _():
            for move in piece_moves(place - 2):
                move.wait()

        job, inside = place // chunks, place % chunks
        start = spots_out[2 * row_blocks + inside // per] + inside % per * chunk
        cols = pl.ds(pl.multiple_of(start, 128), chunk)
        left_t = lefts[jnp.minimum(job, 1)]
        stage[place % 2] = dot(left_t, known[job, :, cols]).astype(bf16)
        for move in piece_moves(place):
            move.start()

    @pl.when(step == pl.num_programs(0) - 1)
    def _():
        out_stage[:, :width] = dot(context_t[...], attn_rows[...]).astype(bf16)
        out_stage[:, width:] = vectors[...].astype(bf16).T
        move = pltpu.make_async_copy(out_stage, out_ref.at[:, pl.ds(0, width + PAIR)], out_sem)
        move.start()
        move.wait()
        for place in (3 * chunks - 2, 3 * chunks - 1):
            for move in piece_moves(place):
                move.wait()


def feed_forward(
    plan,
    sources,
    slot_half,
    spots_in,
    spots_out,
    tokens,
    context,
    cotangent,
    norms,
    feed_total,
    pieces,
    more,
    block=256,
):
    rows, width = tokens.shape
    half = rows // 2
    halves = half // block
    chunk = plan["chunk"]
    chunks = 3 * feed_total // chunk

    def source(i, s):
        return (jnp.minimum(i, 2 * halves - 1) + (1 - s[0]) * halves) % (2 * halves)

    row_spec = pl.BlockSpec((block, width), lambda i, s, *_: (source(i, s), 0))
    keep_spec = pl.BlockSpec((block, width), lambda i, *_: (jnp.clip(i - halves, 0, halves - 1), 0))
    send_spec = pl.BlockSpec((block, width), lambda i, *_: (jnp.minimum(i, halves - 1), 0))
    whole = pl.BlockSpec((8, width), lambda i, *_: (0, 0))
    return pl.pallas_call(
        functools.partial(feed_kernel, plan),
        grid_spec=pltpu.PrefetchScalarGridSpec(
            num_scalar_prefetch=3,
            grid=(rows // block + chunks,),
            in_specs=[row_spec, row_spec, row_spec, whole] + [ANY] * len(sources),
            out_specs=[
                keep_spec,
                send_spec,
                row_spec,
                row_spec,
                ANY,
            ]
            + [ANY] * 2,
            scratch_shapes=[pltpu.VMEM((width, width), bf16)]
            + [pltpu.VMEM((width, feed_total), bf16)] * 3
            + [
                pltpu.VMEM((2, block, feed_total), bf16),
                pltpu.VMEM((3, rows, feed_total), bf16),
                pltpu.VMEM((2, width, rows), bf16),
                pltpu.VMEM((width, rows), bf16),
                pltpu.VMEM((rows, width), bf16),
                pltpu.VMEM((PAIR, width), f32),
                pltpu.VMEM((2, width, chunk), bf16),
                pltpu.VMEM((width, width + PAIR), bf16),
                pltpu.SemaphoreType.DMA((4, weight_copy_count(plan))),
                pltpu.SemaphoreType.DMA((2, 2 * pieces[1])),
                pltpu.SemaphoreType.DMA,
            ],
        ),
        out_shape=[
            jax.ShapeDtypeStruct((half, width), bf16),
            jax.ShapeDtypeStruct((half, width), bf16),
            jax.ShapeDtypeStruct((rows, width), f32),
            jax.ShapeDtypeStruct((rows, width), bf16),
            jax.ShapeDtypeStruct((width, width + PAIR + more), bf16),
        ]
        + [jax.ShapeDtypeStruct((3,) + pieces, bf16)] * 2,
        compiler_params=pltpu.CompilerParams(vmem_limit_bytes=62 * 2**20),
        cost_estimate=cost(
            2 * rows * width * (9 * feed_total + 3 * width),
            rows * 24 * width + 12 * width * feed_total,
        ),
        name="feed_forward",
    )(slot_half, spots_in, spots_out, tokens, context, cotangent, norms, *sources)


class Transfers:
    def __init__(self, mesh):
        self.fsdp = mesh.shape["fsdp"]
        self.ctx = mesh.shape["ctx"]
        self.tp = mesh.shape["tp"]
        self.levels = self.fsdp // 2
        place = lax.axis_index("fsdp")
        self.z = place // 2
        self.core = place % 2
        self.x = lax.axis_index("ctx")
        self.y = lax.axis_index("tp")
        self.paired = self.ctx == 2 and self.tp == 2 and self.fsdp % 2 == 0

    def swap_slots(self, value):
        return lax.ppermute(value, "ctx", [(i, i ^ 1) for i in range(self.ctx)])

    def swap(self, value, axis):
        return lax.ppermute(value, axis, [(0, 1), (1, 0)])

    def swap_core(self, value):
        return lax.ppermute(value, "fsdp", [(i, i ^ 1) for i in range(self.fsdp)])

    def shift(self, value, step):
        pairs = [
            (2 * level + core, 2 * ((level + step) % self.levels) + core)
            for level in range(self.levels)
            for core in range(2)
        ]
        return lax.ppermute(value, "fsdp", pairs)

    def spots(self, rows, sign, width=None):
        found = []
        for side in range(2):
            for part in range(2):
                for step in range(self.levels):
                    level = (self.z + sign * step + self.levels) % self.levels
                    block = 2 * level + jnp.bitwise_xor(self.core, side)
                    found.append(2 * rows * block + rows * jnp.bitwise_xor(self.x, part))
        if width is None:
            found = found + [jnp.zeros((), jnp.int32)]
        else:
            found = found + [self.y * width, (1 - self.y) * width]
        return jnp.stack(found).astype(jnp.int32)

    def mine(self, shard):
        half = shard.shape[0] // 2
        return lax.dynamic_slice_in_dim(shard, self.x * half, half, 0)

    def shifts(self, block):
        return [self.shift(block, step) for step in range(1, self.levels)]

    def gather_feed(self, gate, up, out, norms):
        rows, width = gate.shape
        model = out.shape[1]
        share = rows // self.tp
        block = lax.dynamic_slice_in_dim(out, self.y * share, share, 0)
        tail = jnp.concatenate([block[16 * j : 16 * (j + 1)] for j in range(share // 16)], 1)
        norm_tail = jnp.pad(norms, ((0, 16 - norms.shape[0]), (0, 2 * width - tail.shape[1] - rows)))
        packed = jnp.concatenate(
            [jnp.concatenate([gate, up], 1), jnp.concatenate([tail, norm_tail], 1)], 0
        )
        packed = lax.all_gather(packed, ("fsdp", "tp"), axis=0)
        pieces = [[], [], [], []]
        for place in range(self.fsdp * self.tp):
            row, col = rows * (place // self.tp), width * (place % self.tp)
            for group in range(2):
                pieces[1 + group].append((0, place, 0, group * width, row, col, rows, width))
            for j in range(share // 16):
                row = rows * (place // self.tp) + share * (place % self.tp) + 16 * j
                pieces[0].append((0, place, rows, model * j, row, 0, 16, model))
        blocks = 2 * self.levels
        for side in range(2):
            for col in range(2):
                for row in range(blocks):
                    pieces[3].append(
                        (
                            1 + side,
                            col * blocks + row,
                            0,
                            0,
                            (side * blocks + row,),
                            (2 * blocks + col,),
                            rows // 2,
                            width,
                        )
                    )
        left = model * (share // 16)
        norms = packed[:: self.tp, rows : rows + norms.shape[0], left : left + rows]
        norms = norms.transpose(1, 0, 2).reshape(norms.shape[1], -1)
        return {"sources": 3, "pieces": pieces, "chunk": 768}, packed, norms

    def add(self, left, right):
        return (left.astype(f32) + right.astype(f32)).astype(bf16)

    def level_shifts(self, value):
        return [self.shift(value[step], step) for step in range(1, self.levels)]

    def sum_shifts(self, value, shifts):
        total = value.astype(f32)
        for other in shifts:
            total = total + other.astype(f32)
        return total.astype(bf16)

    def sum_shards(self, value):
        return lax.psum_scatter(value, "fsdp", scatter_dimension=0, tiled=True)

    def sum_all(self, value):
        corners = [(i, i ^ 3) for i in range(4)]
        over_y = self.swap(value, "tp")
        over_x = self.swap(value, "ctx")
        across = lax.ppermute(value, ("ctx", "tp"), corners)
        here = value.astype(f32) + over_y.astype(f32)
        there = over_x.astype(f32) + across.astype(f32)
        return (here + there).astype(bf16)

    def both(self, value, axis, index):
        other = self.swap(value, axis)
        return jnp.where(index == 0, value, other), jnp.where(index == 0, other, value)


def on_device(
    mesh,
    tokens,
    query_key_value_weight,
    output_weight,
    gate_weight,
    up_weight,
    down_weight,
    gain_one,
    shift_one,
    gain_two,
    shift_two,
    lengths,
    positions,
    cotangent,
):
    move = Transfers(mesh)
    shard, model_width = query_key_value_weight.shape[0], tokens.shape[2]
    feed_width = gate_weight.shape[1]
    slot = move.x % 2
    half_rows = tokens.shape[1]

    def sent(value):
        return lax.dynamic_index_in_dim(value, 1 - slot, 0, keepdims=False)

    def to_slot(value, other):
        keep = lax.dynamic_index_in_dim(value, slot, 0, keepdims=False)
        first = jnp.where(slot == 0, keep, other)
        second = jnp.where(slot == 0, other, keep)
        return jnp.concatenate([first, second], 0)

    def from_slot(keep, other):
        return jnp.where(slot == 0, jnp.stack([keep, other]), jnp.stack([other, keep]))

    other_places = move.swap_slots(sent(positions))
    other_tokens = move.swap_slots(sent(tokens))
    length = jnp.where(slot == 0, lengths[0:1], lengths[1:2])
    slot_half = slot[None].astype(jnp.int32)
    norms = jnp.stack([gain_one, shift_one, gain_two, shift_two])
    feed_total = feed_width * move.tp
    down_turned = down_weight.T
    half = shard // 2
    if move.paired:
        levels = move.levels
        blocks = (2, 2 * levels, half)
        narrow = query_key_value_weight.shape[1] // 2
        attn_in = move.spots(half, -1, narrow)
        feed_in = move.spots(half, -1, feed_width)
        plan, packed, norms = move.gather_feed(gate_weight, up_weight, output_weight, norms)
        qkv = lax.dynamic_slice_in_dim(
            move.mine(query_key_value_weight), move.y * narrow, narrow, 1
        )
        down, qkv, send_cotangent, *parts = fence(
            move.mine(down_turned), qkv, sent(cotangent), *move.shifts(qkv)
        )
        qkv = jnp.stack([qkv] + parts)
        qkv_y = move.swap(qkv, "tp")
        down_parts = move.shifts(down)
        slot_tokens = to_slot(tokens, other_tokens)
        cosine, sine = turn_tables(to_slot(positions, other_places))
        qkv, qkv_y, slot_tokens, cosine, sine = fence(qkv, qkv_y, slot_tokens, cosine, sine)
        qkv = jnp.stack([qkv, qkv_y])
        qkv_x = move.swap(qkv, "ctx")
        qkv, qkv_x, send_cotangent, down, *down_parts = fence(
            qkv, qkv_x, send_cotangent, down, *down_parts
        )
        other_cotangent = move.swap_slots(send_cotangent)
        qkv = jnp.stack([qkv, qkv_x], 1).reshape(2, 2 * levels, half, narrow)
        qkv_w = qkv, move.swap_core(qkv)
        down = jnp.stack([down] + down_parts)
        down_y = move.swap(down, "tp")
    else:
        middle = model_width // 2
        attn_in = jnp.asarray([0, middle, 0], jnp.int32)
        feed_in = attn_in

        def whole(value, axes):
            value = lax.all_gather(value, "fsdp", axis=0, tiled=True)
            if axes:
                value = lax.all_gather(value, "tp", axis=1, tiled=True)
            return value[None]

        sources = [
            whole(output_weight, False),
            whole(gate_weight, True),
            whole(up_weight, True),
            whole(down_turned, True),
        ]
        plan = {
            "sources": 4,
            "chunk": 768,
            "pieces": [
                [(place, 0, 0, 0, 0, 0) + source.shape[1:]] for place, source in enumerate(sources)
            ],
        }
        qkv_all = whole(query_key_value_weight, False)
        qkv_w = qkv_all[None, :, :middle], qkv_all[None, :, middle:]
        norms = lax.all_gather(norms, "fsdp", axis=1, tiled=True)
        other_cotangent = move.swap_slots(sent(cotangent))
        slot_tokens = to_slot(tokens, other_tokens)
        cosine, sine = turn_tables(to_slot(positions, other_places))
    norms = jnp.pad(norms.astype(f32), ((0, 4), (0, 0)))

    queries, key_rows, values, tokens_t = project(attn_in, slot_tokens, cosine, sine, *qkv_w)
    if move.paired:
        queries, down, down_y = fence(queries, down, down_y)
        down = jnp.stack([down, down_y])
        down_x = move.swap(down, "ctx")
    mates = move.ctx // 2
    if mates > 1:
        groups = [[2 * j + s for j in range(mates)] for s in range(2)]

        def gather_rows(value):
            return lax.all_gather(value, "ctx", axis=0, tiled=True, axis_index_groups=groups)

        key_rows = gather_rows(key_rows)
        values = gather_rows(values)
    context, summit = attend(length, queries, key_rows, values)
    if move.paired:
        context, down, down_x, other_cotangent = fence(context, down, down_x, other_cotangent)
        down = jnp.stack([down, down_x], 1).reshape(4 * levels, half, feed_width)
        down = down.reshape((2 * 2 * levels, half, feed_width))
        sources = [packed, down, move.swap_core(down)]
    slot_cotangent = to_slot(cotangent, other_cotangent)
    pieces = (2, 2 * levels, half, feed_width) if move.paired else (1, 1, middle, feed_total)
    feed_out = move.spots(half, 1, feed_width) if move.paired else attn_in
    (
        mixed_keep,
        mixed_send,
        grad_mix_one,
        grad_context,
        attn_o,
        feed_keep,
        feed_send,
    ) = feed_forward(
        plan,
        sources,
        slot_half,
        feed_in,
        feed_out,
        slot_tokens,
        context,
        slot_cotangent,
        norms,
        feed_total,
        pieces,
        4 * 3 * PAIR if move.paired else 0,
    )

    pairs = model_width // PAIR
    if move.paired:
        def back(first, count, grads, waits=(), base=None):
            return attend_back(
                length,
                queries,
                key_rows,
                values,
                context,
                summit,
                grads,
                cosine,
                sine,
                tokens_t,
                first,
                count,
                waits,
                base,
            )

        feed_core = move.swap_core(feed_send)
        other_mixed = move.swap_slots(mixed_send)
        attn_a, raw_0 = back(0, 1, grad_context, (), attn_o)

        raw_0, feed_keep, grad_context = fence(
            raw_0, feed_keep, grad_context, waits=(feed_core,)
        )
        width = feed_width // 2
        shape = (3, 2, 2, levels, half, feed_width)
        feed_keep, feed_core = feed_keep.reshape(shape), feed_core.reshape(shape)

        def joined(job, place):
            return move.add(feed_keep[job][place], feed_core[job][place])

        every = slice(None)
        first, last = (..., slice(0, width)), (..., slice(width, None))
        down_send = joined(0, (every, 1))
        down_x = move.swap(down_send, "ctx")
        gate_send = joined(1, (1,))
        gate_y = move.swap(gate_send, "tp")
        up_a_send = joined(2, (every, 1) + first)
        up_a_x = move.swap(up_a_send, "ctx")
        up_b_send = joined(2, (1,) + last)
        up_b_y = move.swap(up_b_send, "tp")
        down, gate = joined(0, (every, 0)), joined(1, (0,))
        up_a, up_b = joined(2, (every, 0) + first), joined(2, (0,) + last)
        sends = (down_send, gate_send, up_a_send, up_b_send)
        attn_a, raw_1 = back(1, 3, grad_context, (raw_0, *sends), attn_a)

        raw_1, attn_a, grad_context, down, gate = fence(
            raw_1, attn_a, grad_context, down, gate, waits=(down_x, gate_y, other_mixed)
        )
        attn_a = move.sum_shards(attn_a)
        down_send, down = move.add(down[1], down_x[1]), move.add(down[0], down_x[0])
        gate_send, gate = move.add(gate[1], gate_y[1]), move.add(gate[0], gate_y[0])
        down_y = move.swap(down_send, "tp")
        gate_x = move.swap(gate_send, "ctx")
        attn_c, raw_2 = back(4, 2, grad_context, (down_send, gate_send))

        raw_2, attn_c, down, gate, up_a, up_b = fence(
            raw_2, attn_c, down, gate, up_a, up_b, waits=(down_y, gate_x, up_a_x, up_b_y)
        )
        attn_c = move.sum_shards(attn_c)
        up_a_send, up_a = move.add(up_a[1], up_a_x[1]), move.add(up_a[0], up_a_x[0])
        up_b_send, up_b = move.add(up_b[1], up_b_y[1]), move.add(up_b[0], up_b_y[0])
        up_a_y = move.swap(up_a_send, "tp")
        up_b_x = move.swap(up_b_send, "ctx")
        some = jnp.concatenate([move.add(down, down_y), move.add(gate, gate_x)], 2)
        some_shifts = move.level_shifts(some)
        keep_rows, send_rows = token_gradient(
            slot_half,
            attn_in,
            (raw_0, raw_1, raw_2),
            grad_mix_one,
            *qkv_w,
            (up_a_send, up_b_send, some),
        )

        send_rows, up_a, up_b, attn_a, some = fence(
            send_rows, up_a, up_b, attn_a, some[0], waits=(up_a_y, up_b_x)
        )
        attn_x = move.swap(attn_a, "ctx")
        other_rows = move.swap_slots(send_rows)
        up = [
            jnp.concatenate(
                [move.add(up_a[step], up_a_y[step]), move.add(up_b[step], up_b_x[step])], 1
            )
            for step in range(levels)
        ]

        attn_a, some, *up = fence(attn_a, some, *up, waits=(attn_x, *some_shifts))
        up_shifts = move.level_shifts(up)
        some = move.sum_shifts(some, some_shifts)
        attn_a = move.add(attn_a, attn_x)
        attn_y = move.swap(attn_a, "tp")

        up, attn_a, attn_c, some = fence(
            up[0], attn_a, attn_c, some, waits=(attn_y, *up_shifts)
        )
        feed = jnp.concatenate([some, move.sum_shifts(up, up_shifts)], 1)
        feed_x = move.swap(feed, "ctx")
        attn_a = move.add(attn_a, attn_y)
        attn_c = move.sum_all(attn_c)
        low = jnp.where(move.x == 0, feed, feed_x)
        high = jnp.where(move.x == 0, feed_x, feed)
        feed = jnp.concatenate([low, high], 0).astype(f32)
        attn = attn_a
        down_gradient = feed[:, :feed_width].T
        gate_gradient = feed[:, feed_width : 2 * feed_width]
        up_gradient = feed[:, 2 * feed_width :]
        out_gradient = attn[:, :model_width].astype(f32)
        vector_grads = [attn[:, model_width + place].astype(f32) for place in range(4)]
        attn = jnp.concatenate([attn[:, model_width + PAIR :], attn_c], 1)
        qkv_gradient = attn.reshape(shard, pairs, 3, PAIR).transpose(0, 2, 1, 3)
        qkv_gradient = qkv_gradient.reshape(shard, 3 * model_width).astype(f32)
        mixed_out = from_slot(mixed_keep, other_mixed)
        grad_tokens = from_slot(keep_rows, other_rows.astype(f32))
    else:
        mixed_out = from_slot(mixed_keep, move.swap_slots(mixed_send))
        grad_query, grad_keys, grad_values = attend_back_plain(
            length, queries, key_rows, values, context, summit, grad_context
        )
        if mates > 1:

            def scatter_rows(value):
                return lax.psum_scatter(
                    value, "ctx", scatter_dimension=0, axis_index_groups=groups, tiled=True
                )

            grad_keys, grad_values = scatter_rows(grad_keys), scatter_rows(grad_values)

        def turn_back(value):
            value = value.reshape(-1, HEADS, 2, HEAD_DIM // 2)
            ahead, behind = value[:, :, 0], value[:, :, 1]
            cos_half = cosine[:, None, : HEAD_DIM // 2]
            sin_half = sine[:, None, HEAD_DIM // 2 : HEAD_DIM]
            value = jnp.stack(
                [ahead * cos_half + behind * sin_half, behind * cos_half - ahead * sin_half], 2
            )
            return value.reshape(-1, model_width)

        grad_raw = jnp.concatenate(
            [turn_back(grad_query), turn_back(grad_keys), grad_values], 1
        ).astype(bf16)
        total = grad_mix_one + dot(grad_raw, qkv_all[0], NT)
        first = lax.dynamic_slice_in_dim(total, slot * half_rows, half_rows, 0)
        second = lax.dynamic_slice_in_dim(total, (1 - slot) * half_rows, half_rows, 0)
        other_rows = move.swap_slots(second.astype(bf16))
        grad_tokens = from_slot(first, other_rows.astype(f32))
        every = ("ctx", "tp")

        def scatter(value, split):
            value = lax.psum(value, every)
            value = lax.psum_scatter(value, "fsdp", scatter_dimension=0, tiled=True)
            if split:
                value = lax.dynamic_slice_in_dim(value, move.y * feed_width, feed_width, 1)
            return value.astype(f32)

        feed = jnp.concatenate([feed_keep[:, 0, 0], feed_send[:, 0, 0]], 1)
        down_gradient = scatter(feed[0], True).T
        gate_gradient = scatter(feed[1], True)
        up_gradient = scatter(feed[2], True)
        outer = dot(slot_tokens, grad_raw, (((0,), (0,)), ((), ())))
        qkv_gradient = scatter(outer.astype(bf16), False)
        attn_o = scatter(attn_o, False)
        out_gradient = attn_o[:, :model_width]
        vector_grads = [attn_o[:, model_width + place] for place in range(4)]
    return (
        mixed_out,
        grad_tokens,
        qkv_gradient,
        out_gradient,
        gate_gradient,
        up_gradient,
        down_gradient,
        *vector_grads,
    )


def solution(mesh):
    in_specs = (
        P(("fsdp", "tp"), "ctx", None),
        P("fsdp", None),
        P("fsdp", None),
        P("fsdp", "tp"),
        P("fsdp", "tp"),
        P("tp", "fsdp"),
        P("fsdp"),
        P("fsdp"),
        P("fsdp"),
        P("fsdp"),
        P(("fsdp", "tp")),
        P(("fsdp", "tp"), "ctx"),
        P(("fsdp", "tp"), "ctx", None),
    )
    out_specs = (
        P(("fsdp", "tp"), "ctx", None),
        P(("fsdp", "tp"), "ctx", None),
        P("fsdp", None),
        P("fsdp", None),
        P("fsdp", "tp"),
        P("fsdp", "tp"),
        P("tp", "fsdp"),
        P("fsdp"),
        P("fsdp"),
        P("fsdp"),
        P("fsdp"),
    )
    return jax.shard_map(
        functools.partial(on_device, mesh),
        mesh=mesh,
        in_specs=in_specs,
        out_specs=out_specs,
        check_vma=False,
    )
```

```python
import functools

import jax
import jax.numpy as jnp
from jax import lax
from jax.experimental import pallas as pl
from jax.experimental.pallas import tpu as pltpu
from jax.sharding import PartitionSpec as P

HEADS = 12
HEAD_DIM = 64
PAIR = 2 * HEAD_DIM

norm_eps = 1e-05
rope_base = 1000.0
masked_bias = -1000000000.0

bf16 = jnp.bfloat16
f32 = jnp.float32
NN = (((1,), (0,)), ((), ()))
NT = (((1,), (1,)), ((), ()))
ANY = pl.BlockSpec(memory_space=pl.ANY)


def dot(left, right, dims=NN):
    return lax.dot_general(left, right, dims, preferred_element_type=f32)


def params(limit=60):
    return pltpu.CompilerParams(vmem_limit_bytes=limit * 2**20)


def cost(flops, moved, exps=0):
    return pl.CostEstimate(flops=int(flops), bytes_accessed=int(moved), transcendentals=int(exps))


def fence(*values, waits=()):
    def nothing(*refs):
        pass

    return pl.pallas_call(
        nothing,
        in_specs=[ANY] * (len(values) + len(waits)),
        out_specs=[ANY] * len(values),
        out_shape=[jax.ShapeDtypeStruct(value.shape, value.dtype) for value in values],
        input_output_aliases={place: place for place in range(len(values))},
        compiler_params=params(),
        name="fence",
    )(*values, *waits)


def piece_copies(own, other, spots, full, sems):
    col_blocks, row_blocks, rows, width = own.shape
    copies = []
    for side, source in enumerate((own, other)):
        for row in range(row_blocks):
            for col in range(col_blocks):
                start = pl.multiple_of(spots[side * row_blocks + row], 16)
                left = pl.multiple_of(spots[2 * row_blocks + col], 128)
                copies.append(
                    pltpu.make_async_copy(
                        source.at[col, row],
                        full.at[pl.ds(start, rows), pl.ds(left, width)],
                        sems.at[(side * row_blocks + row) * col_blocks + col],
                    )
                )
    return copies


def piece_count(own):
    return 2 * own.shape[0] * own.shape[1]


def turned(block, cosine, sine):
    lane = lax.broadcasted_iota(jnp.int32, block.shape, 1)
    first = (lane % HEAD_DIM) < HEAD_DIM // 2
    partner = jnp.where(
        first, pltpu.roll(block, PAIR - HEAD_DIM // 2, 1), pltpu.roll(block, HEAD_DIM // 2, 1)
    )
    return block * cosine + partner * sine


def turn_tables(places):
    half_dim = HEAD_DIM // 2
    frequency = rope_base ** (-jnp.arange(half_dim, dtype=f32) * 2.0 / HEAD_DIM)
    angles = places.astype(f32)[:, None] * frequency
    cosine = jnp.cos(angles)
    sine = jnp.sin(angles)
    return jnp.concatenate([cosine] * 4, 1), jnp.concatenate([-sine, sine, -sine, sine], 1)


def project_kernel(
    spots, tokens, cosine, sine, own, other, q_out, k_out, v_out, tokens_t, weight, sems
):
    width = q_out.shape[1]

    @pl.when(pl.program_id(0) == 0)
    def _():
        copies = piece_copies(own, other, spots, weight, sems)
        for copy in copies:
            copy.start()
        for copy in copies:
            copy.wait()

    rows = tokens[...]
    tokens_t[...] = rows.T
    cos_part = cosine[...]
    sin_part = sine[...]
    for part, out in enumerate((q_out, k_out, v_out)):
        raw = dot(rows, weight[:, part * width : (part + 1) * width])
        for pair in range(width // PAIR):
            cols = slice(pair * PAIR, (pair + 1) * PAIR)
            block = raw[:, cols]
            if part < 2:
                block = turned(block, cos_part, sin_part)
            block = block.astype(bf16)
            if part == 0:
                block = block * jnp.asarray(HEAD_DIM**-0.5, bf16)
            out[:, cols] = block


def project(spots, tokens, cosine, sine, own, other, block=256):
    rows, width = tokens.shape
    total = own.shape[0] * own.shape[3]
    row_spec = pl.BlockSpec((block, width), lambda i, *_: (i, 0))
    table = pl.BlockSpec((block, PAIR), lambda i, *_: (i, 0))
    part = total // 3
    out_spec = pl.BlockSpec((block, part), lambda i, *_: (i, 0))
    return pl.pallas_call(
        project_kernel,
        grid_spec=pltpu.PrefetchScalarGridSpec(
            num_scalar_prefetch=1,
            grid=(rows // block,),
            in_specs=[row_spec, table, table, ANY, ANY],
            out_specs=[out_spec] * 3 + [pl.BlockSpec((width, block), lambda i, *_: (0, i))],
            scratch_shapes=[
                pltpu.VMEM((width, total), bf16),
                pltpu.SemaphoreType.DMA((piece_count(own),)),
            ],
        ),
        out_shape=[jax.ShapeDtypeStruct((rows, part), bf16)] * 3
        + [jax.ShapeDtypeStruct((width, rows), bf16)],
        compiler_params=params(),
        cost_estimate=cost(2 * rows * width * total, 4 * rows * total + 2 * width * total),
        name="project",
    )(spots, tokens, cosine, sine, own, other)


def lane_ids(shape):
    return lax.broadcasted_iota(jnp.int32, shape, 1)


def key_bias(length, shape):
    return jnp.where(lax.broadcasted_iota(jnp.int32, shape, 0) < length, 0.0, masked_bias).astype(
        bf16
    )


def attend_kernel(length, q_ref, k_ref, v_ref, out_ref, summit_ref):
    lane_q = lane_ids(q_ref.shape)
    lane_k = lane_ids(k_ref.shape)
    bias = key_bias(length[0], k_ref.shape)
    queries = q_ref[...]
    keys = k_ref[...]
    values = v_ref[...]
    one = jnp.ones((), bf16)
    zero = jnp.zeros((), bf16)
    outs = []
    summits = []
    for head in range(2):
        mine_q = (lane_q < HEAD_DIM) if head == 0 else (lane_q >= HEAD_DIM)
        mine_k = (lane_k < HEAD_DIM) if head == 0 else (lane_k >= HEAD_DIM)
        spare = HEAD_DIM * (1 - head)
        query = jnp.where(mine_q, queries, jnp.where(lane_q == spare, one, zero))
        key = jnp.where(mine_k, keys, bias)
        value = jnp.where(mine_k, values, one)
        scores = dot(query, key, NT)
        top = jnp.max(scores, axis=1, keepdims=True)
        summed = dot(jnp.exp(scores - top).astype(bf16), value)
        totals = pltpu.roll(summed, HEAD_DIM, 1)
        outs.append(summed / totals)
        summits.append(top + jnp.log(summed))
    low = lane_q < HEAD_DIM
    out_ref[...] = jnp.where(low, outs[0], outs[1]).astype(bf16)
    summit_ref[0] = jnp.where(low, summits[1], summits[0])


def attend(length, queries, keys, values):
    rows, width = queries.shape
    seq = keys.shape[0]
    pairs = width // PAIR
    q_spec = pl.BlockSpec((rows, PAIR), lambda h, *_: (0, h))
    k_spec = pl.BlockSpec((seq, PAIR), lambda h, *_: (0, h))
    return pl.pallas_call(
        attend_kernel,
        grid_spec=pltpu.PrefetchScalarGridSpec(
            num_scalar_prefetch=1,
            grid=(pairs,),
            in_specs=[q_spec, k_spec, k_spec],
            out_specs=[q_spec, pl.BlockSpec((1, rows, PAIR), lambda h, *_: (h, 0, 0))],
        ),
        out_shape=[
            jax.ShapeDtypeStruct((rows, width), bf16),
            jax.ShapeDtypeStruct((pairs, rows, PAIR), f32),
        ],
        compiler_params=params(),
        cost_estimate=cost(16 * rows * seq * width, 12 * rows * width),
        name="attend",
    )(length, queries, keys, values)


def three_parts(value):
    high = value.astype(bf16)
    rest = value - high.astype(f32)
    middle = rest.astype(bf16)
    return high, middle, (rest - middle.astype(f32)).astype(bf16)


def pair_back(length, q_ref, k_ref, v_ref, out_ref, summit_ref, grad_ref):
    rows = q_ref.shape[0]
    lane_q = lane_ids(q_ref.shape)
    lane_k = lane_ids(k_ref.shape)
    bias = key_bias(length[0], k_ref.shape)
    queries = q_ref[...]
    keys = k_ref[...]
    values = v_ref[...]
    grads = grad_ref[...]
    summit = three_parts(summit_ref[0])
    product = grads.astype(f32) * out_ref[...].astype(f32)
    one = jnp.ones((), bf16)
    zero = jnp.zeros((), bf16)
    grads_t = grads.T
    queries_t = queries.T
    dq, dk, dv = [], [], []
    for head in range(2):
        mine_q = (lane_q < HEAD_DIM) if head == 0 else (lane_q >= HEAD_DIM)
        mine_k = (lane_k < HEAD_DIM) if head == 0 else (lane_k >= HEAD_DIM)
        spare = HEAD_DIM * (1 - head)
        own = slice(HEAD_DIM * head, HEAD_DIM * (head + 1))
        row_dot = jnp.sum(jnp.where(mine_q, product, 0.0), axis=1, keepdims=True)
        row_dot = three_parts(jnp.broadcast_to(row_dot, (rows, PAIR)))

        def beside(main, mine, lane, parts, last):
            extra = jnp.where(lane == spare + 3, last, zero)
            for place in range(3):
                extra = jnp.where(lane == spare + place, parts[place], extra)
            return jnp.where(mine, main, extra)

        minus = (-one, -one, -one)
        query = beside(queries, mine_q, lane_q, summit, one)
        key = beside(keys, mine_k, lane_k, minus, bias)
        grad = beside(grads, mine_q, lane_q, row_dot, zero)
        value = beside(values, mine_k, lane_k, minus, zero)
        probs = jnp.exp(dot(query, key, NT))
        grad_scores = (probs * dot(grad, value, NT)).astype(bf16)
        dv.append(dot(grads_t[own], probs.astype(bf16)))
        dk.append(dot(queries_t[own], grad_scores))
        dq.append(dot(grad_scores, keys))
    grad_query = jnp.where(lane_q < HEAD_DIM, dq[0], dq[1]) * HEAD_DIM**-0.5
    return grad_query, jnp.concatenate(dk, 0).T, jnp.concatenate(dv, 0).T


def attend_back_kernel(
    waits,
    length,
    first,
    q_ref,
    k_ref,
    v_ref,
    out_ref,
    summit_ref,
    grad_ref,
    cos_ref,
    sin_ref,
    tokens_t,
    *refs,
):
    outer_ref, raw_ref = refs[-2:]
    grad_query, grad_keys, grad_values = pair_back(
        length, q_ref, k_ref, v_ref, out_ref, summit_ref, grad_ref
    )
    cosine = cos_ref[...]
    sine = sin_ref[...]
    raw = jnp.concatenate(
        [
            turned(grad_query, cosine, -sine).astype(bf16),
            turned(grad_keys, cosine, -sine).astype(bf16),
            grad_values.astype(bf16),
        ],
        1,
    )
    outer_ref[...] = dot(tokens_t[...], raw).astype(bf16)
    raw_ref[...] = raw


def attend_back(
    length,
    queries,
    keys,
    values,
    out,
    summit,
    grads,
    cosine,
    sine,
    tokens_t,
    first,
    pairs,
    waits=(),
    base=None,
):
    rows, width = queries.shape
    q_spec = pl.BlockSpec((rows, PAIR), lambda h, length, first: (0, h + first[0]))
    table = pl.BlockSpec((rows, PAIR), lambda h, *_: (0, 0))
    columns = 3 * PAIR
    if base is None:
        extra, shape, aliases = list(waits), (width, columns * pairs), {}
        outer_spec = pl.BlockSpec((width, columns), lambda h, *_: (0, h))
    else:
        extra, shape = [base] + list(waits), base.shape
        aliases = {11: 0}
        outer_spec = pl.BlockSpec(
            (pl.Element(width), pl.Element(columns)),
            lambda h, length, first: (
                0,
                pl.multiple_of(width + PAIR + (first[0] + h) * columns, PAIR),
            ),
        )
    return pl.pallas_call(
        functools.partial(attend_back_kernel, len(waits)),
        grid_spec=pltpu.PrefetchScalarGridSpec(
            num_scalar_prefetch=2,
            grid=(pairs,),
            in_specs=[
                q_spec,
                q_spec,
                q_spec,
                q_spec,
                pl.BlockSpec((1, rows, PAIR), lambda h, length, first: (h + first[0], 0, 0)),
                q_spec,
                table,
                table,
                pl.BlockSpec(tokens_t.shape, lambda h, *_: (0, 0)),
            ]
            + [ANY] * len(extra),
            out_specs=[
                outer_spec,
                pl.BlockSpec((rows, columns), lambda h, *_: (0, h)),
            ],
        ),
        out_shape=[
            jax.ShapeDtypeStruct(shape, bf16),
            jax.ShapeDtypeStruct((rows, columns * pairs), bf16),
        ],
        input_output_aliases=aliases,
        compiler_params=params(),
        cost_estimate=cost(46 * rows * rows * PAIR * pairs, 16 * rows * PAIR * pairs),
        name="attend_back",
    )(
        length,
        jnp.full((1,), first, jnp.int32),
        queries,
        keys,
        values,
        out,
        summit,
        grads,
        cosine,
        sine,
        tokens_t,
        *extra,
    )


def token_kernel(count, slot_half, spots, *refs):
    raws = refs[:count]
    total_ref, own, other = refs[count : count + 3]
    keep, send, weight, sems = refs[-4:]
    width = total_ref.shape[1]
    step = pl.program_id(0)

    @pl.when(step == 0)
    def _():
        copies = piece_copies(own, other, spots, weight, sems)
        for copy in copies:
            copy.start()
        for copy in copies:
            copy.wait()

    order = [part * width + pair * PAIR for pair in range(width // PAIR) for part in range(3)]
    used = jnp.concatenate([weight[:, left : left + PAIR] for left in order], 1)
    total = total_ref[...]
    left = 0
    for raw in raws:
        size = raw.shape[1]
        total = total + dot(raw[...], used[:, left : left + size], NT)
        left += size

    @pl.when(step < pl.num_programs(0) // 2)
    def _():
        send[...] = total.astype(bf16)

    @pl.when(step >= pl.num_programs(0) // 2)
    def _():
        keep[...] = total


def token_gradient(slot_half, spots, raws, total, own, other, waits=(), block=256):
    rows, width = total.shape
    halves = rows // 2 // block

    def source(i, s):
        return (i + (1 - s[0]) * halves) % (2 * halves)

    def rows_of(value):
        return pl.BlockSpec((block, value.shape[1]), lambda i, s, *_: (source(i, s), 0))

    return pl.pallas_call(
        functools.partial(token_kernel, len(raws)),
        grid_spec=pltpu.PrefetchScalarGridSpec(
            num_scalar_prefetch=2,
            grid=(2 * halves,),
            in_specs=[rows_of(raw) for raw in raws]
            + [rows_of(total), ANY, ANY]
            + [ANY] * len(waits),
            out_specs=[
                pl.BlockSpec((block, width), lambda i, *_: (jnp.maximum(i - halves, 0), 0)),
                pl.BlockSpec((block, width), lambda i, *_: (jnp.minimum(i, halves - 1), 0)),
            ],
            scratch_shapes=[
                pltpu.VMEM((width, 3 * width), bf16),
                pltpu.SemaphoreType.DMA((piece_count(own),)),
            ],
        ),
        out_shape=[
            jax.ShapeDtypeStruct((rows // 2, width), f32),
            jax.ShapeDtypeStruct((rows // 2, width), bf16),
        ],
        compiler_params=params(),
        cost_estimate=cost(6 * rows * width * width, 14 * rows * width + 6 * width * width),
        name="token_gradient",
    )(slot_half, spots, *raws, total, own, other, *waits)


def attend_back_plain_kernel(
    length, q_ref, k_ref, v_ref, out_ref, summit_ref, grad_ref, dq_ref, dk_ref, dv_ref
):
    dq_ref[...], dk_ref[...], dv_ref[...] = pair_back(
        length, q_ref, k_ref, v_ref, out_ref, summit_ref, grad_ref
    )


def attend_back_plain(length, queries, keys, values, out, summit, grads):
    rows, width = queries.shape
    seq = keys.shape[0]
    q_spec = pl.BlockSpec((rows, PAIR), lambda h, *_: (0, h))
    k_spec = pl.BlockSpec((seq, PAIR), lambda h, *_: (0, h))
    return pl.pallas_call(
        attend_back_plain_kernel,
        grid_spec=pltpu.PrefetchScalarGridSpec(
            num_scalar_prefetch=1,
            grid=(width // PAIR,),
            in_specs=[
                q_spec,
                k_spec,
                k_spec,
                q_spec,
                pl.BlockSpec((1, rows, PAIR), lambda h, *_: (h, 0, 0)),
                q_spec,
            ],
            out_specs=[q_spec, k_spec, k_spec],
        ),
        out_shape=[jax.ShapeDtypeStruct((count, width), f32) for count in (rows, seq, seq)],
        compiler_params=params(),
        cost_estimate=cost(40 * rows * seq * width, 16 * rows * width),
        name="attend_back_plain",
    )(length, queries, keys, values, out, summit, grads)


def row_mean(value):
    return jnp.mean(value, axis=-1, keepdims=True)


def normalize(value):
    centered = value - row_mean(value)
    inverse = lax.rsqrt(row_mean(centered * centered) + norm_eps)
    return centered * inverse, inverse


def normalize_back(normed, inverse, gain, upstream):
    scaled = upstream * gain
    return inverse * (scaled - row_mean(scaled) - normed * row_mean(scaled * normed))


def weight_copies(plan, group, sources, weight, spots, sems, chunk):
    copies = [[] for _ in range(weight.shape[1] // chunk)]
    count = 0
    for source, first, top, left, row, col, rows, cols in plan["pieces"][group]:
        dynamic = isinstance(row, tuple)
        if dynamic:
            row = pl.multiple_of(spots[row[0]], 16)
            col = pl.multiple_of(spots[col[0]], 128)
        width = cols if dynamic else min(cols, chunk)
        for inside in range(0, cols, width):
            copy = pltpu.make_async_copy(
                sources[source].at[first, pl.ds(top, rows), pl.ds(left + inside, width)],
                weight.at[pl.ds(row, rows), pl.ds(col + inside, width)],
                sems.at[group, count],
            )
            copies[0 if dynamic else (col + inside) // chunk].append(copy)
            count += 1
    return copies


def weight_copy_count(plan):
    counts = []
    for pieces in plan["pieces"]:
        counts.append(
            sum(
                1 if isinstance(row, tuple) else -(-cols // plan["chunk"])
                for _, _, _, _, row, _, _, cols in pieces
            )
        )
    return max(counts)


def feed_kernel(plan, slot_half, spots_in, spots_out, tokens, context, cotangent, norms, *refs):
    sources = refs[: plan["sources"]]
    (
        mixed_keep,
        mixed_send,
        grad_mix_one,
        grad_context,
        out_ref,
        keep,
        send,
        w_out,
        w_gate,
        w_up,
        w_down,
        slopes,
        known,
        lefts,
        context_t,
        attn_rows,
        vectors,
        stage,
        out_stage,
        sems,
        out_sems,
        out_sem,
    ) = refs[plan["sources"] :]
    chunk = plan["chunk"]
    rows, width = tokens.shape
    steps = known.shape[1] // rows
    step = pl.program_id(0)
    feed_total = w_gate.shape[1]
    chunks = feed_total // chunk
    weights = (w_out, w_gate, w_up, w_down)
    loads = [
        weight_copies(plan, group, sources, weight, spots_in, sems, min(chunk, weight.shape[1]))
        for group, weight in enumerate(weights)
    ]

    @pl.when(step == 0)
    def _():
        order = [loads[0][0]]
        for place in range(chunks):
            order += [loads[1][place], loads[2][place], loads[3][place]]
        for group in order:
            for copy in group:
                copy.start()
        vectors[...] = jnp.zeros_like(vectors)

    def arrive(*groups):
        @pl.when(step == 0)
        def _():
            for group in groups:
                for copy in group:
                    copy.wait()

    @pl.when(step < steps)
    def _():
        here = pl.ds(pl.multiple_of(step * rows, rows), rows)
        gain_one = norms[0:1, :]
        shift_one = norms[1:2, :]
        gain_two = norms[2:3, :]
        shift_two = norms[3:4, :]
        arrive(loads[0][0])
        context_rows = context[...]
        context_t[:, here] = context_rows.T
        normed_one, inverse_one = normalize(
            tokens[...].astype(f32) + dot(context_rows, w_out[...])
        )
        out_one = normed_one * gain_one + shift_one
        feed_in = out_one.astype(bf16)
        lefts[1, :, here] = feed_in.T
        total = out_one
        for place in range(chunks):
            cols = slice(place * chunk, (place + 1) * chunk)
            arrive(loads[1][place], loads[2][place], loads[3][place])
            gate = dot(feed_in, w_gate[:, cols])
            up = dot(feed_in, w_up[:, cols])
            sig = jax.nn.sigmoid(gate)
            swish = gate * sig
            hid = (swish * up).astype(bf16)
            known[0, here, cols] = hid
            slopes[0, :, cols] = swish.astype(bf16)
            slopes[1, :, cols] = (up * (sig + swish * (1.0 - sig))).astype(bf16)
            total = total + dot(hid, w_down[:, cols], NT)
        normed_two, inverse_two = normalize(total)
        mixed = (normed_two * gain_two + shift_two).astype(bf16)

        @pl.when(step < steps // 2)
        def _():
            mixed_send[...] = mixed

        @pl.when(step >= steps // 2)
        def _():
            mixed_keep[...] = mixed

        upstream = cotangent[...].astype(f32)
        grad_mix_two = normalize_back(normed_two, inverse_two, gain_two, upstream)
        branch = grad_mix_two.astype(bf16)
        lefts[0, :, here] = branch.T
        grad_out_one = grad_mix_two
        for place in range(chunks):
            cols = slice(place * chunk, (place + 1) * chunk)
            grad_hidden = dot(branch, w_down[:, cols])
            grad_gate = (grad_hidden * slopes[1, :, cols].astype(f32)).astype(bf16)
            grad_up = (grad_hidden * slopes[0, :, cols].astype(f32)).astype(bf16)
            known[1, here, cols] = grad_gate
            known[2, here, cols] = grad_up
            grad_out_one = (
                grad_out_one
                + dot(grad_gate, w_gate[:, cols], NT)
                + dot(grad_up, w_up[:, cols], NT)
            )
        vectors[0:1, :] += jnp.sum(grad_out_one * normed_one, axis=0, keepdims=True)
        vectors[1:2, :] += jnp.sum(grad_out_one, axis=0, keepdims=True)
        vectors[2:3, :] += jnp.sum(upstream * normed_two, axis=0, keepdims=True)
        vectors[3:4, :] += jnp.sum(upstream, axis=0, keepdims=True)
        grad_one = normalize_back(normed_one, inverse_one, gain_one, grad_out_one)
        grad_mix_one[...] = grad_one
        grad_rows = grad_one.astype(bf16)
        attn_rows[here, :] = grad_rows
        grad_context[...] = dot(grad_rows, w_out[...], NT).astype(bf16)

    _, col_blocks, row_blocks, piece_rows, _ = keep.shape
    per = chunks // col_blocks

    def piece_moves(place):
        job, inside = place // chunks, place % chunks
        col, left = inside // per, inside % per * chunk
        slot = place % 2
        moves = []
        for side, out in enumerate((keep, send)):
            for row in range(row_blocks):
                start = pl.multiple_of(spots_out[side * row_blocks + row], 16)
                moves.append(
                    pltpu.make_async_copy(
                        stage.at[slot, pl.ds(start, piece_rows), :],
                        out.at[job, col, row, :, pl.ds(pl.multiple_of(left, 128), chunk)],
                        out_sems.at[slot, side * row_blocks + row],
                    )
                )
        return moves

    @pl.when(step >= steps)
    def _():
        place = step - steps

        @pl.when(place >= 2)
        def _():
            for move in piece_moves(place - 2):
                move.wait()

        job, inside = place // chunks, place % chunks
        start = spots_out[2 * row_blocks + inside // per] + inside % per * chunk
        cols = pl.ds(pl.multiple_of(start, 128), chunk)
        left_t = lefts[jnp.minimum(job, 1)]
        stage[place % 2] = dot(left_t, known[job, :, cols]).astype(bf16)
        for move in piece_moves(place):
            move.start()

    @pl.when(step == pl.num_programs(0) - 1)
    def _():
        out_stage[:, :width] = dot(context_t[...], attn_rows[...]).astype(bf16)
        out_stage[:, width:] = vectors[...].astype(bf16).T
        move = pltpu.make_async_copy(out_stage, out_ref.at[:, pl.ds(0, width + PAIR)], out_sem)
        move.start()
        move.wait()
        for place in (3 * chunks - 2, 3 * chunks - 1):
            for move in piece_moves(place):
                move.wait()


def feed_forward(
    plan,
    sources,
    slot_half,
    spots_in,
    spots_out,
    tokens,
    context,
    cotangent,
    norms,
    feed_total,
    pieces,
    more,
    block=256,
):
    rows, width = tokens.shape
    half = rows // 2
    halves = half // block
    chunk = plan["chunk"]
    chunks = 3 * feed_total // chunk

    def source(i, s):
        return (jnp.minimum(i, 2 * halves - 1) + (1 - s[0]) * halves) % (2 * halves)

    row_spec = pl.BlockSpec((block, width), lambda i, s, *_: (source(i, s), 0))
    keep_spec = pl.BlockSpec((block, width), lambda i, *_: (jnp.clip(i - halves, 0, halves - 1), 0))
    send_spec = pl.BlockSpec((block, width), lambda i, *_: (jnp.minimum(i, halves - 1), 0))
    whole = pl.BlockSpec((8, width), lambda i, *_: (0, 0))
    return pl.pallas_call(
        functools.partial(feed_kernel, plan),
        grid_spec=pltpu.PrefetchScalarGridSpec(
            num_scalar_prefetch=3,
            grid=(rows // block + chunks,),
            in_specs=[row_spec, row_spec, row_spec, whole] + [ANY] * len(sources),
            out_specs=[
                keep_spec,
                send_spec,
                row_spec,
                row_spec,
                ANY,
            ]
            + [ANY] * 2,
            scratch_shapes=[pltpu.VMEM((width, width), bf16)]
            + [pltpu.VMEM((width, feed_total), bf16)] * 3
            + [
                pltpu.VMEM((2, block, feed_total), bf16),
                pltpu.VMEM((3, rows, feed_total), bf16),
                pltpu.VMEM((2, width, rows), bf16),
                pltpu.VMEM((width, rows), bf16),
                pltpu.VMEM((rows, width), bf16),
                pltpu.VMEM((PAIR, width), f32),
                pltpu.VMEM((2, width, chunk), bf16),
                pltpu.VMEM((width, width + PAIR), bf16),
                pltpu.SemaphoreType.DMA((4, weight_copy_count(plan))),
                pltpu.SemaphoreType.DMA((2, 2 * pieces[1])),
                pltpu.SemaphoreType.DMA,
            ],
        ),
        out_shape=[
            jax.ShapeDtypeStruct((half, width), bf16),
            jax.ShapeDtypeStruct((half, width), bf16),
            jax.ShapeDtypeStruct((rows, width), f32),
            jax.ShapeDtypeStruct((rows, width), bf16),
            jax.ShapeDtypeStruct((width, width + PAIR + more), bf16),
        ]
        + [jax.ShapeDtypeStruct((3,) + pieces, bf16)] * 2,
        compiler_params=pltpu.CompilerParams(vmem_limit_bytes=62 * 2**20),
        cost_estimate=cost(
            2 * rows * width * (9 * feed_total + 3 * width),
            rows * 24 * width + 12 * width * feed_total,
        ),
        name="feed_forward",
    )(slot_half, spots_in, spots_out, tokens, context, cotangent, norms, *sources)


class Transfers:
    def __init__(self, mesh):
        self.fsdp = mesh.shape["fsdp"]
        self.ctx = mesh.shape["ctx"]
        self.tp = mesh.shape["tp"]
        self.levels = self.fsdp // 2
        place = lax.axis_index("fsdp")
        self.z = place // 2
        self.core = place % 2
        self.x = lax.axis_index("ctx")
        self.y = lax.axis_index("tp")
        self.paired = self.ctx == 2 and self.tp == 2 and self.fsdp % 2 == 0

    def swap_slots(self, value):
        return lax.ppermute(value, "ctx", [(i, i ^ 1) for i in range(self.ctx)])

    def swap(self, value, axis):
        return lax.ppermute(value, axis, [(0, 1), (1, 0)])

    def swap_core(self, value):
        return lax.ppermute(value, "fsdp", [(i, i ^ 1) for i in range(self.fsdp)])

    def shift(self, value, step):
        pairs = [
            (2 * level + core, 2 * ((level + step) % self.levels) + core)
            for level in range(self.levels)
            for core in range(2)
        ]
        return lax.ppermute(value, "fsdp", pairs)

    def spots(self, rows, sign, width=None):
        found = []
        for side in range(2):
            for part in range(2):
                for step in range(self.levels):
                    level = (self.z + sign * step + self.levels) % self.levels
                    block = 2 * level + jnp.bitwise_xor(self.core, side)
                    found.append(2 * rows * block + rows * jnp.bitwise_xor(self.x, part))
        if width is None:
            found = found + [jnp.zeros((), jnp.int32)]
        else:
            found = found + [self.y * width, (1 - self.y) * width]
        return jnp.stack(found).astype(jnp.int32)

    def mine(self, shard):
        half = shard.shape[0] // 2
        return lax.dynamic_slice_in_dim(shard, self.x * half, half, 0)

    def shifts(self, block):
        return [self.shift(block, step) for step in range(1, self.levels)]

    def gather_feed(self, gate, up, out, norms):
        rows, width = gate.shape
        model = out.shape[1]
        share = rows // self.tp
        block = lax.dynamic_slice_in_dim(out, self.y * share, share, 0)
        tail = jnp.concatenate([block[16 * j : 16 * (j + 1)] for j in range(share // 16)], 1)
        norm_tail = jnp.pad(norms, ((0, 16 - norms.shape[0]), (0, 2 * width - tail.shape[1] - rows)))
        packed = jnp.concatenate(
            [jnp.concatenate([gate, up], 1), jnp.concatenate([tail, norm_tail], 1)], 0
        )
        packed = lax.all_gather(packed, ("fsdp", "tp"), axis=0)
        pieces = [[], [], [], []]
        for place in range(self.fsdp * self.tp):
            row, col = rows * (place // self.tp), width * (place % self.tp)
            for group in range(2):
                pieces[1 + group].append((0, place, 0, group * width, row, col, rows, width))
            for j in range(share // 16):
                row = rows * (place // self.tp) + share * (place % self.tp) + 16 * j
                pieces[0].append((0, place, rows, model * j, row, 0, 16, model))
        blocks = 2 * self.levels
        for side in range(2):
            for col in range(2):
                for row in range(blocks):
                    pieces[3].append(
                        (
                            1 + side,
                            col * blocks + row,
                            0,
                            0,
                            (side * blocks + row,),
                            (2 * blocks + col,),
                            rows // 2,
                            width,
                        )
                    )
        left = model * (share // 16)
        norms = packed[:: self.tp, rows : rows + norms.shape[0], left : left + rows]
        norms = norms.transpose(1, 0, 2).reshape(norms.shape[1], -1)
        return {"sources": 3, "pieces": pieces, "chunk": 768}, packed, norms

    def add(self, left, right):
        return (left.astype(f32) + right.astype(f32)).astype(bf16)

    def level_shifts(self, value):
        return [self.shift(value[step], step) for step in range(1, self.levels)]

    def sum_shifts(self, value, shifts):
        total = value.astype(f32)
        for other in shifts:
            total = total + other.astype(f32)
        return total.astype(bf16)

    def sum_shards(self, value):
        return lax.psum_scatter(value, "fsdp", scatter_dimension=0, tiled=True)

    def sum_all(self, value):
        corners = [(i, i ^ 3) for i in range(4)]
        over_y = self.swap(value, "tp")
        over_x = self.swap(value, "ctx")
        across = lax.ppermute(value, ("ctx", "tp"), corners)
        here = value.astype(f32) + over_y.astype(f32)
        there = over_x.astype(f32) + across.astype(f32)
        return (here + there).astype(bf16)

    def both(self, value, axis, index):
        other = self.swap(value, axis)
        return jnp.where(index == 0, value, other), jnp.where(index == 0, other, value)


def on_device(
    mesh,
    tokens,
    query_key_value_weight,
    output_weight,
    gate_weight,
    up_weight,
    down_weight,
    gain_one,
    shift_one,
    gain_two,
    shift_two,
    lengths,
    positions,
    cotangent,
):
    move = Transfers(mesh)
    shard, model_width = query_key_value_weight.shape[0], tokens.shape[2]
    feed_width = gate_weight.shape[1]
    slot = move.x % 2
    half_rows = tokens.shape[1]

    def sent(value):
        return lax.dynamic_index_in_dim(value, 1 - slot, 0, keepdims=False)

    def to_slot(value, other):
        keep = lax.dynamic_index_in_dim(value, slot, 0, keepdims=False)
        first = jnp.where(slot == 0, keep, other)
        second = jnp.where(slot == 0, other, keep)
        return jnp.concatenate([first, second], 0)

    def from_slot(keep, other):
        return jnp.where(slot == 0, jnp.stack([keep, other]), jnp.stack([other, keep]))

    other_places = move.swap_slots(sent(positions))
    other_tokens = move.swap_slots(sent(tokens))
    length = jnp.where(slot == 0, lengths[0:1], lengths[1:2])
    slot_half = slot[None].astype(jnp.int32)
    norms = jnp.stack([gain_one, shift_one, gain_two, shift_two])
    feed_total = feed_width * move.tp
    down_turned = down_weight.T
    half = shard // 2
    if move.paired:
        levels = move.levels
        blocks = (2, 2 * levels, half)
        narrow = query_key_value_weight.shape[1] // 2
        attn_in = move.spots(half, -1, narrow)
        feed_in = move.spots(half, -1, feed_width)
        plan, packed, norms = move.gather_feed(gate_weight, up_weight, output_weight, norms)
        qkv = lax.dynamic_slice_in_dim(
            move.mine(query_key_value_weight), move.y * narrow, narrow, 1
        )
        down, qkv, send_cotangent, *parts = fence(
            move.mine(down_turned), qkv, sent(cotangent), *move.shifts(qkv)
        )
        qkv = jnp.stack([qkv] + parts)
        qkv_y = move.swap(qkv, "tp")
        down_parts = move.shifts(down)
        slot_tokens = to_slot(tokens, other_tokens)
        cosine, sine = turn_tables(to_slot(positions, other_places))
        qkv, qkv_y, slot_tokens, cosine, sine = fence(qkv, qkv_y, slot_tokens, cosine, sine)
        qkv = jnp.stack([qkv, qkv_y])
        qkv_x = move.swap(qkv, "ctx")
        qkv, qkv_x, send_cotangent, down, *down_parts = fence(
            qkv, qkv_x, send_cotangent, down, *down_parts
        )
        other_cotangent = move.swap_slots(send_cotangent)
        qkv = jnp.stack([qkv, qkv_x], 1).reshape(2, 2 * levels, half, narrow)
        qkv_w = qkv, move.swap_core(qkv)
        down = jnp.stack([down] + down_parts)
        down_y = move.swap(down, "tp")
    else:
        middle = model_width // 2
        attn_in = jnp.asarray([0, middle, 0], jnp.int32)
        feed_in = attn_in

        def whole(value, axes):
            value = lax.all_gather(value, "fsdp", axis=0, tiled=True)
            if axes:
                value = lax.all_gather(value, "tp", axis=1, tiled=True)
            return value[None]

        sources = [
            whole(output_weight, False),
            whole(gate_weight, True),
            whole(up_weight, True),
            whole(down_turned, True),
        ]
        plan = {
            "sources": 4,
            "chunk": 768,
            "pieces": [
                [(place, 0, 0, 0, 0, 0) + source.shape[1:]] for place, source in enumerate(sources)
            ],
        }
        qkv_all = whole(query_key_value_weight, False)
        qkv_w = qkv_all[None, :, :middle], qkv_all[None, :, middle:]
        norms = lax.all_gather(norms, "fsdp", axis=1, tiled=True)
        other_cotangent = move.swap_slots(sent(cotangent))
        slot_tokens = to_slot(tokens, other_tokens)
        cosine, sine = turn_tables(to_slot(positions, other_places))
    norms = jnp.pad(norms.astype(f32), ((0, 4), (0, 0)))

    queries, key_rows, values, tokens_t = project(attn_in, slot_tokens, cosine, sine, *qkv_w)
    if move.paired:
        queries, down, down_y = fence(queries, down, down_y)
        down = jnp.stack([down, down_y])
        down_x = move.swap(down, "ctx")
    mates = move.ctx // 2
    if mates > 1:
        groups = [[2 * j + s for j in range(mates)] for s in range(2)]

        def gather_rows(value):
            return lax.all_gather(value, "ctx", axis=0, tiled=True, axis_index_groups=groups)

        key_rows = gather_rows(key_rows)
        values = gather_rows(values)
    context, summit = attend(length, queries, key_rows, values)
    if move.paired:
        context, down, down_x, other_cotangent = fence(context, down, down_x, other_cotangent)
        down = jnp.stack([down, down_x], 1).reshape(4 * levels, half, feed_width)
        down = down.reshape((2 * 2 * levels, half, feed_width))
        sources = [packed, down, move.swap_core(down)]
    slot_cotangent = to_slot(cotangent, other_cotangent)
    pieces = (2, 2 * levels, half, feed_width) if move.paired else (1, 1, middle, feed_total)
    feed_out = move.spots(half, 1, feed_width) if move.paired else attn_in
    (
        mixed_keep,
        mixed_send,
        grad_mix_one,
        grad_context,
        attn_o,
        feed_keep,
        feed_send,
    ) = feed_forward(
        plan,
        sources,
        slot_half,
        feed_in,
        feed_out,
        slot_tokens,
        context,
        slot_cotangent,
        norms,
        feed_total,
        pieces,
        4 * 3 * PAIR if move.paired else 0,
    )

    pairs = model_width // PAIR
    if move.paired:
        def back(first, count, grads, waits=(), base=None):
            return attend_back(
                length,
                queries,
                key_rows,
                values,
                context,
                summit,
                grads,
                cosine,
                sine,
                tokens_t,
                first,
                count,
                waits,
                base,
            )

        feed_core = move.swap_core(feed_send)
        other_mixed = move.swap_slots(mixed_send)
        attn_a, raw_0 = back(0, 1, grad_context, (), attn_o)

        raw_0, feed_keep, grad_context = fence(
            raw_0, feed_keep, grad_context, waits=(feed_core,)
        )
        width = feed_width // 2
        shape = (3, 2, 2, levels, half, feed_width)
        feed_keep, feed_core = feed_keep.reshape(shape), feed_core.reshape(shape)

        def joined(job, place):
            return move.add(feed_keep[job][place], feed_core[job][place])

        def joined_with(job, place, other):
            total = feed_keep[job][place].astype(f32) + feed_core[job][place].astype(f32)
            return (total + other.astype(f32)).astype(bf16)

        every = slice(None)
        first, last = (..., slice(0, width)), (..., slice(width, None))
        down_send = joined(0, (every, 1))
        down_x = move.swap(down_send, "ctx")
        gate_send = joined(1, (1,))
        gate_y = move.swap(gate_send, "tp")
        up_a_send = joined(2, (every, 1) + first)
        up_a_x = move.swap(up_a_send, "ctx")
        up_b_send = joined(2, (1,) + last)
        up_b_y = move.swap(up_b_send, "tp")
        sends = (down_send, gate_send, up_a_send, up_b_send)
        attn_a, raw_1 = back(1, 3, grad_context, (raw_0, *sends), attn_a)

        raw_1, attn_a, grad_context, feed_keep = fence(
            raw_1, attn_a, grad_context, feed_keep, waits=(down_x, gate_y, other_mixed)
        )
        attn_a = move.sum_shards(attn_a)
        down_send = joined_with(0, (1, 0), down_x[1])
        gate_send = joined_with(1, (0, 1), gate_y[1])
        down = joined_with(0, (0, 0), down_x[0])
        gate = joined_with(1, (0, 0), gate_y[0])
        down_y = move.swap(down_send, "tp")
        gate_x = move.swap(gate_send, "ctx")
        attn_c, raw_2 = back(4, 2, grad_context, (down_send, gate_send))

        raw_2, attn_c, down, gate, feed_keep = fence(
            raw_2, attn_c, down, gate, feed_keep, waits=(down_y, gate_x, up_a_x, up_b_y)
        )
        attn_c = move.sum_shards(attn_c)
        up_a_send = joined_with(2, (1, 0) + first, up_a_x[1])
        up_b_send = joined_with(2, (0, 1) + last, up_b_y[1])
        up_a = joined_with(2, (0, 0) + first, up_a_x[0])
        up_b = joined_with(2, (0, 0) + last, up_b_y[0])
        up_a_y = move.swap(up_a_send, "tp")
        up_b_x = move.swap(up_b_send, "ctx")
        some = jnp.concatenate([move.add(down, down_y), move.add(gate, gate_x)], 2)
        some_shifts = move.level_shifts(some)
        keep_rows, send_rows = token_gradient(
            slot_half,
            attn_in,
            (raw_0, raw_1, raw_2),
            grad_mix_one,
            *qkv_w,
            (up_a_send, up_b_send, some),
        )

        send_rows, up_a, up_b, attn_a, some = fence(
            send_rows, up_a, up_b, attn_a, some[0], waits=(up_a_y, up_b_x)
        )
        attn_x = move.swap(attn_a, "ctx")
        other_rows = move.swap_slots(send_rows)
        up = [
            jnp.concatenate(
                [move.add(up_a[step], up_a_y[step]), move.add(up_b[step], up_b_x[step])], 1
            )
            for step in range(levels)
        ]

        attn_a, some, *up = fence(attn_a, some, *up, waits=(attn_x, *some_shifts))
        up_shifts = move.level_shifts(up)
        some = move.sum_shifts(some, some_shifts)
        attn_a = move.add(attn_a, attn_x)
        attn_y = move.swap(attn_a, "tp")

        up, attn_a, attn_c, some = fence(
            up[0], attn_a, attn_c, some, waits=(attn_y, *up_shifts)
        )
        feed = jnp.concatenate([some, move.sum_shifts(up, up_shifts)], 1)
        feed_x = move.swap(feed, "ctx")
        attn_a = move.add(attn_a, attn_y)
        attn_c = move.sum_all(attn_c)
        low = jnp.where(move.x == 0, feed, feed_x)
        high = jnp.where(move.x == 0, feed_x, feed)
        feed = jnp.concatenate([low, high], 0).astype(f32)
        attn = attn_a
        down_gradient = feed[:, :feed_width].T
        gate_gradient = feed[:, feed_width : 2 * feed_width]
        up_gradient = feed[:, 2 * feed_width :]
        out_gradient = attn[:, :model_width].astype(f32)
        vector_grads = [attn[:, model_width + place].astype(f32) for place in range(4)]
        attn = jnp.concatenate([attn[:, model_width + PAIR :], attn_c], 1)
        qkv_gradient = attn.reshape(shard, pairs, 3, PAIR).transpose(0, 2, 1, 3)
        qkv_gradient = qkv_gradient.reshape(shard, 3 * model_width).astype(f32)
        mixed_out = from_slot(mixed_keep, other_mixed)
        grad_tokens = from_slot(keep_rows, other_rows.astype(f32))
    else:
        mixed_out = from_slot(mixed_keep, move.swap_slots(mixed_send))
        grad_query, grad_keys, grad_values = attend_back_plain(
            length, queries, key_rows, values, context, summit, grad_context
        )
        if mates > 1:

            def scatter_rows(value):
                return lax.psum_scatter(
                    value, "ctx", scatter_dimension=0, axis_index_groups=groups, tiled=True
                )

            grad_keys, grad_values = scatter_rows(grad_keys), scatter_rows(grad_values)

        def turn_back(value):
            value = value.reshape(-1, HEADS, 2, HEAD_DIM // 2)
            ahead, behind = value[:, :, 0], value[:, :, 1]
            cos_half = cosine[:, None, : HEAD_DIM // 2]
            sin_half = sine[:, None, HEAD_DIM // 2 : HEAD_DIM]
            value = jnp.stack(
                [ahead * cos_half + behind * sin_half, behind * cos_half - ahead * sin_half], 2
            )
            return value.reshape(-1, model_width)

        grad_raw = jnp.concatenate(
            [turn_back(grad_query), turn_back(grad_keys), grad_values], 1
        ).astype(bf16)
        total = grad_mix_one + dot(grad_raw, qkv_all[0], NT)
        first = lax.dynamic_slice_in_dim(total, slot * half_rows, half_rows, 0)
        second = lax.dynamic_slice_in_dim(total, (1 - slot) * half_rows, half_rows, 0)
        other_rows = move.swap_slots(second.astype(bf16))
        grad_tokens = from_slot(first, other_rows.astype(f32))
        every = ("ctx", "tp")

        def scatter(value, split):
            value = lax.psum(value, every)
            value = lax.psum_scatter(value, "fsdp", scatter_dimension=0, tiled=True)
            if split:
                value = lax.dynamic_slice_in_dim(value, move.y * feed_width, feed_width, 1)
            return value.astype(f32)

        feed = jnp.concatenate([feed_keep[:, 0, 0], feed_send[:, 0, 0]], 1)
        down_gradient = scatter(feed[0], True).T
        gate_gradient = scatter(feed[1], True)
        up_gradient = scatter(feed[2], True)
        outer = dot(slot_tokens, grad_raw, (((0,), (0,)), ((), ())))
        qkv_gradient = scatter(outer.astype(bf16), False)
        attn_o = scatter(attn_o, False)
        out_gradient = attn_o[:, :model_width]
        vector_grads = [attn_o[:, model_width + place] for place in range(4)]
    return (
        mixed_out,
        grad_tokens,
        qkv_gradient,
        out_gradient,
        gate_gradient,
        up_gradient,
        down_gradient,
        *vector_grads,
    )


def solution(mesh):
    in_specs = (
        P(("fsdp", "tp"), "ctx", None),
        P("fsdp", None),
        P("fsdp", None),
        P("fsdp", "tp"),
        P("fsdp", "tp"),
        P("tp", "fsdp"),
        P("fsdp"),
        P("fsdp"),
        P("fsdp"),
        P("fsdp"),
        P(("fsdp", "tp")),
        P(("fsdp", "tp"), "ctx"),
        P(("fsdp", "tp"), "ctx", None),
    )
    out_specs = (
        P(("fsdp", "tp"), "ctx", None),
        P(("fsdp", "tp"), "ctx", None),
        P("fsdp", None),
        P("fsdp", None),
        P("fsdp", "tp"),
        P("fsdp", "tp"),
        P("tp", "fsdp"),
        P("fsdp"),
        P("fsdp"),
        P("fsdp"),
        P("fsdp"),
    )
    return jax.shard_map(
        functools.partial(on_device, mesh),
        mesh=mesh,
        in_specs=in_specs,
        out_specs=out_specs,
        check_vma=False,
    )
```
